32 devices in a mesh: rep: 4 (over x, core), shard: 8 (over z, y).
Axes of the slice: x: 2, y: 2, z: 4, core: 2. Of those that a mesh axis runs over, the one named last changes fastest.
Arguments:
- hidden_in: bfloat16 [8192, 1280], P(('rep', 'shard')), may hold values from -6 to 6
- seg_ids: int32 [32, 256], P(('rep', 'shard')), may hold values from 0 to 1, as said below
- patch_rows: int32 [32, 256], P(('rep', 'shard')), may hold values from 0 to 31
- patch_cols: int32 [32, 256], P(('rep', 'shard')), may hold values from 0 to 31
- ln1_scale: bfloat16 [1280], P('shard'), may hold values from 0.5 to 1.5
- ln1_shift: bfloat16 [1280], P('shard'), may hold values from -1.5 to 1.5
- qkv_weight: bfloat16 [1280, 3840], P('shard'), may hold values from -0.15625 to 0.15625
- qkv_bias: bfloat16 [3840], P('shard'), may hold values from -1.5 to 1.5
- out_weight: bfloat16 [1280, 1280], P('shard'), may hold values from -1.25 to 1.25
- out_bias: bfloat16 [1280], P('shard'), may hold values from -1.5 to 1.5
- ln2_scale: bfloat16 [1280], P('shard'), may hold values from 0.5 to 1.5
- ln2_shift: bfloat16 [1280], P('shard'), may hold values from -1.5 to 1.5
- up_weight: bfloat16 [1280, 5120], P('shard'), may hold values from -0.15625 to 0.15625
- up_bias: bfloat16 [5120], P('shard'), may hold values from -1.5 to 1.5
- down_weight: bfloat16 [5120, 1280], P('shard'), may hold values from -0.078125 to 0.078125
- down_bias: bfloat16 [1280], P('shard'), may hold values from -1.5 to 1.5
- cotangent: bfloat16 [8192, 1280], P(('rep', 'shard')), may hold values from -6 to 6
Outputs:
- block_out: bfloat16 [8192, 1280], P(('rep', 'shard'))
- grad_in: bfloat16 [8192, 1280], P(('rep', 'shard'))
- grad_ln1_scale: float32 [1280], P('shard')
- grad_ln1_shift: float32 [1280], P('shard')
- grad_qkv_weight: float32 [1280, 3840], P('shard')
- grad_qkv_bias: float32 [3840], P('shard')
- grad_out_weight: float32 [1280, 1280], P('shard')
- grad_out_bias: float32 [1280], P('shard')
- grad_ln2_scale: float32 [1280], P('shard')
- grad_ln2_shift: float32 [1280], P('shard')
- grad_up_weight: float32 [1280, 5120], P('shard')
- grad_up_bias: float32 [5120], P('shard')
- grad_down_weight: float32 [5120, 1280], P('shard')
- grad_down_bias: float32 [1280], P('shard')
The draws below stay inside these ranges and needn't reach their ends.
Inputs may be any that keep to these rules, and one draw needn't show every extreme that they name: `seg_ids`: each row numbers the images of one block of 256 consecutive patches in order, never falling. Every row holds exactly two images: one of exactly 192 patches and one of 64 patches, in either order.
All inputs are finite; a program needn't handle non-finite values.
Results may differ from the reference program's by a relative error of at most 0.013.
Values may be sent and summed in bfloat16 or wider, within the bound.
No kernel may reach another device: no remote copies, remote signals or barrier semaphores. Data moves between devices by JAX's collectives and lax.ppermute only.
A program may use at most 256 MiB of HBM per device.

```python
import jax
import jax.numpy as jnp
from jax import lax

D = 1280
HEADS = 16
HEAD_DIM = 80
FF = 5120
TOK_DEV = 256
GRID = 32
IMG_MOST = 192
BLOCKS = 32
TOKENS = 8192


def draw_seg_ids(key, part):
    key = jax.random.fold_in(key, 11)
    big_first = jax.random.randint(key, (BLOCKS,), 0, 2)
    first_length = jnp.where(big_first == 1, IMG_MOST, TOK_DEV - IMG_MOST).astype(jnp.int32)
    positions = jnp.arange(TOK_DEV, dtype=jnp.int32)
    return (positions[None, :] >= first_length[:, None]).astype(jnp.int32)


def touch_ends(entries, stream_key, low, top_value):
    longest = entries.shape.index(max(entries.shape))
    spots = []
    for shift in (0, 1):
        where = [jax.random.randint(jax.random.fold_in(stream_key, axis), (), 0, length) for axis, length in enumerate(entries.shape)]
        where[longest] = (where[longest] + shift) % entries.shape[longest]
        spots.append(tuple(where))
    return entries.at[spots[0]].set(low).at[spots[1]].set(top_value)


def spiked(array, stream_key, source, target, blocks, factor):
    owner, partner = [(jnp.arange(array.shape[axis_at]) // (array.shape[axis_at] // blocks)).reshape([-1 if axis == axis_at else 1 for axis in range(array.ndim)]) for axis_at in (source, target)]
    chosen = jax.random.permutation(stream_key, blocks)[partner]
    strong = (owner == chosen) | (owner == (partner + blocks // 2) % blocks)
    return jnp.where(strong, factor * array, array)


def levels(stream_key, extent, cuts, low, high):
    def one(axis_at, parts):
        heights = jax.random.uniform(jax.random.fold_in(jax.random.fold_in(stream_key, 6), axis_at), (parts,), jnp.float32, low / len(cuts), high / len(cuts))
        return jnp.repeat(jnp.exp(heights), extent[axis_at] // parts).reshape((-1,) + (1,) * (len(extent) - axis_at - 1))

    loudness = one(*cuts[0])
    for cut in cuts[1:]:
        loudness = loudness * one(*cut)
    return loudness


def scatter_about(stream_key, extent, scale, limit, cuts=(), kind=jnp.bfloat16):
    values = jax.random.normal(stream_key, extent, jnp.float32) * scale
    if len(cuts) > 0:
        values = levels(stream_key, extent, cuts, -0.22, 0.18) * values
    return jnp.clip(values, min=-limit, max=limit).astype(kind)


def heavy_noise(stream_key, shape, scale, most, cuts, heavy, kind=jnp.bfloat16):
    drawn = scale * jax.random.normal(stream_key, shape, jnp.float32)
    if cuts:
        drawn = drawn * levels(stream_key, shape, cuts, -0.22, 0.18)
    return jnp.clip(spiked(drawn, jax.random.fold_in(stream_key, 3), *heavy), -most, most).astype(kind)


def setup_inputs(seed: int = 0) -> dict:
    seeds = jax.random.split(jax.random.key(seed), 18)
    hidden_in = heavy_noise(seeds[0], (TOKENS, D), 1.0, 6.0, ((0, 32),), (0, 1, 32, 2.75))
    seg_ids = draw_seg_ids(jax.random.fold_in(seeds[17], 71), 0)
    patch_rows = touch_ends(jax.random.randint(seeds[2], (BLOCKS, TOK_DEV), 0, GRID), jax.random.fold_in(seeds[2], 1), 0, GRID - 1).astype(jnp.int32)
    patch_cols = touch_ends(jax.random.randint(seeds[3], (BLOCKS, TOK_DEV), 0, GRID), jax.random.fold_in(seeds[3], 1), 0, GRID - 1).astype(jnp.int32)
    ln1_scale = jnp.clip(1.0 + 0.1 * jax.random.normal(seeds[4], (D,), jnp.float32), 0.5, 1.5).astype(jnp.bfloat16)
    ln1_shift = scatter_about(seeds[5], (D,), 0.3, 1.5, ((0, 8),))
    qkv_weight = scatter_about(seeds[6], (D, 3 * D), D ** -0.5, 0.15625, ((0, 8),))
    qkv_bias = scatter_about(seeds[7], (3 * D,), 0.3, 1.5, ((0, 8),))
    out_weight = scatter_about(seeds[8], (D, D), (D * 4 // TOK_DEV) ** -0.5, 1.25, ((0, 8),))
    out_bias = scatter_about(seeds[9], (D,), 0.3, 1.5, ((0, 8),))
    ln2_scale = jnp.clip(1.0 + 0.1 * jax.random.normal(seeds[10], (D,), jnp.float32), 0.5, 1.5).astype(jnp.bfloat16)
    ln2_shift = scatter_about(seeds[11], (D,), 0.3, 1.5, ((0, 8),))
    up_weight = scatter_about(seeds[12], (D, FF), D ** -0.5, 0.15625, ((0, 8),))
    up_bias = scatter_about(seeds[13], (FF,), 0.3, 1.5, ((0, 8),))
    down_weight = scatter_about(seeds[14], (FF, D), FF ** -0.5, 0.078125, ((0, 8),))
    down_bias = scatter_about(seeds[15], (D,), 0.3, 1.5, ((0, 8),))
    cotangent = scatter_about(seeds[16], (TOKENS, D), 1.0, 6.0, ((0, 32),))
    return {"hidden_in": hidden_in, "seg_ids": seg_ids, "patch_rows": patch_rows, "patch_cols": patch_cols, "ln1_scale": ln1_scale, "ln1_shift": ln1_shift, "qkv_weight": qkv_weight, "qkv_bias": qkv_bias, "out_weight": out_weight, "out_bias": out_bias, "ln2_scale": ln2_scale, "ln2_shift": ln2_shift, "up_weight": up_weight, "up_bias": up_bias, "down_weight": down_weight, "down_bias": down_bias, "cotangent": cotangent}


EPSILON = 1e-06
GELU_SLOPE = 1.702
HIGH = lax.Precision.HIGHEST

@jax.custom_vjp
def low(v):
    return lax.optimization_barrier(v.astype(jnp.bfloat16)).astype(jnp.float32)

@jax.custom_vjp
def low_back(v):
    return v

def low_keep(v):
    return (low(v), None)

def low_pass(kept, grad):
    return (grad,)

def back_keep(v):
    return (v, None)

def back_low(kept, grad):
    return (low(grad),)
low.defvjp(low_keep, low_pass)
low_back.defvjp(back_keep, back_low)

def layer_norm(values, scale, shift):
    center = values - lax.optimization_barrier(jnp.mean(values, -1, keepdims=True))
    spread = lax.optimization_barrier(jnp.mean(center * center, -1, keepdims=True))
    return center * lax.rsqrt(spread + EPSILON) * scale + shift

def rotate_half(values):
    middle = values.shape[-1] // 2
    return jnp.concatenate([-values[..., middle:], values[..., :middle]], -1)

def rotary_angles(rows, columns):
    quarter = HEAD_DIM // 4
    inverse = 10000.0 ** (-4.0 * jnp.arange(quarter, dtype=jnp.float32) / HEAD_DIM)
    row_angles = rows.astype(jnp.float32)[..., None] * inverse
    column_angles = columns.astype(jnp.float32)[..., None] * inverse
    halfway = jnp.concatenate([row_angles, column_angles], -1)
    angles = jnp.concatenate([halfway, halfway], -1)
    return (jnp.cos(angles), jnp.sin(angles))

def block_forward(params, inputs, rows, columns, images):
    ln1_scale, ln1_shift, qkv_weight, qkv_bias, out_weight, out_bias, ln2_scale, ln2_shift, up_weight, up_bias, down_weight, down_bias = params
    groups = rows.shape[0]
    length = rows.shape[1]
    scale_factor = HEAD_DIM ** (-0.5)
    normed = low(layer_norm(inputs, ln1_scale, ln1_shift))
    projected = low_back(jnp.dot(normed, qkv_weight, precision=HIGH) + qkv_bias)
    projected = projected.reshape(groups, length, 3, HEADS, HEAD_DIM)
    cosine, sine = rotary_angles(rows, columns)
    cosine = cosine[:, :, None, :]
    sine = sine[:, :, None, :]
    queries = low(projected[:, :, 0] * cosine + rotate_half(projected[:, :, 0]) * sine)
    keys_rot = low(projected[:, :, 1] * cosine + rotate_half(projected[:, :, 1]) * sine)
    values_low = low(projected[:, :, 2])
    scores = low_back(jnp.einsum('gthd,gshd->ghts', queries, keys_rot, precision=HIGH) * scale_factor)
    same = images[:, None, :, None] == images[:, None, None, :]
    scores = jnp.where(same, scores, -1e+30)
    shifted = scores - lax.optimization_barrier(jnp.max(scores, -1, keepdims=True))
    expo = jnp.exp(shifted)
    probs = expo / lax.optimization_barrier(jnp.sum(expo, -1, keepdims=True))
    mixed = low_back(jnp.einsum('ghts,gshd->gthd', low(probs), values_low, precision=HIGH))
    mixed = low(mixed.reshape(groups * length, HEADS * HEAD_DIM))
    branch = low_back(jnp.dot(mixed, out_weight, precision=HIGH) + out_bias)
    middle = inputs + branch
    normed_two = low(layer_norm(middle, ln2_scale, ln2_shift))
    upward = low_back(jnp.dot(normed_two, up_weight, precision=HIGH) + up_bias)
    activated = low(upward * jax.nn.sigmoid(GELU_SLOPE * upward))
    return middle + jnp.dot(activated, down_weight, precision=HIGH) + down_bias

def reference(hidden_in, seg_ids, patch_rows, patch_cols, ln1_scale, ln1_shift, qkv_weight, qkv_bias, out_weight, out_bias, ln2_scale, ln2_shift, up_weight, up_bias, down_weight, down_bias, cotangent):
    weights = tuple((tensor.astype(jnp.float32) for tensor in (ln1_scale, ln1_shift, qkv_weight, qkv_bias, out_weight, out_bias, ln2_scale, ln2_shift, up_weight, up_bias, down_weight, down_bias)))
    group = 8 if BLOCKS % 8 == 0 else 1
    count = BLOCKS // group

    def forward(inputs, params):

        def step(carry, pieces):
            block_in, rows, columns, images = pieces
            return (carry, jax.checkpoint(block_forward)(params, block_in, rows, columns, images))
        sliced = (inputs.reshape(count, group * TOK_DEV, D), patch_rows.reshape(count, group, TOK_DEV), patch_cols.reshape(count, group, TOK_DEV), seg_ids.reshape(count, group, TOK_DEV))
        _, outputs = lax.scan(step, jnp.zeros((), jnp.float32), sliced)
        return outputs.reshape(TOKENS, D)
    result, pullback = jax.vjp(forward, hidden_in.astype(jnp.float32), weights)
    grad_inputs, grads = pullback(cotangent.astype(jnp.float32))
    return (result.astype(jnp.bfloat16), grad_inputs.astype(jnp.bfloat16), grads[0], grads[1], grads[2], grads[3], grads[4], grads[5], grads[6], grads[7], grads[8], grads[9], grads[10], grads[11])
```

```python
import jax
import jax.numpy as jnp
import numpy as np
from jax import lax
from jax.experimental import pallas as pl
from jax.experimental.pallas import tpu as pltpu
from jax.sharding import PartitionSpec as P

HEADS = 16
EPSILON = 1e-06
GELU_SLOPE = 1.702
LANES = 128
MASKED = -1e30

CORE_PAIRS = [(0, 1), (1, 0), (2, 3), (3, 2)]
X_PAIRS = [(0, 2), (2, 0), (1, 3), (3, 1)]
RING = (0, 2, 4, 6, 7, 5, 3, 1)
RING_AT = tuple(RING.index(i) for i in range(8))
RIGHT = [(RING[i], RING[(i + 1) % 8]) for i in range(8)]
LEFT = [(RING[i], RING[(i - 1) % 8]) for i in range(8)]

F32 = jnp.float32
BF16 = jnp.bfloat16


def norm_parts(values):
    center = values - jnp.mean(values, -1, keepdims=True)
    inverse = lax.rsqrt(jnp.mean(center * center, -1, keepdims=True) + EPSILON)
    return (center * inverse, inverse)


def norm_back(grad_normed, unit, inverse, scale):
    scaled = grad_normed * scale
    return inverse * (
        scaled
        - jnp.mean(scaled, -1, keepdims=True)
        - unit * jnp.mean(scaled * unit, -1, keepdims=True)
    )


def outer(left, right):
    return lax.dot_general(left, right, (((0,), (0,)), ((), ())), preferred_element_type=F32)


def times_transposed(left, right):
    return lax.dot_general(left, right, (((1,), (1,)), ((), ())), preferred_element_type=F32)


def times(left, right):
    return jnp.dot(left, right, preferred_element_type=F32)


def to_core(value):
    return lax.ppermute(value, "rep", CORE_PAIRS)


def to_x(value):
    return lax.ppermute(value, "rep", X_PAIRS)


def gather_rep(value):
    near, far = to_core(value), to_x(value)
    return [value, near, far, to_core(far)]


def reduce_pair(parts):
    low = parts.astype(BF16)
    arrived = to_core(jnp.stack([low[1], low[3]]))
    return (jnp.stack([low[0], low[2]]).astype(F32) + arrived.astype(F32)).astype(BF16)


def scatter_rep(parts):
    pair = reduce_pair(parts)
    return pair[0].astype(F32) + to_x(pair[1]).astype(F32)


def sum_rep(parts):
    pair = reduce_pair(parts)
    arrived = to_x(pair)
    total = (pair.astype(F32) + arrived[::-1].astype(F32)).astype(BF16)
    near = to_core(total)
    return jnp.stack([total[0], near[0], total[1], near[1]])


def by_owner(slots, me):
    core, far = me % 2 == 1, me // 2 == 1
    a, b, c, d = slots
    a, b, c, d = (
        jnp.where(core, b, a),
        jnp.where(core, a, b),
        jnp.where(core, d, c),
        jnp.where(core, c, d),
    )
    return [jnp.where(far, c, a), jnp.where(far, d, b), jnp.where(far, a, c), jnp.where(far, b, d)]


def ring_slot(position, step):
    return jnp.asarray(RING, jnp.int32)[(position + step) % 8]


def gather_shards(pieces, shards):
    if shards != 8:
        return [lax.all_gather(piece, "shard", axis=0) for piece in pieces]
    position = jnp.asarray(RING_AT, jnp.int32)[lax.axis_index("shard")]
    outs = []
    for number, piece in enumerate(pieces):
        rights = 4 if number % 2 == 0 else 3
        whole = jnp.zeros((8,) + piece.shape, piece.dtype)
        right = left = piece
        whole = lax.dynamic_update_slice(whole, piece[None], (ring_slot(position, 0), 0, 0))
        for step in range(1, 5):
            if step <= rights:
                right = lax.ppermute(right, "shard", RIGHT)
                whole = lax.dynamic_update_slice(
                    whole, right[None], (ring_slot(position, 8 - step), 0, 0)
                )
            if step <= 7 - rights:
                left = lax.ppermute(left, "shard", LEFT)
                whole = lax.dynamic_update_slice(
                    whole, left[None], (ring_slot(position, step), 0, 0)
                )
        outs.append(whole)
    return outs


def scatter_shards(whole, shards, rights):
    if shards != 8:
        return lax.psum_scatter(whole, "shard", scatter_dimension=0, tiled=False)
    position = jnp.asarray(RING_AT, jnp.int32)[lax.axis_index("shard")]

    def own(step):
        return lax.dynamic_index_in_dim(whole, ring_slot(position, step), 0, False)

    def plus(one, other):
        return (one.astype(F32) + other.astype(F32)).astype(whole.dtype)

    right = left = None
    for step in range(4, 0, -1):
        if step <= rights:
            term = own(step)
            right = lax.ppermute(term if right is None else plus(right, term), "shard", RIGHT)
        if step <= 7 - rights:
            term = own(8 - step)
            left = lax.ppermute(term if left is None else plus(left, term), "shard", LEFT)
    return (right.astype(F32) + left.astype(F32) + own(0).astype(F32)).astype(whole.dtype)


def window(values, start, size):
    part = values[:, start : start + size]
    return jnp.concatenate([part, jnp.zeros((part.shape[0], LANES - size), part.dtype)], 1)


def turned(values, half, lane):
    return jnp.where(
        lane < half,
        pltpu.roll(values, LANES - half, 1),
        pltpu.roll(values, half, 1),
    )


def attend_kernel(
    heads, size, x_ref, gain_ref, shift_ref, w_ref, bias_ref, cos_ref, sin_ref, row_ref, col_ref,
    normed_ref, qkv_ref, lse_ref, out_ref,
):
    unit, _ = norm_parts(x_ref[...].astype(F32))
    normed = (unit * gain_ref[...] + shift_ref[...]).astype(BF16)
    normed_ref[...] = normed
    projected = times(normed, w_ref[...]) + bias_ref[...]
    cosine, sine = cos_ref[...], sin_ref[...]
    rows = projected.shape[0]
    lane = lax.broadcasted_iota(jnp.int32, (rows, LANES), 1)
    same = col_ref[...] == row_ref[0]
    scale = size**-0.5
    half = size // 2
    outs = []
    lses = jnp.zeros((rows, LANES), F32)
    for head in range(heads):
        query, key, value = (
            window(projected, (part * heads + head) * size, size) for part in range(3)
        )
        query = (query * cosine + turned(query, half, lane) * sine).astype(BF16)
        key = (key * cosine + turned(key, half, lane) * sine).astype(BF16)
        value = value.astype(BF16)
        for part, kept in enumerate((query, key, value)):
            at = (part * heads + head) * LANES
            qkv_ref[:, at : at + LANES] = kept
        scores = jnp.where(same, times_transposed(query, key) * scale, MASKED)
        most = jnp.max(scores, -1, keepdims=True)
        expo = jnp.exp(scores - most)
        total = jnp.sum(expo, -1, keepdims=True)
        probs = (expo * (1.0 / total)).astype(BF16)
        outs.append(times(probs, value)[:, :size])
        lses = jnp.where(lane == head, most + jnp.log(total), lses)
    lse_ref[...] = lses
    out_ref[...] = jnp.concatenate(outs, 1).astype(BF16)


def attend(x, gain, shift, weight, bias, cosine, sine, seg_rows, seg_cols, heads, size):
    tokens, width = x.shape
    length = seg_rows.shape[-1]
    part = heads * size
    by_block = lambda columns: pl.BlockSpec((length, columns), lambda i: (i, 0))
    fixed = lambda array: pl.BlockSpec(array.shape, lambda i: (0,) * array.ndim)
    return pl.pallas_call(
        lambda *refs: attend_kernel(heads, size, *refs),
        grid=(tokens // length,),
        in_specs=[
            by_block(width),
            fixed(gain),
            fixed(shift),
            fixed(weight),
            fixed(bias),
            by_block(LANES),
            by_block(LANES),
            pl.BlockSpec((1, 1, length), lambda i: (i, 0, 0)),
            by_block(1),
        ],
        out_specs=[by_block(width), by_block(3 * heads * LANES), by_block(LANES), by_block(part)],
        out_shape=[
            jax.ShapeDtypeStruct((tokens, width), BF16),
            jax.ShapeDtypeStruct((tokens, 3 * heads * LANES), BF16),
            jax.ShapeDtypeStruct((tokens, LANES), F32),
            jax.ShapeDtypeStruct((tokens, part), BF16),
        ],
        compiler_params=pltpu.CompilerParams(vmem_limit_bytes=48 * 1024 * 1024),
        cost_estimate=pl.CostEstimate(
            flops=2 * tokens * width * 3 * part + 4 * tokens * length * part,
            bytes_accessed=4 * tokens * width + weight.size * 2 + tokens * 3 * heads * LANES * 2,
            transcendentals=tokens * length * heads,
        ),
    )(x, gain, shift, weight, bias, cosine, sine, seg_rows, seg_cols)


def attend_back_kernel(
    heads, size, db_ref, wo_ref, qkv_ref, lse_ref, cos_ref, sin_ref, row_ref, col_ref, w_ref,
    x_ref, grad_ref, dn_ref, sum_ref, gain_ref, shift_ref,
):
    mixed = times_transposed(db_ref[...], wo_ref[...])
    cosine, sine = cos_ref[...], sin_ref[...]
    rows = mixed.shape[0]
    lane = lax.broadcasted_iota(jnp.int32, (rows, LANES), 1)
    same = col_ref[...] == row_ref[0]
    scale = size**-0.5
    half = size // 2
    lses = lse_ref[...]
    grads = [None] * (3 * heads)
    for head in range(heads):
        query, key, value = (
            qkv_ref[:, (part * heads + head) * LANES : (part * heads + head + 1) * LANES]
            for part in range(3)
        )
        lse = jnp.sum(jnp.where(lane == head, lses, 0.0), -1, keepdims=True)
        scores = jnp.where(same, times_transposed(query, key) * scale, MASKED)
        probs = jnp.exp(scores - lse)
        grad_mixed = window(mixed, head * size, size).astype(BF16)
        grad_probs = times_transposed(grad_mixed, value)
        grad_value = outer(probs.astype(BF16), grad_mixed)
        inner = jnp.sum(probs * grad_probs, -1, keepdims=True)
        low = (probs * (grad_probs - inner)).astype(BF16)
        grad_query = times(low, key) * scale
        grad_key = outer(low, query) * scale
        grad_query = grad_query * cosine + turned(grad_query * sine, half, lane)
        grad_key = grad_key * cosine + turned(grad_key * sine, half, lane)
        grads[head] = grad_query[:, :size]
        grads[heads + head] = grad_key[:, :size]
        grads[2 * heads + head] = grad_value[:, :size]
    grad = jnp.concatenate(grads, 1).astype(BF16)
    grad_ref[...] = grad
    grad_normed = times_transposed(grad, w_ref[...])
    dn_ref[...] = grad_normed.astype(BF16)
    unit, _ = norm_parts(x_ref[...].astype(F32))

    @pl.when(pl.program_id(0) == 0)
    def _():
        sum_ref[...] = jnp.zeros_like(sum_ref)
        gain_ref[...] = jnp.zeros_like(gain_ref)
        shift_ref[...] = jnp.zeros_like(shift_ref)

    sum_ref[...] += jnp.sum(grad.astype(F32), 0, keepdims=True)
    gain_ref[...] += jnp.sum(grad_normed * unit, 0, keepdims=True)
    shift_ref[...] += jnp.sum(grad_normed, 0, keepdims=True)


def attend_back(db, w_out, qkv, lse, cosine, sine, seg_rows, seg_cols, weight, x, heads, size):
    tokens, width = x.shape
    length = seg_rows.shape[-1]
    part = heads * size
    by_block = lambda columns: pl.BlockSpec((length, columns), lambda i: (i, 0))
    fixed = lambda shape: pl.BlockSpec(shape, lambda i: (0,) * len(shape))
    return pl.pallas_call(
        lambda *refs: attend_back_kernel(heads, size, *refs),
        grid=(tokens // length,),
        in_specs=[
            by_block(width),
            fixed(w_out.shape),
            by_block(3 * heads * LANES),
            by_block(LANES),
            by_block(LANES),
            by_block(LANES),
            pl.BlockSpec((1, 1, length), lambda i: (i, 0, 0)),
            by_block(1),
            fixed(weight.shape),
            by_block(width),
        ],
        out_specs=[
            by_block(3 * part),
            by_block(width),
            fixed((1, 3 * part)),
            fixed((1, width)),
            fixed((1, width)),
        ],
        out_shape=[
            jax.ShapeDtypeStruct((tokens, 3 * part), BF16),
            jax.ShapeDtypeStruct((tokens, width), BF16),
            jax.ShapeDtypeStruct((1, 3 * part), F32),
            jax.ShapeDtypeStruct((1, width), F32),
            jax.ShapeDtypeStruct((1, width), F32),
        ],
        compiler_params=pltpu.CompilerParams(vmem_limit_bytes=48 * 1024 * 1024),
        cost_estimate=pl.CostEstimate(
            flops=2 * tokens * width * 4 * part + 10 * tokens * length * part,
            bytes_accessed=6 * tokens * width + weight.size * 2 + tokens * 3 * heads * LANES * 2,
            transcendentals=tokens * length * heads,
        ),
    )(db, w_out, qkv, lse, cosine, sine, seg_rows, seg_cols, weight, x)


def rotary(rows, columns, size):
    quarter = size // 4
    inverse = 10000.0 ** (-4.0 * jnp.arange(quarter, dtype=F32) / size)
    angles = jnp.concatenate(
        [rows.astype(F32)[:, None] * inverse, columns.astype(F32)[:, None] * inverse], -1
    )
    cosine, sine = jnp.cos(angles), jnp.sin(angles)
    nothing = jnp.zeros((rows.shape[0], LANES - size), F32)
    return (
        jnp.concatenate([cosine, cosine, nothing], -1),
        jnp.concatenate([-sine, sine, nothing], -1),
    )


def on_device(
    shards,
    hidden_in,
    seg_ids,
    patch_rows,
    patch_cols,
    ln1_scale,
    ln1_shift,
    qkv_weight,
    qkv_bias,
    out_weight,
    out_bias,
    ln2_scale,
    ln2_shift,
    up_weight,
    up_bias,
    down_weight,
    down_bias,
    cotangent,
):
    copies = 4
    me = lax.axis_index("rep")
    length, width = hidden_in.shape
    rows = ln1_scale.shape[0]
    size = width // HEADS
    heads = HEADS // copies
    part = heads * size
    hidden = up_weight.shape[1]
    own_hidden = hidden // copies
    step = hidden // shards // copies

    def own(array, axis):
        return lax.dynamic_index_in_dim(array, me, axis, False)

    own_qkv = own(qkv_weight.reshape(rows, 3, copies, part), 2).reshape(rows, 3 * part)
    own_up = own(up_weight.reshape(rows, shards, copies, step), 2).reshape(rows, own_hidden)
    own_down = own(down_weight.reshape(copies, step, width), 0)
    own_out = own(out_weight.reshape(copies, rows // copies, width), 0)
    vectors = (
        ln1_scale, ln1_shift, out_bias, ln2_scale, ln2_shift, down_bias, qkv_bias, up_bias,
    )
    small = jnp.concatenate(vectors)
    small_rows = 8
    small = jnp.pad(small, (0, small_rows * 3 * part - small.size)).reshape(small_rows, 3 * part)
    first, up_full, out_all, down_full = gather_shards(
        [
            jnp.concatenate([own_qkv, small]),
            own_up,
            own_out,
            own_down,
        ],
        shards,
    )
    w_qkv = first[:, :rows].reshape(width, 3 * part)
    small = first[:, rows:].reshape(shards, -1)
    up_full = up_full.reshape(width, own_hidden)
    down_full = down_full.reshape(own_hidden, width)
    full = []
    at = 0
    for vector in vectors:
        full.append(small[:, at : at + vector.size].astype(F32))
        at += vector.size
    gain_one, shift_one, out_offset, gain_two, shift_two, down_offset = (
        v.reshape(1, width) for v in full[:6]
    )
    qkv_offset = own(full[6].reshape(3, copies, part), 1).reshape(1, 3 * part)
    up_offset = own(full[7].reshape(shards, copies, step), 1).reshape(1, own_hidden)

    ids = jnp.concatenate([seg_ids, patch_rows, patch_cols])
    ids = jnp.stack(gather_rep(ids))
    seg_rows, seg_cols = ids[:, :1], ids[:, 0].reshape(-1, 1)
    x_low = jnp.concatenate(gather_rep(hidden_in))
    grad_out = jnp.concatenate(gather_rep(cotangent))
    tokens = x_low.shape[0]
    cosine, sine = rotary(ids[:, 1].reshape(-1), ids[:, 2].reshape(-1), size)

    normed_one, qkv, lse, mixed = attend(
        x_low, gain_one, shift_one, w_qkv, qkv_offset, cosine, sine, seg_rows, seg_cols, heads, size
    )
    out_full = jnp.stack(by_owner(gather_rep(out_all), me), 1).reshape(width, width)
    blocks = mixed.reshape(copies, length, part)
    near, far = to_core(blocks), to_x(blocks)
    both = to_core(far)
    mixed_slots = [
        mixed,
        near[jnp.array([1, 0, 3, 2])].reshape(tokens, part),
        far[jnp.array([2, 3, 0, 1])].reshape(tokens, part),
        both[jnp.array([3, 2, 1, 0])].reshape(tokens, part),
    ]
    mixed_full = jnp.concatenate(by_owner(mixed_slots, me), 1)

    middle = x_low.astype(F32) + times(mixed_full, out_full) + out_offset
    unit_two, inverse_two = norm_parts(middle)
    normed_two = (unit_two * gain_two + shift_two).astype(BF16)
    upward = times(normed_two, up_full) + up_offset
    sigma = jax.nn.sigmoid(GELU_SLOPE * upward)
    activated = (upward * sigma).astype(BF16)
    slope = sigma + GELU_SLOPE * upward * sigma * (1.0 - sigma)

    grad_down = outer(activated, grad_out).astype(BF16)
    grad_up_low = (times_transposed(grad_out, down_full) * slope).astype(BF16)
    grad_normed_two = sum_rep(times_transposed(grad_up_low, up_full).reshape(copies, length, width))
    grad_up = outer(normed_two, grad_up_low).astype(BF16)
    grad_up_bias = jnp.sum(grad_up_low.astype(F32), 0)
    branch = scatter_rep(times(activated, down_full).reshape(copies, length, width))
    output = middle[:length] + branch + down_offset

    grad_normed_two = grad_normed_two.reshape(tokens, width).astype(F32)
    grad_middle = grad_out.astype(F32) + norm_back(
        grad_normed_two, unit_two, inverse_two, gain_two
    )
    grad_branch = grad_middle.astype(BF16)
    grad_out_w = outer(mixed_full, own(grad_branch.reshape(tokens, copies, part), 1)).astype(BF16)

    own_w_out = lax.dynamic_slice_in_dim(out_full, me * part, part, 0)
    grad_qkv_low, grad_normed_one, sum_qkv, sum_gain, sum_shift = attend_back(
        grad_branch, own_w_out, qkv, lse, cosine, sine, seg_rows, seg_cols, w_qkv, x_low, heads, size
    )
    grad_qkv = outer(normed_one, grad_qkv_low).astype(BF16)
    grad_normed_one = scatter_rep(grad_normed_one.reshape(copies, length, width))
    unit_one, inverse_one = norm_parts(hidden_in.astype(F32))
    grad_inputs = grad_middle[:length] + norm_back(grad_normed_one, unit_one, inverse_one, gain_one)

    def sum_of(values):
        return jnp.sum(values[:length], 0).reshape(shards, rows)

    def placed(values, like, axis):
        return lax.dynamic_update_index_in_dim(jnp.zeros(like, F32), values, me, axis)

    sums = [
        sum_gain.reshape(shards, rows),
        sum_shift.reshape(shards, rows),
        sum_of(grad_branch.astype(F32)),
        sum_of(grad_normed_two * unit_two),
        sum_of(grad_normed_two),
        sum_of(grad_out.astype(F32)),
        placed(sum_qkv.reshape(3, part), (3, copies, part), 1).reshape(shards, -1),
        placed(grad_up_bias.reshape(shards, step), (shards, copies, step), 1).reshape(shards, -1),
    ]
    sums = jnp.concatenate(sums, 1)
    sums = jnp.pad(sums, ((0, 0), (0, small_rows * 3 * part - sums.shape[1])))
    last = jnp.concatenate(
        [grad_qkv.reshape(shards, rows, 3 * part), sums.astype(BF16).reshape(shards, small_rows, -1)],
        1,
    )

    done_down = scatter_shards(grad_down.reshape(shards, step, width), shards, 4)
    done_up = scatter_shards(grad_up.reshape(shards, rows, own_hidden), shards, 3)
    done_out = scatter_shards(grad_out_w.reshape(shards, rows, part), shards, 4)
    done_last = scatter_shards(last, shards, 4)

    whole_down = jnp.concatenate(by_owner(gather_rep(done_down), me), 0).astype(F32)
    whole_up = jnp.stack(
        [p.reshape(rows, shards, step) for p in by_owner(gather_rep(done_up), me)], 2
    )
    whole_up = whole_up.reshape(rows, hidden).astype(F32)
    whole_out = jnp.concatenate(by_owner(gather_rep(done_out), me), 1).astype(F32)
    last_slots = gather_rep(done_last)
    whole_qkv = jnp.stack(
        [p[:rows].reshape(rows, 3, part) for p in by_owner(last_slots, me)], 2
    )
    whole_qkv = whole_qkv.reshape(rows, 3 * width).astype(F32)
    summed = sum(p[rows:].astype(F32) for p in by_owner(last_slots, me)).reshape(-1)
    totals = []
    at = 0
    for vector in vectors:
        totals.append(summed[at : at + vector.size])
        at += vector.size
    return (
        output.astype(BF16),
        grad_inputs.astype(BF16),
        totals[0],
        totals[1],
        whole_qkv,
        totals[6],
        whole_out,
        totals[2],
        totals[3],
        totals[4],
        whole_up,
        totals[7],
        whole_down,
        totals[5],
    )


def solution(mesh):
    shards = mesh.shape["shard"]
    tokens, vector, matrix = P(("rep", "shard"), None), P("shard"), P("shard", None)
    in_specs = (
        (tokens,) * 4
        + (vector, vector, matrix, vector, matrix, vector)
        + (vector, vector, matrix, vector, matrix, vector)
        + (tokens,)
    )
    out_specs = (
        (tokens, tokens)
        + (vector, vector, matrix, vector, matrix, vector)
        + (vector, vector, matrix, vector, matrix, vector)
    )
    return jax.shard_map(
        lambda *args: on_device(shards, *args),
        mesh=mesh,
        in_specs=in_specs,
        out_specs=out_specs,
        check_vma=False,
    )
```

```python
import jax
import jax.numpy as jnp
import numpy as np
from jax import lax
from jax.experimental import pallas as pl
from jax.experimental.pallas import tpu as pltpu
from jax.sharding import PartitionSpec as P

HEADS = 16
EPSILON = 1e-06
GELU_SLOPE = 1.702
LANES = 128
MASKED = -1e30
COPIES = 4
EXTRA = 16

CORE_PAIRS = [(0, 1), (1, 0), (2, 3), (3, 2)]
X_PAIRS = [(0, 2), (2, 0), (1, 3), (3, 1)]
RING = (0, 2, 4, 6, 7, 5, 3, 1)
RING_AT = tuple(RING.index(i) for i in range(8))
RIGHT = [(RING[i], RING[(i + 1) % 8]) for i in range(8)]
LEFT = [(RING[i], RING[(i - 1) % 8]) for i in range(8)]
OFFSETS = (0, -1, 1, -2, 2, -3, 3, 4, 4)

F32 = jnp.float32
BF16 = jnp.bfloat16
VMEM_LIMIT = 32 * 1024 * 1024


def norm_parts(values):
    center = values - jnp.mean(values, -1, keepdims=True)
    inverse = lax.rsqrt(jnp.mean(center * center, -1, keepdims=True) + EPSILON)
    return (center * inverse, inverse)


def norm_back(grad_normed, unit, inverse, scale):
    scaled = grad_normed * scale
    return inverse * (
        scaled
        - jnp.mean(scaled, -1, keepdims=True)
        - unit * jnp.mean(scaled * unit, -1, keepdims=True)
    )


def outer(left, right):
    return lax.dot_general(left, right, (((0,), (0,)), ((), ())), preferred_element_type=F32)


def times_transposed(left, right):
    return lax.dot_general(left, right, (((1,), (1,)), ((), ())), preferred_element_type=F32)


def times(left, right):
    return jnp.dot(left, right, preferred_element_type=F32)


def tie(values, after=()):
    values, after = tuple(values), tuple(after)
    return lax.optimization_barrier(values + after)[: len(values)]


def to_core(value):
    return lax.ppermute(value, "rep", CORE_PAIRS)


def to_x(value):
    return lax.ppermute(value, "rep", X_PAIRS)


def gather_rep(value):
    near, far = to_core(value), to_x(value)
    return [value, near, far, to_core(far)]


def reduce_pair(parts):
    low = parts.astype(BF16)
    arrived = to_core(jnp.stack([low[1], low[3]]))
    return (jnp.stack([low[0], low[2]]).astype(F32) + arrived.astype(F32)).astype(BF16)


def scatter_rep(parts):
    pair = reduce_pair(parts)
    return pair[0].astype(F32) + to_x(pair[1]).astype(F32)


def sum_rep(parts):
    pair = reduce_pair(parts)
    arrived = to_x(pair)
    total = (pair.astype(F32) + arrived[::-1].astype(F32)).astype(BF16)
    near = to_core(total)
    return jnp.stack([total[0], near[0], total[1], near[1]])


def by_owner(slots, me):
    core, far = me % 2 == 1, me // 2 == 1
    a, b, c, d = slots
    a, b, c, d = (
        jnp.where(core, b, a),
        jnp.where(core, a, b),
        jnp.where(core, d, c),
        jnp.where(core, c, d),
    )
    return [jnp.where(far, c, a), jnp.where(far, d, b), jnp.where(far, a, c), jnp.where(far, b, d)]


def gather_shards(pieces, shards):
    return [lax.all_gather(piece, "shard", axis=0) for piece in pieces]


def scatter_shards(whole, shards, rights):
    return lax.psum_scatter(whole, "shard", scatter_dimension=0, tiled=False)


def window(values, start, size):
    part = values[:, start : start + size]
    return jnp.concatenate([part, jnp.zeros((part.shape[0], LANES - size), part.dtype)], 1)


def turned(values, half, lane):
    return jnp.where(
        lane < half,
        pltpu.roll(values, LANES - half, 1),
        pltpu.roll(values, half, 1),
    )


def attend_kernel(
    heads, size, x_ref, gain_ref, shift_ref, w_ref, bias_ref, cos_ref, sin_ref, row_ref, col_ref,
    normed_ref, qkv_ref, lse_ref, out_ref,
):
    unit, _ = norm_parts(x_ref[...].astype(F32))
    normed = (unit * gain_ref[...] + shift_ref[...]).astype(BF16)
    normed_ref[...] = normed
    projected = times(normed, w_ref[...]) + bias_ref[...]
    cosine, sine = cos_ref[...], sin_ref[...]
    rows = projected.shape[0]
    lane = lax.broadcasted_iota(jnp.int32, (rows, LANES), 1)
    same = col_ref[...] == row_ref[0]
    scale = size**-0.5
    half = size // 2
    outs = []
    lses = jnp.zeros((rows, LANES), F32)
    for head in range(heads):
        query, key, value = (
            window(projected, (part * heads + head) * size, size) for part in range(3)
        )
        query = (query * cosine + turned(query, half, lane) * sine).astype(BF16)
        key = (key * cosine + turned(key, half, lane) * sine).astype(BF16)
        value = value.astype(BF16)
        for part, kept in enumerate((query, key, value)):
            at = (part * heads + head) * LANES
            qkv_ref[:, at : at + LANES] = kept
        scores = jnp.where(same, times_transposed(query, key) * scale, MASKED)
        most = jnp.max(scores, -1, keepdims=True)
        expo = jnp.exp(scores - most)
        total = jnp.sum(expo, -1, keepdims=True)
        probs = (expo * (1.0 / total)).astype(BF16)
        outs.append(times(probs, value)[:, :size])
        lses = jnp.where(lane == head, most + jnp.log(total), lses)
    lse_ref[...] = lses
    out_ref[...] = jnp.concatenate(outs, 1).astype(BF16)


def attend(x, gain, shift, weight, bias, cosine, sine, seg_rows, seg_cols, heads, size):
    tokens, width = x.shape
    length = seg_rows.shape[-1]
    part = heads * size
    by_block = lambda columns: pl.BlockSpec((length, columns), lambda i: (i, 0))
    fixed = lambda array: pl.BlockSpec(array.shape, lambda i: (0,) * array.ndim)
    return pl.pallas_call(
        lambda *refs: attend_kernel(heads, size, *refs),
        grid=(tokens // length,),
        in_specs=[
            by_block(width),
            fixed(gain),
            fixed(shift),
            fixed(weight),
            fixed(bias),
            by_block(LANES),
            by_block(LANES),
            pl.BlockSpec((1, 1, length), lambda i: (i, 0, 0)),
            by_block(1),
        ],
        out_specs=[by_block(width), by_block(3 * heads * LANES), by_block(LANES), by_block(part)],
        out_shape=[
            jax.ShapeDtypeStruct((tokens, width), BF16),
            jax.ShapeDtypeStruct((tokens, 3 * heads * LANES), BF16),
            jax.ShapeDtypeStruct((tokens, LANES), F32),
            jax.ShapeDtypeStruct((tokens, part), BF16),
        ],
        compiler_params=pltpu.CompilerParams(vmem_limit_bytes=48 * 1024 * 1024),
        cost_estimate=pl.CostEstimate(
            flops=2 * tokens * width * 3 * part + 4 * tokens * length * part,
            bytes_accessed=4 * tokens * width + weight.size * 2 + tokens * 3 * heads * LANES * 2,
            transcendentals=tokens * length * heads,
        ),
    )(x, gain, shift, weight, bias, cosine, sine, seg_rows, seg_cols)


def attend_back_kernel(
    heads, size, db_ref, wo_ref, qkv_ref, lse_ref, cos_ref, sin_ref, row_ref, col_ref, w_ref,
    x_ref, grad_ref, dn_ref, sum_ref, gain_ref, shift_ref,
):
    mixed = times_transposed(db_ref[...], wo_ref[...])
    cosine, sine = cos_ref[...], sin_ref[...]
    rows = mixed.shape[0]
    lane = lax.broadcasted_iota(jnp.int32, (rows, LANES), 1)
    same = col_ref[...] == row_ref[0]
    scale = size**-0.5
    half = size // 2
    lses = lse_ref[...]
    grads = [None] * (3 * heads)
    for head in range(heads):
        query, key, value = (
            qkv_ref[:, (part * heads + head) * LANES : (part * heads + head + 1) * LANES]
            for part in range(3)
        )
        lse = jnp.sum(jnp.where(lane == head, lses, 0.0), -1, keepdims=True)
        scores = jnp.where(same, times_transposed(query, key) * scale, MASKED)
        probs = jnp.exp(scores - lse)
        grad_mixed = window(mixed, head * size, size).astype(BF16)
        grad_probs = times_transposed(grad_mixed, value)
        grad_value = outer(probs.astype(BF16), grad_mixed)
        inner = jnp.sum(probs * grad_probs, -1, keepdims=True)
        low = (probs * (grad_probs - inner)).astype(BF16)
        grad_query = times(low, key) * scale
        grad_key = outer(low, query) * scale
        grad_query = grad_query * cosine + turned(grad_query * sine, half, lane)
        grad_key = grad_key * cosine + turned(grad_key * sine, half, lane)
        grads[head] = grad_query[:, :size]
        grads[heads + head] = grad_key[:, :size]
        grads[2 * heads + head] = grad_value[:, :size]
    grad = jnp.concatenate(grads, 1).astype(BF16)
    grad_ref[...] = grad
    grad_normed = times_transposed(grad, w_ref[...])
    dn_ref[...] = grad_normed.astype(BF16)
    unit, _ = norm_parts(x_ref[...].astype(F32))

    @pl.when(pl.program_id(0) == 0)
    def _():
        sum_ref[...] = jnp.zeros_like(sum_ref)
        gain_ref[...] = jnp.zeros_like(gain_ref)
        shift_ref[...] = jnp.zeros_like(shift_ref)

    sum_ref[...] += jnp.sum(grad.astype(F32), 0, keepdims=True)
    gain_ref[...] += jnp.sum(grad_normed * unit, 0, keepdims=True)
    shift_ref[...] += jnp.sum(grad_normed, 0, keepdims=True)


def attend_back(db, w_out, qkv, lse, cosine, sine, seg_rows, seg_cols, weight, x, heads, size):
    tokens, width = x.shape
    length = seg_rows.shape[-1]
    part = heads * size
    by_block = lambda columns: pl.BlockSpec((length, columns), lambda i: (i, 0))
    fixed = lambda shape: pl.BlockSpec(shape, lambda i: (0,) * len(shape))
    return pl.pallas_call(
        lambda *refs: attend_back_kernel(heads, size, *refs),
        grid=(tokens // length,),
        in_specs=[
            by_block(width),
            fixed(w_out.shape),
            by_block(3 * heads * LANES),
            by_block(LANES),
            by_block(LANES),
            by_block(LANES),
            pl.BlockSpec((1, 1, length), lambda i: (i, 0, 0)),
            by_block(1),
            fixed(weight.shape),
            by_block(width),
        ],
        out_specs=[
            by_block(3 * part),
            by_block(width),
            fixed((1, 3 * part)),
            fixed((1, width)),
            fixed((1, width)),
        ],
        out_shape=[
            jax.ShapeDtypeStruct((tokens, 3 * part), BF16),
            jax.ShapeDtypeStruct((tokens, width), BF16),
            jax.ShapeDtypeStruct((1, 3 * part), F32),
            jax.ShapeDtypeStruct((1, width), F32),
            jax.ShapeDtypeStruct((1, width), F32),
        ],
        compiler_params=pltpu.CompilerParams(vmem_limit_bytes=48 * 1024 * 1024),
        cost_estimate=pl.CostEstimate(
            flops=2 * tokens * width * 4 * part + 10 * tokens * length * part,
            bytes_accessed=6 * tokens * width + weight.size * 2 + tokens * 3 * heads * LANES * 2,
            transcendentals=tokens * length * heads,
        ),
    )(db, w_out, qkv, lse, cosine, sine, seg_rows, seg_cols, weight, x)


def rotary(rows, columns, size):
    quarter = size // 4
    inverse = 10000.0 ** (-4.0 * jnp.arange(quarter, dtype=F32) / size)
    angles = jnp.concatenate(
        [rows.astype(F32)[:, None] * inverse, columns.astype(F32)[:, None] * inverse], -1
    )
    cosine, sine = jnp.cos(angles), jnp.sin(angles)
    nothing = jnp.zeros((rows.shape[0], LANES - size), F32)
    return (
        jnp.concatenate([cosine, cosine, nothing], -1),
        jnp.concatenate([-sine, sine, nothing], -1),
    )


def on_any(
    shards,
    hidden_in,
    seg_ids,
    patch_rows,
    patch_cols,
    ln1_scale,
    ln1_shift,
    qkv_weight,
    qkv_bias,
    out_weight,
    out_bias,
    ln2_scale,
    ln2_shift,
    up_weight,
    up_bias,
    down_weight,
    down_bias,
    cotangent,
):
    copies = 4
    me = lax.axis_index("rep")
    length, width = hidden_in.shape
    rows = ln1_scale.shape[0]
    size = width // HEADS
    heads = HEADS // copies
    part = heads * size
    hidden = up_weight.shape[1]
    own_hidden = hidden // copies
    step = hidden // shards // copies

    def own(array, axis):
        return lax.dynamic_index_in_dim(array, me, axis, False)

    own_qkv = own(qkv_weight.reshape(rows, 3, copies, part), 2).reshape(rows, 3 * part)
    own_up = own(up_weight.reshape(rows, shards, copies, step), 2).reshape(rows, own_hidden)
    own_down = own(down_weight.reshape(copies, step, width), 0)
    own_out = own(out_weight.reshape(copies, rows // copies, width), 0)
    vectors = (
        ln1_scale, ln1_shift, out_bias, ln2_scale, ln2_shift, down_bias, qkv_bias, up_bias,
    )
    small = jnp.concatenate(vectors)
    small_rows = 8
    small = jnp.pad(small, (0, small_rows * 3 * part - small.size)).reshape(small_rows, 3 * part)
    first, up_full, out_all, down_full = gather_shards(
        [
            jnp.concatenate([own_qkv, small]),
            own_up,
            own_out,
            own_down,
        ],
        shards,
    )
    w_qkv = first[:, :rows].reshape(width, 3 * part)
    small = first[:, rows:].reshape(shards, -1)
    up_full = up_full.reshape(width, own_hidden)
    down_full = down_full.reshape(own_hidden, width)
    full = []
    at = 0
    for vector in vectors:
        full.append(small[:, at : at + vector.size].astype(F32))
        at += vector.size
    gain_one, shift_one, out_offset, gain_two, shift_two, down_offset = (
        v.reshape(1, width) for v in full[:6]
    )
    qkv_offset = own(full[6].reshape(3, copies, part), 1).reshape(1, 3 * part)
    up_offset = own(full[7].reshape(shards, copies, step), 1).reshape(1, own_hidden)

    ids = jnp.concatenate([seg_ids, patch_rows, patch_cols])
    ids = jnp.stack(gather_rep(ids))
    seg_rows, seg_cols = ids[:, :1], ids[:, 0].reshape(-1, 1)
    x_low = jnp.concatenate(gather_rep(hidden_in))
    grad_out = jnp.concatenate(gather_rep(cotangent))
    tokens = x_low.shape[0]
    cosine, sine = rotary(ids[:, 1].reshape(-1), ids[:, 2].reshape(-1), size)

    normed_one, qkv, lse, mixed = attend(
        x_low, gain_one, shift_one, w_qkv, qkv_offset, cosine, sine, seg_rows, seg_cols, heads, size
    )
    out_full = jnp.stack(by_owner(gather_rep(out_all), me), 1).reshape(width, width)
    blocks = mixed.reshape(copies, length, part)
    near, far = to_core(blocks), to_x(blocks)
    both = to_core(far)
    mixed_slots = [
        mixed,
        near[jnp.array([1, 0, 3, 2])].reshape(tokens, part),
        far[jnp.array([2, 3, 0, 1])].reshape(tokens, part),
        both[jnp.array([3, 2, 1, 0])].reshape(tokens, part),
    ]
    mixed_full = jnp.concatenate(by_owner(mixed_slots, me), 1)

    middle = x_low.astype(F32) + times(mixed_full, out_full) + out_offset
    unit_two, inverse_two = norm_parts(middle)
    normed_two = (unit_two * gain_two + shift_two).astype(BF16)
    upward = times(normed_two, up_full) + up_offset
    sigma = jax.nn.sigmoid(GELU_SLOPE * upward)
    activated = (upward * sigma).astype(BF16)
    slope = sigma + GELU_SLOPE * upward * sigma * (1.0 - sigma)

    grad_down = outer(activated, grad_out).astype(BF16)
    grad_up_low = (times_transposed(grad_out, down_full) * slope).astype(BF16)
    grad_normed_two = sum_rep(times_transposed(grad_up_low, up_full).reshape(copies, length, width))
    grad_up = outer(normed_two, grad_up_low).astype(BF16)
    grad_up_bias = jnp.sum(grad_up_low.astype(F32), 0)
    branch = scatter_rep(times(activated, down_full).reshape(copies, length, width))
    output = middle[:length] + branch + down_offset

    grad_normed_two = grad_normed_two.reshape(tokens, width).astype(F32)
    grad_middle = grad_out.astype(F32) + norm_back(
        grad_normed_two, unit_two, inverse_two, gain_two
    )
    grad_branch = grad_middle.astype(BF16)
    grad_out_w = outer(mixed_full, own(grad_branch.reshape(tokens, copies, part), 1)).astype(BF16)

    own_w_out = lax.dynamic_slice_in_dim(out_full, me * part, part, 0)
    grad_qkv_low, grad_normed_one, sum_qkv, sum_gain, sum_shift = attend_back(
        grad_branch, own_w_out, qkv, lse, cosine, sine, seg_rows, seg_cols, w_qkv, x_low, heads, size
    )
    grad_qkv = outer(normed_one, grad_qkv_low).astype(BF16)
    grad_normed_one = scatter_rep(grad_normed_one.reshape(copies, length, width))
    unit_one, inverse_one = norm_parts(hidden_in.astype(F32))
    grad_inputs = grad_middle[:length] + norm_back(grad_normed_one, unit_one, inverse_one, gain_one)

    def sum_of(values):
        return jnp.sum(values[:length], 0).reshape(shards, rows)

    def placed(values, like, axis):
        return lax.dynamic_update_index_in_dim(jnp.zeros(like, F32), values, me, axis)

    sums = [
        sum_gain.reshape(shards, rows),
        sum_shift.reshape(shards, rows),
        sum_of(grad_branch.astype(F32)),
        sum_of(grad_normed_two * unit_two),
        sum_of(grad_normed_two),
        sum_of(grad_out.astype(F32)),
        placed(sum_qkv.reshape(3, part), (3, copies, part), 1).reshape(shards, -1),
        placed(grad_up_bias.reshape(shards, step), (shards, copies, step), 1).reshape(shards, -1),
    ]
    sums = jnp.concatenate(sums, 1)
    sums = jnp.pad(sums, ((0, 0), (0, small_rows * 3 * part - sums.shape[1])))
    last = jnp.concatenate(
        [grad_qkv.reshape(shards, rows, 3 * part), sums.astype(BF16).reshape(shards, small_rows, -1)],
        1,
    )

    done_down = scatter_shards(grad_down.reshape(shards, step, width), shards, 4)
    done_up = scatter_shards(grad_up.reshape(shards, rows, own_hidden), shards, 3)
    done_out = scatter_shards(grad_out_w.reshape(shards, rows, part), shards, 4)
    done_last = scatter_shards(last, shards, 4)

    whole_down = jnp.concatenate(by_owner(gather_rep(done_down), me), 0).astype(F32)
    whole_up = jnp.stack(
        [p.reshape(rows, shards, step) for p in by_owner(gather_rep(done_up), me)], 2
    )
    whole_up = whole_up.reshape(rows, hidden).astype(F32)
    whole_out = jnp.concatenate(by_owner(gather_rep(done_out), me), 1).astype(F32)
    last_slots = gather_rep(done_last)
    whole_qkv = jnp.stack(
        [p[:rows].reshape(rows, 3, part) for p in by_owner(last_slots, me)], 2
    )
    whole_qkv = whole_qkv.reshape(rows, 3 * width).astype(F32)
    summed = sum(p[rows:].astype(F32) for p in by_owner(last_slots, me)).reshape(-1)
    totals = []
    at = 0
    for vector in vectors:
        totals.append(summed[at : at + vector.size])
        at += vector.size
    return (
        output.astype(BF16),
        grad_inputs.astype(BF16),
        totals[0],
        totals[1],
        whole_qkv,
        totals[6],
        whole_out,
        totals[2],
        totals[3],
        totals[4],
        whole_up,
        totals[7],
        whole_down,
        totals[5],
    )


def ring_slots():
    position = jnp.asarray(RING_AT, jnp.int32)[lax.axis_index("shard")]
    return jnp.asarray(RING, jnp.int32)[(position + jnp.asarray(OFFSETS, jnp.int32)) % 8]


def half_of(rows):
    return (rows // 2 + 15) // 16 * 16


def ring_gather(piece, after=(), others=None):
    right = left = piece
    if after:
        right, left = tie((piece, piece), after)
    pieces = [piece]
    for hop in range(4):
        if hop == 3:
            cut = half_of(piece.shape[0])
            right, left = right[:cut], left[cut:]
        right, left = tie(
            (lax.ppermute(right, "shard", RIGHT), lax.ppermute(left, "shard", LEFT)),
            (others or {}).get(hop, ()),
        )
        pieces += [right, left]
    return pieces


def ring_scatter(whole, slots, others, last):
    cut = half_of(whole.shape[1])

    def own(number):
        return lax.dynamic_index_in_dim(whole, slots[number], 0, False)

    def add_low(one, other):
        return (one.astype(F32) + other.astype(F32)).astype(BF16)

    far = own(7)
    right, left = far[:cut], far[cut:]
    for hop in range(4):
        right, left = tie(
            (lax.ppermute(right, "shard", RIGHT), lax.ppermute(left, "shard", LEFT)),
            others.get(hop, ()),
        )
        if hop == 3:
            break
        ahead, behind = own(6 - 2 * hop), own(5 - 2 * hop)
        if hop == 0:
            right = jnp.concatenate([add_low(right, ahead[:cut]), ahead[cut:]])
            left = jnp.concatenate([behind[:cut], add_low(left, behind[cut:])])
        else:
            right, left = add_low(right, ahead), add_low(left, behind)
        if hop == 2:
            right, left, last = tie((right, left, last))
    return (right.astype(F32) + left.astype(F32) + own(0).astype(F32)).astype(BF16), last


def run_copies(copies):
    for copy in copies:
        copy.start()
    for copy in copies:
        copy.wait()


ANYWHERE = pl.BlockSpec(memory_space=pl.ANY)
SCALARS = pl.BlockSpec(memory_space=pltpu.SMEM)
WHOLE = pl.BlockSpec(memory_space=pltpu.VMEM)


def params():
    return pltpu.CompilerParams(vmem_limit_bytes=VMEM_LIMIT)


def fixed(shape):
    return pl.BlockSpec(shape, lambda i: (0,) * len(shape))


def cost(microseconds=0):
    return pl.CostEstimate(flops=1, bytes_accessed=1 + microseconds * 3_690_000, transcendentals=0)


def like(shape, dtype):
    return jax.ShapeDtypeStruct(shape, dtype)


def far(shape, dtype):
    return pltpu.HBM(shape, dtype)


def kept_far(arrays):
    return [pltpu.with_memory_space_constraint(a, pltpu.HBM) for a in arrays]


def joined(slots):
    return jnp.concatenate(slots, 0)


def column_order(heads, size):
    half = size // 2
    left = heads * half - LANES
    order = np.zeros((2 * heads * size, 2 * heads * size), np.float32)
    for part in range(2):
        for head in range(heads):
            for side in range(2):
                for feature in range(half):
                    natural = (part * heads + head) * size + side * half + feature
                    at = head * half + feature
                    group = 2 * part + side
                    to = group * LANES + at if at < LANES else (4 * LANES + group * left + at - LANES)
                    order[natural, to] = 1.0
    return jnp.asarray(order, BF16)


def head_masks(heads, size):
    half = size // 2
    left = heads * half - LANES
    masks = np.zeros((2 * heads, 3 * LANES), np.float32)
    for head in range(heads):
        for lane in range(2 * LANES):
            masks[head, lane] = (lane % LANES) // half == head
        for lane in range(2 * left):
            masks[head, 2 * LANES + lane] = (LANES + lane % left) // half == head
        masks[heads + head, head * size : (head + 1) * size] = 1.0
    return jnp.asarray(masks, F32)


def rotary_tiles(rows, columns, heads, size):
    half, quarter = size // 2, size // 4
    left = heads * half - LANES
    at = np.concatenate([np.arange(LANES), LANES + np.arange(4 * left) % left]) % half
    inverse = 10000.0 ** (-4.0 * jnp.arange(quarter, dtype=F32) / size)
    inverse = inverse[at % quarter]
    by_row = jnp.where(jnp.asarray(at < quarter), inverse, 0.0)
    by_column = jnp.where(jnp.asarray(at < quarter), 0.0, inverse)
    angles = rows.astype(F32)[:, None] * by_row + columns.astype(F32)[:, None] * by_column
    sign = np.ones(2 * LANES, np.float32)
    for group in (0, 2):
        sign[LANES + group * left : LANES + (group + 1) * left] = -1.0
    return jnp.cos(angles), jnp.sin(angles) * jnp.asarray(sign)


def first_kernel(part, *refs):
    me_ref, order_ref, weight_ref, other_ref = refs[:4]
    vectors, out_ref = refs[4:12], refs[12]
    rows, width = out_ref.shape[0] - EXTRA, out_ref.shape[1]
    for me in range(COPIES):

        @pl.when(me_ref[0] == me)
        def _():
            parts = [
                weight_ref[:, (n * COPIES + me) * part : (n * COPIES + me + 1) * part]
                for n in range(3)
            ]
            turned = times(jnp.concatenate(parts[:2], 1), order_ref[...]).astype(BF16)
            out_ref[:rows] = jnp.concatenate(
                [turned, parts[2], other_ref[:, me * part : (me + 1) * part]], 1
            )

    lines = [v[...].astype(F32).reshape(1, -1) for v in vectors]
    lines = [jnp.concatenate(lines[:6], 1), lines[6], lines[7]]
    lines = [
        jnp.concatenate([line, jnp.zeros((1, width - line.shape[1]), F32)], 1) for line in lines
    ]
    lines.append(jnp.zeros((EXTRA - len(lines), width), F32))
    out_ref[rows:] = jnp.concatenate(lines, 0).astype(BF16)


def first_piece(me, order, weight, other, vectors, part):
    rows = weight.shape[0]
    return pl.pallas_call(
        lambda *refs: first_kernel(part, *refs),
        in_specs=[SCALARS] + [WHOLE] * 11,
        out_specs=WHOLE,
        out_shape=like((rows + EXTRA, COPIES * part), BF16),
        compiler_params=params(),
        cost_estimate=cost(),
    )(me, *kept_far([order, weight, other, *vectors]))


def collect_kernel(rows, *refs):
    pieces, (out_ref, lines_ref, semaphores) = refs[:9], refs[9:]
    lanes = lines_ref.shape[2]
    part = out_ref.shape[1] // COPIES
    copies = []
    for number, ref in enumerate(pieces):
        edge = half_of(rows + EXTRA)
        start, count = (edge, rows - edge) if number == 8 else (0, edge if number == 7 else rows)
        copies.append(
            pltpu.make_async_copy(
                ref.at[pl.ds(0, count), pl.ds(ref.shape[1] - lanes, lanes)],
                lines_ref.at[min(number, 7), pl.ds(start, count)],
                semaphores.at[number],
            )
        )
    run_copies(copies)
    for line in range(2):
        out_ref[line * rows : (line + 1) * rows] = jnp.concatenate(
            [lines_ref[2 * n + line][:, lanes - part :] for n in range(COPIES)], 1
        )


def collect(pieces, rows, part):
    lanes = -(-part // LANES) * LANES
    return pl.pallas_call(
        lambda *refs: collect_kernel(rows, *refs),
        in_specs=[ANYWHERE] * len(pieces),
        out_specs=WHOLE,
        out_shape=like((2 * rows, COPIES * part), BF16),
        scratch_shapes=[pltpu.VMEM((8, rows, lanes), BF16), pltpu.SemaphoreType.DMA((9,))],
        compiler_params=params(),
        cost_estimate=cost(),
    )(*kept_far(pieces))


def second_kernel(shards, me_ref, up_ref, down_ref, out_ref):
    rows, hidden = up_ref.shape
    step = hidden // shards // COPIES
    for me in range(COPIES):

        @pl.when(me_ref[0] == me)
        def _():
            out_ref[:rows] = jnp.concatenate(
                [
                    up_ref[:, (n * COPIES + me) * step : (n * COPIES + me + 1) * step]
                    for n in range(shards)
                ],
                1,
            )
            out_ref[rows:] = down_ref[me * step : (me + 1) * step]


def second_piece(me, up, down, shards):
    rows, hidden = up.shape
    step = hidden // shards // COPIES
    return pl.pallas_call(
        lambda *refs: second_kernel(shards, *refs),
        in_specs=[SCALARS] + [WHOLE] * 2,
        out_specs=WHOLE,
        out_shape=like((rows + step, hidden // COPIES), BF16),
        compiler_params=params(),
        cost_estimate=cost(),
    )(me, *kept_far([up, down]))


def first_copies(refs, place, rows, w_ref, small_ref, semaphores):
    cut = half_of(rows + EXTRA)
    copies = []
    for number, ref in enumerate(refs):
        slot = place[number]
        start, count = (cut, rows - cut) if number == 8 else (0, cut if number == 7 else rows)
        at = pl.multiple_of(slot * rows + start, 16)
        copies.append(
            pltpu.make_async_copy(
                ref.at[pl.ds(0, count), pl.ds(0, w_ref.shape[1])],
                w_ref.at[pl.ds(at, count)],
                semaphores.at[0, number],
            )
        )
        if number != 7 and small_ref is not None:
            copies.append(
                pltpu.make_async_copy(
                    ref.at[pl.ds(count, EXTRA)], small_ref.at[slot], semaphores.at[1, number]
                )
            )
    return copies


def vectors_of(me_ref, small_ref, order_ref, vec_ref, bias_ref, full_ref):
    shards = small_ref.shape[0]
    width = vec_ref.shape[1]
    rows = width // shards
    part = width // COPIES
    lines = [small_ref[s].astype(F32) for s in range(shards)]
    for n in range(6):
        vec_ref[n : n + 1] = jnp.concatenate(
            [line[0:1, n * rows : (n + 1) * rows] for line in lines], 1
        )
    full_ref[...] = jnp.concatenate([line[1:2, : 3 * rows] for line in lines], 1)
    vec_ref[7:8] = jnp.zeros((1, width), F32)
    bias_ref[...] = jnp.zeros_like(bias_ref)
    for me in range(COPIES):

        @pl.when(me_ref[0] == me)
        def _():
            vec_ref[6:7] = jnp.concatenate(
                [line[2:3, me * rows : (me + 1) * rows] for line in lines], 1
            )
            parts = [
                full_ref[:, (n * COPIES + me) * part : (n * COPIES + me + 1) * part] for n in range(3)
            ]
            both = jnp.broadcast_to(jnp.concatenate(parts[:2], 1), (8, 2 * part)).astype(BF16)
            bias_ref[:, : 2 * part] = times(both, order_ref[...])[:1]
            bias_ref[:, 2 * part : 3 * part] = parts[2]


def swapped(values, lane, left):
    return jnp.where(
        lane // left % 2 == 0,
        pltpu.roll(values, LANES - left, 1),
        pltpu.roll(values, left, 1),
    )


def tiles(values, count):
    return [values[:, n * LANES : (n + 1) * LANES] for n in range(count)]


def ring_attend_kernel(heads, size, *refs):
    (
        me_ref, place_ref, order_ref, mask_ref, x0, x1, x2, x3, cos_ref, sin_ref, row_ref, col_ref,
    ), refs = refs[:12], refs[12:]
    pieces, refs = refs[:9], refs[9:]
    (
        normed_ref, qkv_ref, lse_ref, out_ref, vec_ref, w_ref, small_ref, bias_ref, full_ref, all_ref,
        project_ref, semaphores,
    ) = refs
    i = pl.program_id(0)
    length, width = x0.shape
    rows = width // 8
    part = heads * size

    @pl.when(i == 0)
    def _():
        copies = first_copies(pieces, place_ref, rows, w_ref, small_ref, semaphores)
        for copy in copies:
            copy.start()
        for copy in copies[1:14:2] + copies[-1:]:
            copy.wait()
        vectors_of(me_ref, small_ref, order_ref, vec_ref, bias_ref, full_ref)
        for slot, x_ref in enumerate((x0, x1, x2, x3)):
            unit, _ = norm_parts(x_ref[...].astype(F32))
            all_ref[slot * length : (slot + 1) * length] = (
                unit * vec_ref[0:1] + vec_ref[1:2]
            ).astype(BF16)
        for copy in copies[0:14:2] + copies[14:16]:
            copy.wait()
        project_ref[...] = times(all_ref[...], w_ref[...]) + bias_ref[...]

    here = pl.ds(pl.multiple_of(i * length, 16), length)
    normed_ref[...] = all_ref[here, :]
    q1, q2, k1, k2, rest = tiles(project_ref[here, : 5 * LANES], 5)
    value = project_ref[here, 5 * LANES :]
    lane = lax.broadcasted_iota(jnp.int32, (length, LANES), 1)
    wide = lax.broadcasted_iota(jnp.int32, (length, 3 * LANES), 1)
    cosine, cosine_rest = tiles(cos_ref[...], 2)
    sine, sine_rest = tiles(sin_ref[...], 2)
    left = heads * size // 2 - LANES
    rest = rest * cosine_rest + swapped(rest, lane, left) * sine_rest
    query = jnp.concatenate(
        [q1 * cosine - q2 * sine, q2 * cosine + q1 * sine, jnp.where(lane < 2 * left, rest, 0.0)], 1
    ).astype(BF16)
    key = jnp.concatenate(
        [
            k1 * cosine - k2 * sine,
            k2 * cosine + k1 * sine,
            jnp.where(lane < 2 * left, pltpu.roll(rest, 2 * left, 1), 0.0),
        ],
        1,
    ).astype(BF16)
    value = jnp.where(wide < part, value, 0.0).astype(BF16)
    qkv_ref[...] = jnp.concatenate([query, key, value], 1)
    masks = mask_ref[...].astype(BF16)
    same = col_ref[...] == row_ref[0]
    scale = size**-0.5
    all_probs, all_values = [], []
    lses = jnp.zeros((length, LANES), F32)
    for head in range(heads):
        scores = times_transposed(query * masks[head : head + 1], key)
        scores = jnp.where(same, scores * scale, MASKED)
        most = jnp.max(scores, -1, keepdims=True)
        expo = jnp.exp(scores - most)
        total = jnp.sum(expo, -1, keepdims=True)
        all_probs.append((expo * (1.0 / total)).astype(BF16))
        all_values.append(value * masks[heads + head : heads + head + 1])
        lses = jnp.where(lane == head, most + jnp.log(total), lses)
    lse_ref[...] = lses
    out = times(jnp.concatenate(all_probs, 1), joined(all_values))[:, :part].astype(BF16)
    count = out_ref.shape[1]
    out_ref[0] = jnp.concatenate([out[n * count : (n + 1) * count] for n in range(COPIES)], 1)


def ring_attend(me, place, order, masks, x, cosine, sine, seg_rows, seg_cols, pieces, heads, size):
    length, width = x[0].shape
    tokens = COPIES * length
    by_block = lambda columns: pl.BlockSpec((length, columns), lambda i: (i, 0))
    return pl.pallas_call(
        lambda *refs: ring_attend_kernel(heads, size, *refs),
        grid=(COPIES,),
        in_specs=[SCALARS, SCALARS, fixed(order.shape), fixed(masks.shape)]
        + [fixed((length, width))] * COPIES
        + [
            by_block(2 * LANES),
            by_block(2 * LANES),
            pl.BlockSpec((1, 1, length), lambda i: (i, 0, 0)),
            by_block(1),
        ]
        + [ANYWHERE] * len(pieces),
        out_specs=[
            by_block(width),
            by_block(9 * LANES),
            by_block(LANES),
            pl.BlockSpec((1, length // COPIES, width), lambda i: (i, 0, 0)),
            fixed((8, width)),
        ],
        out_shape=[
            far((tokens, width), BF16),
            far((tokens, 9 * LANES), BF16),
            far((tokens, LANES), F32),
            like((COPIES, length // COPIES, width), BF16),
            like((8, width), F32),
        ],
        scratch_shapes=[
            pltpu.VMEM((width, 8 * LANES), BF16),
            pltpu.VMEM((8, EXTRA, width), BF16),
            pltpu.VMEM((1, 8 * LANES), F32),
            pltpu.VMEM((1, 3 * width), F32),
            pltpu.VMEM((tokens, width), BF16),
            pltpu.VMEM((tokens, 8 * LANES), F32),
            pltpu.SemaphoreType.DMA((2, len(pieces))),
        ],
        compiler_params=params(),
        cost_estimate=cost(25),
    )(
        me, place, *kept_far([order, masks, *x, cosine, sine]), seg_rows, seg_cols, *kept_far(pieces)
    )


def middle_kernel(rows, part, *refs):
    me_ref, place_ref, own_ref, near_ref, far_ref, both_ref, vec_ref, x0, x1, x2, x3 = refs[:11]
    weights, (all_ref, middle_ref, normed_ref, wown_ref, w_ref, x_ref) = (
        refs[11:15],
        refs[15:],
    )
    j = pl.program_id(0)

    @pl.when(j == 0)
    def _():
        me = me_ref[0]
        for own in range(COPIES):

            @pl.when(me == own)
            def _():
                for n in range(8):
                    here = slice(n % 2 * rows, (n % 2 + 1) * rows)
                    lanes = slice(n // 2 * part, (n // 2 + 1) * part)
                    at = pl.multiple_of(place_ref[n] * rows, 16)
                    w_ref[pl.ds(at, rows), :] = jnp.concatenate(
                        [weights[own ^ b][here, lanes] for b in range(COPIES)], 1
                    )

        wown_ref[...] = w_ref[pl.ds(pl.multiple_of(me * part, 16), part), :]
        x_ref[...] = joined([x0[...], x1[...]])

    @pl.when(j == 1)
    def _():
        x_ref[...] = joined([x2[...], x3[...]])

    def unpacked(ref, order):
        return joined(
            [ref[b, :, n * part : (n + 1) * part] for b in order for n in range(COPIES)]
        )

    slots = [
        unpacked(own_ref, (0, 1)),
        unpacked(near_ref, (1, 0)),
        unpacked(far_ref, (0, 1)),
        unpacked(both_ref, (1, 0)),
    ]
    for me in range(COPIES):

        @pl.when(me_ref[0] == me)
        def _():
            all_ref[...] = jnp.concatenate([slots[me ^ n] for n in range(COPIES)], 1)

    middle = x_ref[...].astype(F32) + times(all_ref[...], w_ref[...]) + vec_ref[2:3]
    unit, _ = norm_parts(middle)
    normed = (unit * vec_ref[3:4] + vec_ref[4:5]).astype(BF16)
    length = middle_ref.shape[2]
    for core in range(2):
        middle_ref[0, core] = middle[core * length : (core + 1) * length]
        normed_ref[0, core] = normed[core * length : (core + 1) * length]


def middle_of(me, place, mixed, vec, x, weights, rows):
    length, width = x[0].shape
    part = width // COPIES
    tokens = COPIES * length
    by_slots = lambda flip: pl.BlockSpec(
        (2,) + mixed[0].shape[1:], lambda j: ((1 - j) if flip else j, 0, 0)
    )
    by_half = pl.BlockSpec((1, 2, length, width), lambda j: (j, 0, 0, 0))
    return pl.pallas_call(
        lambda *refs: middle_kernel(rows, part, *refs),
        grid=(2,),
        in_specs=[SCALARS, SCALARS]
        + [by_slots(False), by_slots(False), by_slots(True), by_slots(True), fixed(vec.shape)]
        + [fixed((length, width))] * COPIES
        + [fixed(weights[0].shape)] * COPIES,
        out_specs=[
            pl.BlockSpec((2 * length, width), lambda j: (j, 0)),
            by_half,
            by_half,
            fixed((part, width)),
        ],
        out_shape=[
            far((tokens, width), BF16),
            far((2, 2, length, width), F32),
            like((2, 2, length, width), BF16),
            far((part, width), BF16),
        ],
        scratch_shapes=[
            pltpu.VMEM((width, width), BF16),
            pltpu.VMEM((2 * length, width), BF16),
        ],
        compiler_params=params(),
        cost_estimate=cost(13),
    )(me, place, *mixed, vec, *kept_far([*x, *weights]))


def split_copies(pieces, place, up_ref, down_ref, semaphores):
    copies = []
    for number, ref in enumerate(pieces):
        for line, target in enumerate((up_ref, down_ref)):
            if target is None or (number == 7 and line == 1) or (number == 8 and line == 0):
                continue
            count = target.shape[0] // 8
            copies.append(
                pltpu.make_async_copy(
                    ref.at[pl.ds(count if line == 1 and number < 7 else 0, count)],
                    target.at[pl.ds(pl.multiple_of(place[number] * count, 16), count)],
                    semaphores.at[line, number],
                )
            )
    return copies


def feed_kernel(place_ref, normed_ref, g0, g1, g2, g3, vec_ref, *refs):
    pieces, refs = refs[:9], refs[9:]
    act_ref, dh_ref, sent_ref, kept_ref, sum_ref, up_ref, down_ref, grad_ref, semaphores = refs
    j = pl.program_id(0)

    @pl.when(j == 0)
    def _():
        run_copies(split_copies(pieces, place_ref, up_ref, down_ref, semaphores))
        sum_ref[...] = jnp.zeros_like(sum_ref)
        sum_ref[1:2] = jnp.sum(g0[...].astype(F32), 0, keepdims=True)
        grad_ref[...] = joined([g1[...], g3[...]])

    @pl.when(j == 1)
    def _():
        grad_ref[...] = joined([g0[...], g2[...]])

    normed = joined([normed_ref[0, 0], normed_ref[1, 0]])
    upward = times(normed, up_ref[...]) + vec_ref[6:7]
    sigma = jax.nn.sigmoid(GELU_SLOPE * upward)
    act = (upward * sigma).astype(BF16)
    slope = sigma + GELU_SLOPE * upward * sigma * (1.0 - sigma)
    low = (times_transposed(grad_ref[...], down_ref[...]) * slope).astype(BF16)
    sum_ref[0:1] += jnp.sum(low.astype(F32), 0, keepdims=True)
    back = times_transposed(low, up_ref[...]).astype(BF16)
    length = normed_ref.shape[2]
    for half in range(2):
        here = slice(half * length, (half + 1) * length)
        act_ref[half, 0] = act[here]
        dh_ref[half, 0] = low[here]

    @pl.when(j == 0)
    def _():
        for half in range(2):
            sent_ref[half] = back[half * length : (half + 1) * length]

    @pl.when(j == 1)
    def _():
        for half in range(2):
            kept_ref[half] = back[half * length : (half + 1) * length]


def feed(place, normed, grad, vec, pieces, hidden):
    _, _, length, width = normed.shape
    by_core = lambda columns: pl.BlockSpec((2, 1, length, columns), lambda j: (0, 1 - j, 0, 0))
    pair = like((2, length, width), BF16)
    return pl.pallas_call(
        feed_kernel,
        grid=(2,),
        in_specs=[SCALARS, by_core(width)]
        + [fixed((length, width))] * COPIES
        + [fixed(vec.shape)]
        + [ANYWHERE] * len(pieces),
        out_specs=[
            by_core(hidden),
            by_core(hidden),
            fixed((2, length, width)),
            fixed((2, length, width)),
            fixed((8, hidden)),
        ],
        out_shape=[
            like((2, 2, length, hidden), BF16),
            like((2, 2, length, hidden), BF16),
            pair,
            pair,
            like((8, hidden), F32),
        ],
        scratch_shapes=[
            pltpu.VMEM((width, hidden), BF16),
            pltpu.VMEM((hidden, width), BF16),
            pltpu.VMEM((2 * length, width), BF16),
            pltpu.SemaphoreType.DMA((2, 9)),
        ],
        compiler_params=params(),
        cost_estimate=cost(20),
    )(place, normed, *kept_far(grad), vec, *kept_far(pieces))


def down_kernel(place_ref, act_ref, *refs):
    pieces, (sent_ref, kept_ref, down_ref, semaphores) = refs[:9], refs[9:]
    j = pl.program_id(0)

    @pl.when(j == 0)
    def _():
        run_copies(split_copies(pieces, place_ref, None, down_ref, semaphores))

    value = times(joined([act_ref[0, 0], act_ref[1, 0]]), down_ref[...]).astype(BF16)
    length = act_ref.shape[2]

    @pl.when(j == 0)
    def _():
        for half in range(2):
            sent_ref[half] = value[half * length : (half + 1) * length]

    @pl.when(j == 1)
    def _():
        for half in range(2):
            kept_ref[half] = value[half * length : (half + 1) * length]


def down_of(place, act, pieces, width):
    _, _, length, hidden = act.shape
    pair = like((2, length, width), BF16)
    return pl.pallas_call(
        down_kernel,
        grid=(2,),
        in_specs=[SCALARS, pl.BlockSpec((2, 1, length, hidden), lambda j: (0, 1 - j, 0, 0))]
        + [ANYWHERE] * len(pieces),
        out_specs=[fixed((2, length, width)), fixed((2, length, width))],
        out_shape=[pair, pair],
        scratch_shapes=[pltpu.VMEM((hidden, width), BF16), pltpu.SemaphoreType.DMA((2, 9))],
        compiler_params=params(),
        cost_estimate=cost(),
    )(place, act, *kept_far(pieces))


def feed_grad_kernel(normed_ref, act_ref, dh_ref, g0, g1, g2, g3, out_ref):
    i = pl.program_id(0)
    half = pl.num_programs(0) // 2
    width = normed_ref.shape[1]
    rows = width * half // 8

    def put(value, start):
        first = lax.rem(i, half) * width
        for n in range(width // 32):
            at = first + 32 * n
            shard = lax.div(at, rows)
            row = pl.multiple_of(at - shard * rows + start, 32)
            out_ref[shard, pl.ds(row, 32)] = value[32 * n : 32 * n + 32]

    @pl.when(i < half)
    def _():
        put(outer(normed_ref[...], dh_ref[...]).astype(BF16), 0)

    @pl.when(i >= half)
    def _():
        grad = joined([g0[...], g1[...], g2[...], g3[...]])
        put(outer(act_ref[...], grad).astype(BF16), rows)


def feed_grads(normed, act, dh, grad):
    tokens, width = normed.shape
    length = grad[0].shape[0]
    block = 256
    half = width // block
    return pl.pallas_call(
        feed_grad_kernel,
        grid=(2 * half,),
        in_specs=[
            pl.BlockSpec((tokens, block), lambda i: (0, jnp.minimum(i, half - 1))),
            pl.BlockSpec((tokens, block), lambda i: (0, jnp.maximum(i - half, 0))),
            fixed(dh.shape),
        ]
        + [fixed((length, width))] * COPIES,
        out_specs=fixed((8, width // 4, width)),
        out_shape=far((8, width // 4, width), BF16),
        compiler_params=params(),
        cost_estimate=cost(),
    )(normed, act, dh, *kept_far(grad))


def ring_back_kernel(heads, size, *refs):
    (
        me_ref, place_ref, order_ref, mask_ref, total_ref, near_ref, middle_ref, g0, g1, g2, g3, x0, x1, x2,
        x3, vec_ref, wo_ref, qkv_ref, lse_ref, cos_ref, sin_ref, row_ref, col_ref,
    ), refs = refs[:23], refs[23:]
    pieces, refs = refs[:9], refs[9:]
    cols_ref, grad_ref, sent_ref, kept_ref, dx_ref, sums_ref, w_ref, cot_ref, all_ref, semaphores = refs
    i = pl.program_id(0)
    length, width = x0.shape
    rows = width // 8
    part = heads * size
    turns = (1, 3, 0, 2)

    @pl.when(i == 0)
    def _():
        for copy in first_copies(pieces, place_ref, rows, w_ref, None, semaphores):
            copy.start()
        sums_ref[...] = jnp.zeros_like(sums_ref)

    for n, slot in enumerate(turns):

        @pl.when(i == n)
        def _():
            cot_ref[...] = (g0, g1, g2, g3)[slot][...].astype(F32)

    grad_normed = jnp.where(i < 2, near_ref[0], total_ref[0]).astype(F32)
    unit, inverse = norm_parts(middle_ref[0, 0])
    grad_middle = cot_ref[...] + norm_back(grad_normed, unit, inverse, vec_ref[3:4])
    branch = grad_middle.astype(BF16)

    @pl.when(i == 2)
    def _():
        dx_ref[...] = grad_middle
        sums_ref[2:3] = jnp.sum(branch.astype(F32), 0, keepdims=True)
        sums_ref[3:4] = jnp.sum(grad_normed * unit, 0, keepdims=True)
        sums_ref[4:5] = jnp.sum(grad_normed, 0, keepdims=True)

    for me in range(COPIES):

        @pl.when(me_ref[0] == me)
        def _():
            cols_ref[...] = branch[:, me * part : (me + 1) * part]

    mixed = times_transposed(branch, wo_ref[...]).astype(BF16)
    mixed = jnp.concatenate([mixed, jnp.zeros((length, 3 * LANES - part), BF16)], 1)
    query, key, value = (qkv_ref[:, 3 * n * LANES : 3 * (n + 1) * LANES] for n in range(3))
    masks = mask_ref[...].astype(BF16)
    same = col_ref[...] == row_ref[0]
    scale = size**-0.5
    lses = lse_ref[...]
    all_probs, all_lows, queries, keys, mixes = [], [], [], [], []
    for head in range(heads):
        queries.append(query * masks[head : head + 1])
        keys.append(key * masks[head : head + 1])
        mixes.append(mixed * masks[heads + head : heads + head + 1])
        scores = jnp.where(same, times_transposed(queries[-1], key) * scale, MASKED)
        probs = jnp.exp(scores - lses[:, head : head + 1])
        grad_probs = times_transposed(mixes[-1], value)
        inner = jnp.sum(probs * grad_probs, -1, keepdims=True)
        all_probs.append(probs.astype(BF16))
        all_lows.append((probs * (grad_probs - inner)).astype(BF16))
    grad_query = times(jnp.concatenate(all_lows, 1), joined(keys)) * scale
    grad_key = outer(joined(all_lows), joined(queries)) * scale
    grad_value = outer(joined(all_probs), joined(mixes)).astype(BF16)
    lane = lax.broadcasted_iota(jnp.int32, (length, LANES), 1)
    cosine, cosine_rest = tiles(cos_ref[...], 2)
    sine, sine_rest = tiles(sin_ref[...], 2)
    left = heads * size // 2 - LANES
    q1, q2, q_rest = tiles(grad_query, 3)
    k1, k2, k_rest = tiles(grad_key, 3)
    rest = jnp.where(lane < 2 * left, q_rest, pltpu.roll(k_rest, 2 * left, 1))
    rest = rest * cosine_rest + swapped(rest * sine_rest, lane, left)
    grad = jnp.concatenate(
        [
            q1 * cosine + q2 * sine,
            q2 * cosine - q1 * sine,
            k1 * cosine + k2 * sine,
            k2 * cosine - k1 * sine,
            rest,
        ],
        1,
    ).astype(BF16)
    here = pl.ds(pl.multiple_of(i * length, 16), length)
    all_ref[here, :] = jnp.concatenate([grad, grad_value], 1)
    natural = times_transposed(grad, order_ref[...])
    grad_ref[:, : 2 * part] = natural.astype(BF16)
    grad_ref[:, 2 * part :] = grad_value[:, :part]
    sums_ref[5:6, : 2 * part] += jnp.sum(natural, 0, keepdims=True)
    sums_ref[5:6, 2 * part : 3 * part] += jnp.sum(grad_value[:, :part].astype(F32), 0, keepdims=True)

    @pl.when(i == COPIES - 1)
    def _():
        for copy in first_copies(pieces, place_ref, rows, w_ref, None, semaphores):
            copy.wait()
        for out_ref, base in ((sent_ref, 0), (kept_ref, 2)):
            share = times_transposed(all_ref[base * length : (base + 2) * length], w_ref[...])
            for n in range(2):
                here = share[n * length : (n + 1) * length]
                unit, _ = norm_parts((x0, x1, x2, x3)[turns[base + n]][...].astype(F32))
                sums_ref[0:1] += jnp.sum(here * unit, 0, keepdims=True)
                sums_ref[1:2] += jnp.sum(here, 0, keepdims=True)
                out_ref[n] = here.astype(BF16)


def ring_back(
    me, place, order, masks, total, near, middle, grad, x, vec, w_own, qkv, lse, cosine, sine, seg_rows,
    seg_cols, pieces, heads, size,
):
    length, width = x[0].shape
    tokens = COPIES * length
    part = heads * size
    slot = lambda i: jnp.where(i < 2, 2 * i + 1, 2 * i - 4)
    by_block = lambda columns: pl.BlockSpec((length, columns), lambda i: (slot(i), 0))
    return pl.pallas_call(
        lambda *refs: ring_back_kernel(heads, size, *refs),
        grid=(COPIES,),
        in_specs=[
            SCALARS,
            SCALARS,
            fixed(order.shape),
            fixed(masks.shape),
            pl.BlockSpec((1, length, width), lambda i: (jnp.maximum(i - 2, 0), 0, 0)),
            pl.BlockSpec((1, length, width), lambda i: (jnp.minimum(i, 1), 0, 0)),
            pl.BlockSpec(
                (1, 1, length, width), lambda i: (lax.rem(i, 2), jnp.where(i < 2, 1, 0), 0, 0)
            ),
        ]
        + [fixed((length, width))] * (2 * COPIES)
        + [
            fixed(vec.shape),
            fixed(w_own.shape),
            by_block(9 * LANES),
            by_block(LANES),
            by_block(2 * LANES),
            by_block(2 * LANES),
            pl.BlockSpec((1, 1, length), lambda i: (slot(i), 0, 0)),
            by_block(1),
        ]
        + [ANYWHERE] * len(pieces),
        out_specs=[
            by_block(part),
            by_block(3 * part),
            fixed((2, length, width)),
            fixed((2, length, width)),
            fixed((length, width)),
            fixed((8, width)),
        ],
        out_shape=[
            like((tokens, part), BF16),
            like((tokens, 3 * part), BF16),
            like((2, length, width), BF16),
            like((2, length, width), BF16),
            far((length, width), F32),
            like((8, width), F32),
        ],
        scratch_shapes=[
            pltpu.VMEM((width, 8 * LANES), BF16),
            pltpu.VMEM((length, width), F32),
            pltpu.VMEM((tokens, 8 * LANES), BF16),
            pltpu.SemaphoreType.DMA((2, len(pieces))),
        ],
        compiler_params=params(),
        cost_estimate=cost(200),
    )(
        me, place, *kept_far([order, masks]), total, near, *kept_far([middle, *grad, *x]), vec,
        *kept_far([w_own, qkv, lse, cosine, sine]), seg_rows, seg_cols, *kept_far(pieces),
    )


def last_grad_kernel(me_ref, normed_ref, mixed_ref, grad_ref, cols_ref, sums_ref, feed_ref, out_ref, line_ref):
    i = pl.program_id(0)
    width = normed_ref.shape[1]
    rows = width * pl.num_programs(0) // 8
    parts, part = grad_ref.shape[1], cols_ref.shape[1]
    left = outer(normed_ref[...], grad_ref[...]).astype(BF16)
    right = outer(mixed_ref[...], cols_ref[...]).astype(BF16)
    value = jnp.concatenate([left, right], 1)
    for n in range(width // 32):
        at = i * width + 32 * n
        shard = lax.div(at, rows)
        row = pl.multiple_of(at - shard * rows, 32)
        out_ref[shard, pl.ds(row, 32)] = value[32 * n : 32 * n + 32]

    @pl.when(i == 0)
    def _():
        line_ref[...] = jnp.zeros_like(line_ref)
        for shard in range(8):
            here = slice(shard * rows, (shard + 1) * rows)
            for n in range(5):
                line_ref[shard, n : n + 1, :rows] = sums_ref[n : n + 1, here]
            line_ref[shard, 5:6, :rows] = feed_ref[1:2, here]
        for me in range(COPIES):

            @pl.when(me_ref[0] == me)
            def _():
                for shard in range(8):
                    line_ref[shard, 7:8, me * rows : (me + 1) * rows] = feed_ref[
                        0:1, shard * rows : (shard + 1) * rows
                    ]
                for n in range(3):
                    start = (n * COPIES + me) * part
                    for shard in range(8):
                        low = max(start, shard * 3 * rows)
                        high = min(start + part, (shard + 1) * 3 * rows)
                        if low < high:
                            line_ref[shard, 6:7, low - shard * 3 * rows : high - shard * 3 * rows] = (
                                sums_ref[5:6, n * part + low - start : n * part + high - start]
                            )

        for shard in range(8):
            out_ref[shard, rows:] = line_ref[shard].astype(BF16)


def last_grads(me, normed, mixed, grad, cols, sums, feed_sums):
    tokens, width = normed.shape
    block = 256
    rows = width // 8
    by_columns = pl.BlockSpec((tokens, block), lambda i: (0, i))
    shape = (8, rows + EXTRA, grad.shape[1] + cols.shape[1])
    return pl.pallas_call(
        last_grad_kernel,
        grid=(width // block,),
        in_specs=[
            SCALARS,
            by_columns,
            by_columns,
            fixed(grad.shape),
            fixed(cols.shape),
            fixed(sums.shape),
            fixed(feed_sums.shape),
        ],
        out_specs=fixed(shape),
        out_shape=like(shape, BF16),
        scratch_shapes=[pltpu.VMEM((8, EXTRA, shape[2]), F32)],
        compiler_params=params(),
        cost_estimate=cost(10),
    )(me, *kept_far([normed, mixed]), grad, cols, sums, feed_sums)


def output_kernel(middle_ref, pair_ref, far_ref, vec_ref, out_ref):
    out_ref[...] = (
        middle_ref[0, 0] + pair_ref[0].astype(F32) + far_ref[...].astype(F32) + vec_ref[5:6]
    ).astype(BF16)


def output_of(middle, pair, far, vec):
    length, width = far.shape
    return pl.pallas_call(
        output_kernel,
        grid=(1,),
        in_specs=[
            fixed((1, 1, length, width)),
            fixed(pair.shape),
            fixed(far.shape),
            fixed(vec.shape),
        ],
        out_specs=fixed(far.shape),
        out_shape=like(far.shape, BF16),
        compiler_params=params(),
        cost_estimate=cost(),
    )(middle, pair, far, vec)


def last_norm_kernel(dx_ref, pair_ref, far_ref, x_ref, vec_ref, out_ref):
    grad_normed = pair_ref[0].astype(F32) + far_ref[...].astype(F32)
    unit, inverse = norm_parts(x_ref[...].astype(F32))
    out_ref[...] = (
        dx_ref[...] + norm_back(grad_normed, unit, inverse, vec_ref[0:1])
    ).astype(BF16)


def last_norm(dx, pair, far, x, vec):
    return pl.pallas_call(
        last_norm_kernel,
        in_specs=[WHOLE] * 5,
        out_specs=WHOLE,
        out_shape=like(x.shape, BF16),
        compiler_params=params(),
        cost_estimate=cost(),
    )(dx, pair, far, x, vec)


def spread_kernel(me_ref, s0, s1, s2, s3, whole_up_ref, whole_down_ref):
    slots = (s0, s1, s2, s3)
    rows = whole_up_ref.shape[0]
    step = s0.shape[0] - rows
    size = s0.shape[1] // 8
    for me in range(COPIES):

        @pl.when(me_ref[0] == me)
        def _():
            for n in range(COPIES):
                whole_down_ref[n * step : (n + 1) * step] = slots[me ^ n][rows:].astype(F32)
            for group in range(8):
                at = group * size * COPIES
                whole_up_ref[:, at : at + size * COPIES] = jnp.concatenate(
                    [
                        slots[me ^ n][:rows, group * size : (group + 1) * size]
                        for n in range(COPIES)
                    ],
                    1,
                ).astype(F32)


def spread(me, slots, rows):
    lines, width = slots[0].shape
    return pl.pallas_call(
        spread_kernel,
        in_specs=[SCALARS] + [WHOLE] * COPIES,
        out_specs=[WHOLE] * 2,
        out_shape=[
            like((rows, COPIES * width), F32),
            like((COPIES * (lines - rows), width), F32),
        ],
        compiler_params=params(),
        cost_estimate=cost(),
    )(me, *slots)


def finish_kernel(part, me_ref, s0, s1, s2, s3, whole_qkv_ref, whole_out_ref, *sum_refs):
    slots = (s0, s1, s2, s3)
    rows = whole_qkv_ref.shape[0]
    for me in range(COPIES):

        @pl.when(me_ref[0] == me)
        def _():
            for n in range(3):
                whole_qkv_ref[:, n * COPIES * part : (n + 1) * COPIES * part] = jnp.concatenate(
                    [slots[me ^ m][:rows, n * part : (n + 1) * part] for m in range(COPIES)], 1
                ).astype(F32)
            whole_out_ref[...] = jnp.concatenate(
                [slots[me ^ m][:rows, 3 * part :] for m in range(COPIES)], 1
            ).astype(F32)
            sums = sum(slots[me ^ m][rows:].astype(F32) for m in range(COPIES))
            for n, ref in enumerate(sum_refs):
                ref[...] = sums[n, : ref.shape[0]]


def finish(me, slots, part, vectors):
    lines, width = slots[0].shape
    rows = lines - EXTRA
    return pl.pallas_call(
        lambda *refs: finish_kernel(part, *refs),
        in_specs=[SCALARS] + [WHOLE] * COPIES,
        out_specs=[WHOLE] * (2 + len(vectors)),
        out_shape=[like((rows, 3 * COPIES * part), F32), like((rows, COPIES * part), F32)]
        + [like(shape, F32) for shape in vectors],
        compiler_params=params(),
        cost_estimate=cost(),
    )(me, *slots)


def slot_pairs(kept, sent):
    return (kept.astype(F32) + to_core(sent).astype(F32)).astype(BF16)


def on_eight(
    hidden_in,
    seg_ids,
    patch_rows,
    patch_cols,
    ln1_scale,
    ln1_shift,
    qkv_weight,
    qkv_bias,
    out_weight,
    out_bias,
    ln2_scale,
    ln2_shift,
    up_weight,
    up_bias,
    down_weight,
    down_bias,
    cotangent,
):
    me = lax.axis_index("rep")
    me_list = me.reshape(1).astype(jnp.int32)
    length, width = hidden_in.shape
    rows = ln1_scale.shape[0]
    size = width // HEADS
    heads = HEADS // COPIES
    part = heads * size
    hidden = up_weight.shape[1] // COPIES
    slots = ring_slots()
    vectors = (
        ln1_scale, ln1_shift, out_bias, ln2_scale, ln2_shift, down_bias, qkv_bias, up_bias,
    )

    order, masks = column_order(heads, size), head_masks(heads, size)
    ids = gather_rep(jnp.concatenate([seg_ids, patch_rows, patch_cols]))
    x = gather_rep(hidden_in)
    grad = gather_rep(cotangent)
    own_feed = second_piece(me_list, up_weight, down_weight, 8)
    seg_ids, patches = jnp.stack([v[0] for v in ids]), jnp.stack(ids)
    seg_rows, seg_cols = seg_ids[:, None], seg_ids.reshape(-1, 1)
    cosine, sine = rotary_tiles(patches[:, 1].reshape(-1), patches[:, 2].reshape(-1), heads, size)
    qkv_pieces = ring_gather(
        first_piece(me_list, order, qkv_weight, out_weight, vectors, part),
        (),
        {1: x + [cosine, sine, seg_rows, seg_cols], 2: [own_feed] + grad},
    )
    out_pieces = gather_rep(collect(qkv_pieces, rows, part))
    feed_weights = ring_gather(own_feed, qkv_pieces[7:])

    normed_one, qkv, lse, mixed, vec = ring_attend(
        me_list, slots, order, masks, x, cosine, sine, seg_rows, seg_cols, qkv_pieces, heads, size
    )
    mixed_all, middle, normed_two, w_own = middle_of(
        me_list, slots, gather_rep(mixed), vec, x, out_pieces, rows
    )
    act, low, sent, kept, feed_sums = feed(
        slots, normed_two, grad, vec, feed_weights, hidden
    )

    arrived = to_core(sent)
    act, low, normed_two, arrived = tie((act, low, normed_two, arrived))
    pair = (kept.astype(F32) + arrived.astype(F32)).astype(BF16)
    total = (pair.astype(F32) + to_x(pair)[::-1].astype(F32)).astype(BF16)
    near = to_core(total)

    tokens = COPIES * length
    feed_grad = feed_grads(
        normed_two.reshape(tokens, width), act.reshape(tokens, hidden), low.reshape(tokens, hidden), grad
    )
    feed_grad = lax.psum_scatter(
        feed_grad.reshape(-1, width), "shard", scatter_dimension=0, tiled=True
    )

    sent, kept = down_of(slots, act, feed_weights, width)
    out_pair = slot_pairs(kept, sent)
    total, near, out_pair = tie((total, near, out_pair))

    cols, grad_qkv, sent_one, kept_one, grad_middle, sums = ring_back(
        me_list, slots, order, masks, total, near, middle, grad, x, vec, w_own, qkv, lse, cosine, sine,
        seg_rows, seg_cols, qkv_pieces, heads, size,
    )
    out_far = to_x(out_pair[1])
    grad_qkv, out_far = tie((grad_qkv, out_far))
    output = output_of(middle, out_pair, out_far, vec)

    pair = slot_pairs(kept_one, sent_one)
    far = to_x(pair[1])
    last = last_grads(me_list, normed_one, mixed_all, grad_qkv, cols, sums, feed_sums)
    last, feed_grad = ring_scatter(last, slots, {0: [pair], 1: [far]}, feed_grad)
    whole_up, whole_down = spread(me_list, gather_rep(feed_grad), rows)
    whole_qkv, whole_out, *totals = finish(
        me_list, gather_rep(last), part, [vector.shape for vector in vectors]
    )
    grad_inputs = last_norm(grad_middle, pair, far, hidden_in, vec)
    return (
        output,
        grad_inputs,
        totals[0],
        totals[1],
        whole_qkv,
        totals[6],
        whole_out,
        totals[2],
        totals[3],
        totals[4],
        whole_up,
        totals[7],
        whole_down,
        totals[5],
    )


def solution(mesh):
    shards = mesh.shape["shard"]
    tokens, vector, matrix = P(("rep", "shard"), None), P("shard"), P("shard", None)
    in_specs = (
        (tokens,) * 4
        + (vector, vector, matrix, vector, matrix, vector)
        + (vector, vector, matrix, vector, matrix, vector)
        + (tokens,)
    )
    out_specs = (
        (tokens, tokens)
        + (vector, vector, matrix, vector, matrix, vector)
        + (vector, vector, matrix, vector, matrix, vector)
    )
    return jax.shard_map(
        on_eight if shards == 8 else lambda *args: on_any(shards, *args),
        mesh=mesh,
        in_specs=in_specs,
        out_specs=out_specs,
        check_vma=False,
    )
```

```python
import jax
import jax.numpy as jnp
import numpy as np
from jax import lax
from jax.experimental import pallas as pl
from jax.experimental.pallas import tpu as pltpu
from jax.sharding import PartitionSpec as P

HEADS = 16
EPSILON = 1e-06
GELU_SLOPE = 1.702
LANES = 128
MASKED = -1e30
COPIES = 4
EXTRA = 16
GRID = 32

CORE_PAIRS = [(0, 1), (1, 0), (2, 3), (3, 2)]
X_PAIRS = [(0, 2), (2, 0), (1, 3), (3, 1)]
RING = (0, 2, 4, 6, 7, 5, 3, 1)
RING_AT = tuple(RING.index(i) for i in range(8))
RIGHT = [(RING[i], RING[(i + 1) % 8]) for i in range(8)]
LEFT = [(RING[i], RING[(i - 1) % 8]) for i in range(8)]
OFFSETS = (0, -1, 1, -2, 2, -3, 3, 4, 4)

F32 = jnp.float32
BF16 = jnp.bfloat16
VMEM_LIMIT = 32 * 1024 * 1024


def norm_parts(values):
    center = values - jnp.mean(values, -1, keepdims=True)
    inverse = lax.rsqrt(jnp.mean(center * center, -1, keepdims=True) + EPSILON)
    return (center * inverse, inverse)


def norm_back(grad_normed, unit, inverse, scale):
    scaled = grad_normed * scale
    return inverse * (
        scaled
        - jnp.mean(scaled, -1, keepdims=True)
        - unit * jnp.mean(scaled * unit, -1, keepdims=True)
    )


def outer(left, right):
    return lax.dot_general(left, right, (((0,), (0,)), ((), ())), preferred_element_type=F32)


def times_transposed(left, right):
    return lax.dot_general(left, right, (((1,), (1,)), ((), ())), preferred_element_type=F32)


def times(left, right):
    return jnp.dot(left, right, preferred_element_type=F32)


def tie(values, after=()):
    values, after = tuple(values), tuple(after)
    return lax.optimization_barrier(values + after)[: len(values)]


def to_core(value):
    return lax.ppermute(value, "rep", CORE_PAIRS)


def to_x(value):
    return lax.ppermute(value, "rep", X_PAIRS)


def gather_rep(value):
    near, far = to_core(value), to_x(value)
    return [value, near, far, to_core(far)]


def reduce_pair(parts):
    low = parts.astype(BF16)
    arrived = to_core(jnp.stack([low[1], low[3]]))
    return (jnp.stack([low[0], low[2]]).astype(F32) + arrived.astype(F32)).astype(BF16)


def scatter_rep(parts):
    pair = reduce_pair(parts)
    return pair[0].astype(F32) + to_x(pair[1]).astype(F32)


def sum_rep(parts):
    pair = reduce_pair(parts)
    arrived = to_x(pair)
    total = (pair.astype(F32) + arrived[::-1].astype(F32)).astype(BF16)
    near = to_core(total)
    return jnp.stack([total[0], near[0], total[1], near[1]])


def by_owner(slots, me):
    core, far = me % 2 == 1, me // 2 == 1
    a, b, c, d = slots
    a, b, c, d = (
        jnp.where(core, b, a),
        jnp.where(core, a, b),
        jnp.where(core, d, c),
        jnp.where(core, c, d),
    )
    return [jnp.where(far, c, a), jnp.where(far, d, b), jnp.where(far, a, c), jnp.where(far, b, d)]


def gather_shards(pieces, shards):
    return [lax.all_gather(piece, "shard", axis=0) for piece in pieces]


def scatter_shards(whole, shards, rights):
    return lax.psum_scatter(whole, "shard", scatter_dimension=0, tiled=False)


def window(values, start, size):
    part = values[:, start : start + size]
    return jnp.concatenate([part, jnp.zeros((part.shape[0], LANES - size), part.dtype)], 1)


def turned(values, half, lane):
    return jnp.where(
        lane < half,
        pltpu.roll(values, LANES - half, 1),
        pltpu.roll(values, half, 1),
    )


def attend_kernel(
    heads, size, x_ref, gain_ref, shift_ref, w_ref, bias_ref, cos_ref, sin_ref, row_ref, col_ref,
    normed_ref, qkv_ref, lse_ref, out_ref,
):
    unit, _ = norm_parts(x_ref[...].astype(F32))
    normed = (unit * gain_ref[...] + shift_ref[...]).astype(BF16)
    normed_ref[...] = normed
    projected = times(normed, w_ref[...]) + bias_ref[...]
    cosine, sine = cos_ref[...], sin_ref[...]
    rows = projected.shape[0]
    lane = lax.broadcasted_iota(jnp.int32, (rows, LANES), 1)
    same = col_ref[...] == row_ref[0]
    scale = size**-0.5
    half = size // 2
    outs = []
    lses = jnp.zeros((rows, LANES), F32)
    for head in range(heads):
        query, key, value = (
            window(projected, (part * heads + head) * size, size) for part in range(3)
        )
        query = (query * cosine + turned(query, half, lane) * sine).astype(BF16)
        key = (key * cosine + turned(key, half, lane) * sine).astype(BF16)
        value = value.astype(BF16)
        for part, kept in enumerate((query, key, value)):
            at = (part * heads + head) * LANES
            qkv_ref[:, at : at + LANES] = kept
        scores = jnp.where(same, times_transposed(query, key) * scale, MASKED)
        most = jnp.max(scores, -1, keepdims=True)
        expo = jnp.exp(scores - most)
        total = jnp.sum(expo, -1, keepdims=True)
        probs = (expo * (1.0 / total)).astype(BF16)
        outs.append(times(probs, value)[:, :size])
        lses = jnp.where(lane == head, most + jnp.log(total), lses)
    lse_ref[...] = lses
    out_ref[...] = jnp.concatenate(outs, 1).astype(BF16)


def attend(x, gain, shift, weight, bias, cosine, sine, seg_rows, seg_cols, heads, size):
    tokens, width = x.shape
    length = seg_rows.shape[-1]
    part = heads * size
    by_block = lambda columns: pl.BlockSpec((length, columns), lambda i: (i, 0))
    fixed = lambda array: pl.BlockSpec(array.shape, lambda i: (0,) * array.ndim)
    return pl.pallas_call(
        lambda *refs: attend_kernel(heads, size, *refs),
        grid=(tokens // length,),
        in_specs=[
            by_block(width),
            fixed(gain),
            fixed(shift),
            fixed(weight),
            fixed(bias),
            by_block(LANES),
            by_block(LANES),
            pl.BlockSpec((1, 1, length), lambda i: (i, 0, 0)),
            by_block(1),
        ],
        out_specs=[by_block(width), by_block(3 * heads * LANES), by_block(LANES), by_block(part)],
        out_shape=[
            jax.ShapeDtypeStruct((tokens, width), BF16),
            jax.ShapeDtypeStruct((tokens, 3 * heads * LANES), BF16),
            jax.ShapeDtypeStruct((tokens, LANES), F32),
            jax.ShapeDtypeStruct((tokens, part), BF16),
        ],
        compiler_params=pltpu.CompilerParams(vmem_limit_bytes=48 * 1024 * 1024),
        cost_estimate=pl.CostEstimate(
            flops=2 * tokens * width * 3 * part + 4 * tokens * length * part,
            bytes_accessed=4 * tokens * width + weight.size * 2 + tokens * 3 * heads * LANES * 2,
            transcendentals=tokens * length * heads,
        ),
    )(x, gain, shift, weight, bias, cosine, sine, seg_rows, seg_cols)


def attend_back_kernel(
    heads, size, db_ref, wo_ref, qkv_ref, lse_ref, cos_ref, sin_ref, row_ref, col_ref, w_ref,
    x_ref, grad_ref, dn_ref, sum_ref, gain_ref, shift_ref,
):
    mixed = times_transposed(db_ref[...], wo_ref[...])
    cosine, sine = cos_ref[...], sin_ref[...]
    rows = mixed.shape[0]
    lane = lax.broadcasted_iota(jnp.int32, (rows, LANES), 1)
    same = col_ref[...] == row_ref[0]
    scale = size**-0.5
    half = size // 2
    lses = lse_ref[...]
    grads = [None] * (3 * heads)
    for head in range(heads):
        query, key, value = (
            qkv_ref[:, (part * heads + head) * LANES : (part * heads + head + 1) * LANES]
            for part in range(3)
        )
        lse = jnp.sum(jnp.where(lane == head, lses, 0.0), -1, keepdims=True)
        scores = jnp.where(same, times_transposed(query, key) * scale, MASKED)
        probs = jnp.exp(scores - lse)
        grad_mixed = window(mixed, head * size, size).astype(BF16)
        grad_probs = times_transposed(grad_mixed, value)
        grad_value = outer(probs.astype(BF16), grad_mixed)
        inner = jnp.sum(probs * grad_probs, -1, keepdims=True)
        low = (probs * (grad_probs - inner)).astype(BF16)
        grad_query = times(low, key) * scale
        grad_key = outer(low, query) * scale
        grad_query = grad_query * cosine + turned(grad_query * sine, half, lane)
        grad_key = grad_key * cosine + turned(grad_key * sine, half, lane)
        grads[head] = grad_query[:, :size]
        grads[heads + head] = grad_key[:, :size]
        grads[2 * heads + head] = grad_value[:, :size]
    grad = jnp.concatenate(grads, 1).astype(BF16)
    grad_ref[...] = grad
    grad_normed = times_transposed(grad, w_ref[...])
    dn_ref[...] = grad_normed.astype(BF16)
    unit, _ = norm_parts(x_ref[...].astype(F32))

    @pl.when(pl.program_id(0) == 0)
    def _():
        sum_ref[...] = jnp.zeros_like(sum_ref)
        gain_ref[...] = jnp.zeros_like(gain_ref)
        shift_ref[...] = jnp.zeros_like(shift_ref)

    sum_ref[...] += jnp.sum(grad.astype(F32), 0, keepdims=True)
    gain_ref[...] += jnp.sum(grad_normed * unit, 0, keepdims=True)
    shift_ref[...] += jnp.sum(grad_normed, 0, keepdims=True)


def attend_back(db, w_out, qkv, lse, cosine, sine, seg_rows, seg_cols, weight, x, heads, size):
    tokens, width = x.shape
    length = seg_rows.shape[-1]
    part = heads * size
    by_block = lambda columns: pl.BlockSpec((length, columns), lambda i: (i, 0))
    fixed = lambda shape: pl.BlockSpec(shape, lambda i: (0,) * len(shape))
    return pl.pallas_call(
        lambda *refs: attend_back_kernel(heads, size, *refs),
        grid=(tokens // length,),
        in_specs=[
            by_block(width),
            fixed(w_out.shape),
            by_block(3 * heads * LANES),
            by_block(LANES),
            by_block(LANES),
            by_block(LANES),
            pl.BlockSpec((1, 1, length), lambda i: (i, 0, 0)),
            by_block(1),
            fixed(weight.shape),
            by_block(width),
        ],
        out_specs=[
            by_block(3 * part),
            by_block(width),
            fixed((1, 3 * part)),
            fixed((1, width)),
            fixed((1, width)),
        ],
        out_shape=[
            jax.ShapeDtypeStruct((tokens, 3 * part), BF16),
            jax.ShapeDtypeStruct((tokens, width), BF16),
            jax.ShapeDtypeStruct((1, 3 * part), F32),
            jax.ShapeDtypeStruct((1, width), F32),
            jax.ShapeDtypeStruct((1, width), F32),
        ],
        compiler_params=pltpu.CompilerParams(vmem_limit_bytes=48 * 1024 * 1024),
        cost_estimate=pl.CostEstimate(
            flops=2 * tokens * width * 4 * part + 10 * tokens * length * part,
            bytes_accessed=6 * tokens * width + weight.size * 2 + tokens * 3 * heads * LANES * 2,
            transcendentals=tokens * length * heads,
        ),
    )(db, w_out, qkv, lse, cosine, sine, seg_rows, seg_cols, weight, x)


def rotary(rows, columns, size):
    quarter = size // 4
    inverse = 10000.0 ** (-4.0 * jnp.arange(quarter, dtype=F32) / size)
    angles = jnp.concatenate(
        [rows.astype(F32)[:, None] * inverse, columns.astype(F32)[:, None] * inverse], -1
    )
    cosine, sine = jnp.cos(angles), jnp.sin(angles)
    nothing = jnp.zeros((rows.shape[0], LANES - size), F32)
    return (
        jnp.concatenate([cosine, cosine, nothing], -1),
        jnp.concatenate([-sine, sine, nothing], -1),
    )


def on_any(
    shards,
    hidden_in,
    seg_ids,
    patch_rows,
    patch_cols,
    ln1_scale,
    ln1_shift,
    qkv_weight,
    qkv_bias,
    out_weight,
    out_bias,
    ln2_scale,
    ln2_shift,
    up_weight,
    up_bias,
    down_weight,
    down_bias,
    cotangent,
):
    copies = 4
    me = lax.axis_index("rep")
    length, width = hidden_in.shape
    rows = ln1_scale.shape[0]
    size = width // HEADS
    heads = HEADS // copies
    part = heads * size
    hidden = up_weight.shape[1]
    own_hidden = hidden // copies
    step = hidden // shards // copies

    def own(array, axis):
        return lax.dynamic_index_in_dim(array, me, axis, False)

    own_qkv = own(qkv_weight.reshape(rows, 3, copies, part), 2).reshape(rows, 3 * part)
    own_up = own(up_weight.reshape(rows, shards, copies, step), 2).reshape(rows, own_hidden)
    own_down = own(down_weight.reshape(copies, step, width), 0)
    own_out = own(out_weight.reshape(copies, rows // copies, width), 0)
    vectors = (
        ln1_scale, ln1_shift, out_bias, ln2_scale, ln2_shift, down_bias, qkv_bias, up_bias,
    )
    small = jnp.concatenate(vectors)
    small_rows = 8
    small = jnp.pad(small, (0, small_rows * 3 * part - small.size)).reshape(small_rows, 3 * part)
    first, up_full, out_all, down_full = gather_shards(
        [
            jnp.concatenate([own_qkv, small]),
            own_up,
            own_out,
            own_down,
        ],
        shards,
    )
    w_qkv = first[:, :rows].reshape(width, 3 * part)
    small = first[:, rows:].reshape(shards, -1)
    up_full = up_full.reshape(width, own_hidden)
    down_full = down_full.reshape(own_hidden, width)
    full = []
    at = 0
    for vector in vectors:
        full.append(small[:, at : at + vector.size].astype(F32))
        at += vector.size
    gain_one, shift_one, out_offset, gain_two, shift_two, down_offset = (
        v.reshape(1, width) for v in full[:6]
    )
    qkv_offset = own(full[6].reshape(3, copies, part), 1).reshape(1, 3 * part)
    up_offset = own(full[7].reshape(shards, copies, step), 1).reshape(1, own_hidden)

    ids = jnp.concatenate([seg_ids, patch_rows, patch_cols])
    ids = jnp.stack(gather_rep(ids))
    seg_rows, seg_cols = ids[:, :1], ids[:, 0].reshape(-1, 1)
    x_low = jnp.concatenate(gather_rep(hidden_in))
    grad_out = jnp.concatenate(gather_rep(cotangent))
    tokens = x_low.shape[0]
    cosine, sine = rotary(ids[:, 1].reshape(-1), ids[:, 2].reshape(-1), size)

    normed_one, qkv, lse, mixed = attend(
        x_low, gain_one, shift_one, w_qkv, qkv_offset, cosine, sine, seg_rows, seg_cols, heads, size
    )
    out_full = jnp.stack(by_owner(gather_rep(out_all), me), 1).reshape(width, width)
    blocks = mixed.reshape(copies, length, part)
    near, far = to_core(blocks), to_x(blocks)
    both = to_core(far)
    mixed_slots = [
        mixed,
        near[jnp.array([1, 0, 3, 2])].reshape(tokens, part),
        far[jnp.array([2, 3, 0, 1])].reshape(tokens, part),
        both[jnp.array([3, 2, 1, 0])].reshape(tokens, part),
    ]
    mixed_full = jnp.concatenate(by_owner(mixed_slots, me), 1)

    middle = x_low.astype(F32) + times(mixed_full, out_full) + out_offset
    unit_two, inverse_two = norm_parts(middle)
    normed_two = (unit_two * gain_two + shift_two).astype(BF16)
    upward = times(normed_two, up_full) + up_offset
    sigma = jax.nn.sigmoid(GELU_SLOPE * upward)
    activated = (upward * sigma).astype(BF16)
    slope = sigma + GELU_SLOPE * upward * sigma * (1.0 - sigma)

    grad_down = outer(activated, grad_out).astype(BF16)
    grad_up_low = (times_transposed(grad_out, down_full) * slope).astype(BF16)
    grad_normed_two = sum_rep(times_transposed(grad_up_low, up_full).reshape(copies, length, width))
    grad_up = outer(normed_two, grad_up_low).astype(BF16)
    grad_up_bias = jnp.sum(grad_up_low.astype(F32), 0)
    branch = scatter_rep(times(activated, down_full).reshape(copies, length, width))
    output = middle[:length] + branch + down_offset

    grad_normed_two = grad_normed_two.reshape(tokens, width).astype(F32)
    grad_middle = grad_out.astype(F32) + norm_back(
        grad_normed_two, unit_two, inverse_two, gain_two
    )
    grad_branch = grad_middle.astype(BF16)
    grad_out_w = outer(mixed_full, own(grad_branch.reshape(tokens, copies, part), 1)).astype(BF16)

    own_w_out = lax.dynamic_slice_in_dim(out_full, me * part, part, 0)
    grad_qkv_low, grad_normed_one, sum_qkv, sum_gain, sum_shift = attend_back(
        grad_branch, own_w_out, qkv, lse, cosine, sine, seg_rows, seg_cols, w_qkv, x_low, heads, size
    )
    grad_qkv = outer(normed_one, grad_qkv_low).astype(BF16)
    grad_normed_one = scatter_rep(grad_normed_one.reshape(copies, length, width))
    unit_one, inverse_one = norm_parts(hidden_in.astype(F32))
    grad_inputs = grad_middle[:length] + norm_back(grad_normed_one, unit_one, inverse_one, gain_one)

    def sum_of(values):
        return jnp.sum(values[:length], 0).reshape(shards, rows)

    def placed(values, like, axis):
        return lax.dynamic_update_index_in_dim(jnp.zeros(like, F32), values, me, axis)

    sums = [
        sum_gain.reshape(shards, rows),
        sum_shift.reshape(shards, rows),
        sum_of(grad_branch.astype(F32)),
        sum_of(grad_normed_two * unit_two),
        sum_of(grad_normed_two),
        sum_of(grad_out.astype(F32)),
        placed(sum_qkv.reshape(3, part), (3, copies, part), 1).reshape(shards, -1),
        placed(grad_up_bias.reshape(shards, step), (shards, copies, step), 1).reshape(shards, -1),
    ]
    sums = jnp.concatenate(sums, 1)
    sums = jnp.pad(sums, ((0, 0), (0, small_rows * 3 * part - sums.shape[1])))
    last = jnp.concatenate(
        [grad_qkv.reshape(shards, rows, 3 * part), sums.astype(BF16).reshape(shards, small_rows, -1)],
        1,
    )

    done_down = scatter_shards(grad_down.reshape(shards, step, width), shards, 4)
    done_up = scatter_shards(grad_up.reshape(shards, rows, own_hidden), shards, 3)
    done_out = scatter_shards(grad_out_w.reshape(shards, rows, part), shards, 4)
    done_last = scatter_shards(last, shards, 4)

    whole_down = jnp.concatenate(by_owner(gather_rep(done_down), me), 0).astype(F32)
    whole_up = jnp.stack(
        [p.reshape(rows, shards, step) for p in by_owner(gather_rep(done_up), me)], 2
    )
    whole_up = whole_up.reshape(rows, hidden).astype(F32)
    whole_out = jnp.concatenate(by_owner(gather_rep(done_out), me), 1).astype(F32)
    last_slots = gather_rep(done_last)
    whole_qkv = jnp.stack(
        [p[:rows].reshape(rows, 3, part) for p in by_owner(last_slots, me)], 2
    )
    whole_qkv = whole_qkv.reshape(rows, 3 * width).astype(F32)
    summed = sum(p[rows:].astype(F32) for p in by_owner(last_slots, me)).reshape(-1)
    totals = []
    at = 0
    for vector in vectors:
        totals.append(summed[at : at + vector.size])
        at += vector.size
    return (
        output.astype(BF16),
        grad_inputs.astype(BF16),
        totals[0],
        totals[1],
        whole_qkv,
        totals[6],
        whole_out,
        totals[2],
        totals[3],
        totals[4],
        whole_up,
        totals[7],
        whole_down,
        totals[5],
    )


def ring_slots():
    position = jnp.asarray(RING_AT, jnp.int32)[lax.axis_index("shard")]
    return jnp.asarray(RING, jnp.int32)[(position + jnp.asarray(OFFSETS, jnp.int32)) % 8]


def half_of(rows):
    return (rows // 2 + 15) // 16 * 16


def ring_gather(piece, after=(), others=None):
    right = left = piece
    if after:
        right, left = tie((piece, piece), after)
    pieces = [piece]
    for hop in range(4):
        if hop == 3:
            cut = half_of(piece.shape[0])
            right, left = right[:cut], left[cut:]
        right, left = tie(
            (lax.ppermute(right, "shard", RIGHT), lax.ppermute(left, "shard", LEFT)),
            (others or {}).get(hop, ()),
        )
        pieces += [right, left]
    return pieces


def hop_kernel(first, _, ahead_ref, behind_ref, right_ref, left_ref, to_right_ref, to_left_ref):
    i = pl.program_id(0)

    def plus(out_ref, own_ref, other_ref):
        out_ref[...] = (own_ref[0].astype(F32) + other_ref[...].astype(F32)).astype(BF16)

    def copy(out_ref, own_ref):
        out_ref[...] = own_ref[0]

    if not first:
        plus(to_right_ref, ahead_ref, right_ref)
        plus(to_left_ref, behind_ref, left_ref)
        return

    @pl.when(i < pl.num_programs(0) // 2)
    def _():
        plus(to_right_ref, ahead_ref, right_ref)
        copy(to_left_ref, behind_ref)

    @pl.when(i >= pl.num_programs(0) // 2)
    def _():
        copy(to_right_ref, ahead_ref)
        plus(to_left_ref, behind_ref, left_ref)


def hop_sums(whole, slots, right, left, hop, steps):
    _, rows, width = whole.shape
    tile = rows // steps
    half = steps // 2
    first = hop == 0
    term = lambda n: pl.BlockSpec((1, tile, width), lambda i, s: (s[n], i, 0))
    block = lambda at: pl.BlockSpec((tile, width), lambda i, s: (at(i), 0))
    same = lambda i: i
    return pl.pallas_call(
        lambda *refs: hop_kernel(first, *refs),
        grid_spec=pltpu.PrefetchScalarGridSpec(
            num_scalar_prefetch=1,
            grid=(steps,),
            in_specs=[
                term(6 - 2 * hop),
                term(5 - 2 * hop),
                block((lambda i: jnp.minimum(i, half - 1)) if first else same),
                block((lambda i: jnp.maximum(i - half, 0)) if first else same),
            ],
            out_specs=[block(same), block(same)],
        ),
        out_shape=[like((rows, width), BF16)] * 2,
        compiler_params=params(),
        cost_estimate=cost(),
    )(slots, whole, whole, right, left)


def ring_scatter(whole, right, left, slots, others=None, after=(), steps=0):
    cut = right.shape[0]

    def own(number):
        return lax.dynamic_slice(
            whole, (slots[number], 0, 0), (1,) + whole.shape[1:], allow_negative_indices=False
        )[0]

    def add_low(one, other):
        return (one.astype(F32) + other.astype(F32)).astype(BF16)

    if after:
        right, left = tie((right, left), after)
    for hop in range(4):
        right, left = tie(
            (lax.ppermute(right, "shard", RIGHT), lax.ppermute(left, "shard", LEFT)),
            (others or {}).get(hop, ()),
        )
        if hop == 3:
            break
        if steps:
            right, left = hop_sums(whole, slots, right, left, hop, steps)
            continue
        ahead, behind = own(6 - 2 * hop), own(5 - 2 * hop)
        if hop == 0:
            right = jnp.concatenate([add_low(right, ahead[:cut]), ahead[cut:]])
            left = jnp.concatenate([behind[:cut], add_low(left, behind[cut:])])
        else:
            right, left = add_low(right, ahead), add_low(left, behind)
    return (right.astype(F32) + left.astype(F32) + own(0).astype(F32)).astype(BF16)


def run_copies(copies):
    for copy in copies:
        copy.start()
    for copy in copies:
        copy.wait()


ANYWHERE = pl.BlockSpec(memory_space=pl.ANY)
SCALARS = pl.BlockSpec(memory_space=pltpu.SMEM)
WHOLE = pl.BlockSpec(memory_space=pltpu.VMEM)


def params():
    return pltpu.CompilerParams(vmem_limit_bytes=VMEM_LIMIT)


def fixed(shape):
    return pl.BlockSpec(shape, lambda i: (0,) * len(shape))


def cost(microseconds=0):
    return pl.CostEstimate(flops=1, bytes_accessed=1 + microseconds * 3_690_000, transcendentals=0)


def like(shape, dtype):
    return jax.ShapeDtypeStruct(shape, dtype)


def far(shape, dtype):
    return pltpu.HBM(shape, dtype)


def kept_far(arrays):
    return [pltpu.with_memory_space_constraint(a, pltpu.HBM) for a in arrays]


def joined(slots):
    return jnp.concatenate(slots, 0)


def column_order(heads, size):
    half = size // 2
    left = heads * half - LANES
    order = np.zeros((2 * heads * size, 2 * heads * size), np.float32)
    for part in range(2):
        for head in range(heads):
            for side in range(2):
                for feature in range(half):
                    natural = (part * heads + head) * size + side * half + feature
                    at = head * half + feature
                    group = 2 * part + side
                    to = group * LANES + at if at < LANES else (4 * LANES + group * left + at - LANES)
                    order[natural, to] = 1.0
    return jnp.asarray(order, BF16)


def head_masks(heads, size):
    half = size // 2
    left = heads * half - LANES
    masks = np.zeros((2 * heads, 3 * LANES), np.float32)
    for head in range(heads):
        for lane in range(2 * LANES):
            masks[head, lane] = (lane % LANES) // half == head
        for lane in range(2 * left):
            masks[head, 2 * LANES + lane] = (LANES + lane % left) // half == head
        masks[heads + head, head * size : (head + 1) * size] = 1.0
    return jnp.asarray(masks, F32)


def rotary_table(heads, size):
    half, quarter = size // 2, size // 4
    left = heads * half - LANES
    at = np.concatenate([np.arange(LANES), LANES + np.arange(4 * left) % left]) % half
    inverse = (10000.0 ** (-4.0 * np.arange(quarter, dtype=np.float32) / size)).astype(np.float32)
    angles = np.arange(GRID, dtype=np.float32)[:, None] * inverse[at % quarter]
    sign = np.ones(2 * LANES, np.float32)
    for group in (0, 2):
        sign[LANES + group * left : LANES + (group + 1) * left] = -1.0
    both = np.concatenate([np.cos(angles), np.sin(angles) * sign], 1)
    by_row = np.concatenate([at < quarter, at < quarter])
    return jnp.asarray(np.concatenate([np.where(by_row, both, 0.0), np.where(by_row, 0.0, both)]), F32)


def positions(ids, table):
    grid = lax.broadcasted_iota(jnp.int32, (GRID, ids.shape[1]), 0)
    picks = jnp.concatenate([grid == ids[1:2], grid == ids[2:3]], 0).astype(F32)
    both = lax.dot_general(
        picks, table, (((0,), (0,)), ((), ())), precision=lax.Precision.HIGHEST,
        preferred_element_type=F32,
    )
    image = (grid[:8] == ids[0:1]).astype(F32)
    return tiles(both, 4), outer(image, image) > 0.5


def first_kernel(part, *refs):
    me_ref, order_ref, weight_ref, other_ref = refs[:4]
    vectors, out_ref = refs[4:12], refs[12]
    rows, width = out_ref.shape[0] - EXTRA, out_ref.shape[1]
    for me in range(COPIES):

        @pl.when(me_ref[0] == me)
        def _():
            parts = [
                weight_ref[:, (n * COPIES + me) * part : (n * COPIES + me + 1) * part]
                for n in range(3)
            ]
            turned = times(jnp.concatenate(parts[:2], 1), order_ref[...]).astype(BF16)
            out_ref[:rows] = jnp.concatenate(
                [turned, parts[2], other_ref[:, me * part : (me + 1) * part]], 1
            )

    lines = [v[...].astype(F32).reshape(1, -1) for v in vectors]
    lines = [jnp.concatenate(lines[:6], 1), lines[6], lines[7]]
    lines = [
        jnp.concatenate([line, jnp.zeros((1, width - line.shape[1]), F32)], 1) for line in lines
    ]
    lines.append(jnp.zeros((EXTRA - len(lines), width), F32))
    out_ref[rows:] = jnp.concatenate(lines, 0).astype(BF16)


def first_piece(me, order, weight, other, vectors, part):
    rows = weight.shape[0]
    return pl.pallas_call(
        lambda *refs: first_kernel(part, *refs),
        in_specs=[SCALARS] + [WHOLE] * 11,
        out_specs=WHOLE,
        out_shape=like((rows + EXTRA, COPIES * part), BF16),
        compiler_params=params(),
        cost_estimate=cost(),
    )(me, *kept_far([order, weight, other, *vectors]))


def collect_kernel(rows, *refs):
    pieces, (out_ref, lines_ref, semaphores) = refs[:9], refs[9:]
    lanes = lines_ref.shape[2]
    part = out_ref.shape[1] // COPIES
    copies = []
    for number, ref in enumerate(pieces):
        edge = half_of(rows + EXTRA)
        start, count = (edge, rows - edge) if number == 8 else (0, edge if number == 7 else rows)
        copies.append(
            pltpu.make_async_copy(
                ref.at[pl.ds(0, count), pl.ds(ref.shape[1] - lanes, lanes)],
                lines_ref.at[min(number, 7), pl.ds(start, count)],
                semaphores.at[number],
            )
        )
    run_copies(copies)
    for line in range(2):
        out_ref[line * rows : (line + 1) * rows] = jnp.concatenate(
            [lines_ref[2 * n + line][:, lanes - part :] for n in range(COPIES)], 1
        )


def collect(pieces, rows, part):
    lanes = -(-part // LANES) * LANES
    return pl.pallas_call(
        lambda *refs: collect_kernel(rows, *refs),
        in_specs=[ANYWHERE] * len(pieces),
        out_specs=WHOLE,
        out_shape=like((2 * rows, COPIES * part), BF16),
        scratch_shapes=[pltpu.VMEM((8, rows, lanes), BF16), pltpu.SemaphoreType.DMA((9,))],
        compiler_params=params(),
        cost_estimate=cost(),
    )(*kept_far(pieces))


def second_kernel(shards, me_ref, up_ref, down_ref, out_ref):
    rows, hidden = up_ref.shape
    step = hidden // shards // COPIES
    for me in range(COPIES):

        @pl.when(me_ref[0] == me)
        def _():
            out_ref[:rows] = jnp.concatenate(
                [
                    up_ref[:, (n * COPIES + me) * step : (n * COPIES + me + 1) * step]
                    for n in range(shards)
                ],
                1,
            )
            out_ref[rows:] = down_ref[me * step : (me + 1) * step]


def second_piece(me, up, down, shards):
    rows, hidden = up.shape
    step = hidden // shards // COPIES
    return pl.pallas_call(
        lambda *refs: second_kernel(shards, *refs),
        in_specs=[SCALARS] + [WHOLE] * 2,
        out_specs=WHOLE,
        out_shape=like((rows + step, hidden // COPIES), BF16),
        compiler_params=params(),
        cost_estimate=cost(),
    )(me, *kept_far([up, down]))


def first_copies(refs, place, rows, w_ref, small_ref, semaphores):
    cut = half_of(rows + EXTRA)
    copies = []
    for number, ref in enumerate(refs):
        slot = place[number]
        start, count = (cut, rows - cut) if number == 8 else (0, cut if number == 7 else rows)
        at = pl.multiple_of(slot * rows + start, 16)
        copies.append(
            pltpu.make_async_copy(
                ref.at[pl.ds(0, count), pl.ds(0, w_ref.shape[1])],
                w_ref.at[pl.ds(at, count)],
                semaphores.at[0, number],
            )
        )
        if number != 7 and small_ref is not None:
            copies.append(
                pltpu.make_async_copy(
                    ref.at[pl.ds(count, EXTRA)], small_ref.at[slot], semaphores.at[1, number]
                )
            )
    return copies


def vectors_of(me_ref, small_ref, order_ref, vec_ref, bias_ref, full_ref):
    shards = small_ref.shape[0]
    width = vec_ref.shape[1]
    rows = width // shards
    part = width // COPIES
    lines = [small_ref[s].astype(F32) for s in range(shards)]
    for n in range(6):
        vec_ref[n : n + 1] = jnp.concatenate(
            [line[0:1, n * rows : (n + 1) * rows] for line in lines], 1
        )
    full_ref[...] = jnp.concatenate([line[1:2, : 3 * rows] for line in lines], 1)
    vec_ref[7:8] = jnp.zeros((1, width), F32)
    bias_ref[...] = jnp.zeros_like(bias_ref)
    for me in range(COPIES):

        @pl.when(me_ref[0] == me)
        def _():
            vec_ref[6:7] = jnp.concatenate(
                [line[2:3, me * rows : (me + 1) * rows] for line in lines], 1
            )
            parts = [
                full_ref[:, (n * COPIES + me) * part : (n * COPIES + me + 1) * part] for n in range(3)
            ]
            both = jnp.broadcast_to(jnp.concatenate(parts[:2], 1), (8, 2 * part)).astype(BF16)
            bias_ref[:, : 2 * part] = times(both, order_ref[...])[:1]
            bias_ref[:, 2 * part : 3 * part] = parts[2]


def swapped(values, lane, left):
    return jnp.where(
        lane // left % 2 == 0,
        pltpu.roll(values, LANES - left, 1),
        pltpu.roll(values, left, 1),
    )


def tiles(values, count):
    return [values[:, n * LANES : (n + 1) * LANES] for n in range(count)]


def ring_attend_kernel(heads, size, *refs):
    (
        me_ref, place_ref, order_ref, mask_ref, table_ref, x0, x1, x2, x3, ids_ref,
    ), refs = refs[:10], refs[10:]
    pieces, refs = refs[:9], refs[9:]
    (
        normed_ref, qkv_ref, lse_ref, out_ref, vec_ref, w_ref, small_ref, bias_ref, full_ref, all_ref,
        project_ref, semaphores,
    ) = refs
    i = pl.program_id(0)
    length, width = x0.shape
    rows = width // 8
    part = heads * size

    @pl.when(i == 0)
    def _():
        copies = first_copies(pieces, place_ref, rows, w_ref, small_ref, semaphores)
        for copy in copies:
            copy.start()
        for copy in copies[1:14:2] + copies[-1:]:
            copy.wait()
        vectors_of(me_ref, small_ref, order_ref, vec_ref, bias_ref, full_ref)
        for slot, x_ref in enumerate((x0, x1, x2, x3)):
            unit, _ = norm_parts(x_ref[...].astype(F32))
            all_ref[slot * length : (slot + 1) * length] = (
                unit * vec_ref[0:1] + vec_ref[1:2]
            ).astype(BF16)
        for copy in copies[0:14:2] + copies[14:16]:
            copy.wait()
        project_ref[...] = times(all_ref[...], w_ref[...]) + bias_ref[...]

    here = pl.ds(pl.multiple_of(i * length, 16), length)
    normed_ref[...] = all_ref[here, :]
    q1, q2, k1, k2, rest = tiles(project_ref[here, : 5 * LANES], 5)
    value = project_ref[here, 5 * LANES :]
    lane = lax.broadcasted_iota(jnp.int32, (length, LANES), 1)
    wide = lax.broadcasted_iota(jnp.int32, (length, 3 * LANES), 1)
    (cosine, cosine_rest, sine, sine_rest), same = positions(ids_ref[0], table_ref[...])
    left = heads * size // 2 - LANES
    rest = rest * cosine_rest + swapped(rest, lane, left) * sine_rest
    query = jnp.concatenate(
        [q1 * cosine - q2 * sine, q2 * cosine + q1 * sine, jnp.where(lane < 2 * left, rest, 0.0)], 1
    ).astype(BF16)
    key = jnp.concatenate(
        [
            k1 * cosine - k2 * sine,
            k2 * cosine + k1 * sine,
            jnp.where(lane < 2 * left, pltpu.roll(rest, 2 * left, 1), 0.0),
        ],
        1,
    ).astype(BF16)
    value = jnp.where(wide < part, value, 0.0).astype(BF16)
    qkv_ref[...] = jnp.concatenate([query, key, value], 1)
    masks = mask_ref[...].astype(BF16)
    scale = size**-0.5
    all_probs, all_values = [], []
    lses = jnp.zeros((length, LANES), F32)
    for head in range(heads):
        scores = times_transposed(query * masks[head : head + 1], key)
        scores = jnp.where(same, scores * scale, MASKED)
        most = jnp.max(scores, -1, keepdims=True)
        expo = jnp.exp(scores - most)
        total = jnp.sum(expo, -1, keepdims=True)
        all_probs.append((expo * (1.0 / total)).astype(BF16))
        all_values.append(value * masks[heads + head : heads + head + 1])
        lses = jnp.where(lane == head, most + jnp.log(total), lses)
    lse_ref[...] = lses
    out = times(jnp.concatenate(all_probs, 1), joined(all_values))[:, :part].astype(BF16)
    count = out_ref.shape[1]
    out_ref[0] = jnp.concatenate([out[n * count : (n + 1) * count] for n in range(COPIES)], 1)


def ring_attend(me, place, order, masks, table, x, ids, pieces, heads, size):
    length, width = x[0].shape
    tokens = COPIES * length
    by_block = lambda columns: pl.BlockSpec((length, columns), lambda i: (i, 0))
    return pl.pallas_call(
        lambda *refs: ring_attend_kernel(heads, size, *refs),
        grid=(COPIES,),
        in_specs=[SCALARS, SCALARS, fixed(order.shape), fixed(masks.shape), fixed(table.shape)]
        + [fixed((length, width))] * COPIES
        + [pl.BlockSpec((1,) + ids.shape[1:], lambda i: (i, 0, 0))]
        + [ANYWHERE] * len(pieces),
        out_specs=[
            by_block(width),
            by_block(9 * LANES),
            by_block(LANES),
            pl.BlockSpec((1, length // COPIES, width), lambda i: (i, 0, 0)),
            fixed((8, width)),
        ],
        out_shape=[
            far((tokens, width), BF16),
            far((tokens, 9 * LANES), BF16),
            far((tokens, LANES), F32),
            like((COPIES, length // COPIES, width), BF16),
            like((8, width), F32),
        ],
        scratch_shapes=[
            pltpu.VMEM((width, 8 * LANES), BF16),
            pltpu.VMEM((8, EXTRA, width), BF16),
            pltpu.VMEM((1, 8 * LANES), F32),
            pltpu.VMEM((1, 3 * width), F32),
            pltpu.VMEM((tokens, width), BF16),
            pltpu.VMEM((tokens, 8 * LANES), F32),
            pltpu.SemaphoreType.DMA((2, len(pieces))),
        ],
        compiler_params=params(),
        cost_estimate=cost(25),
    )(
        me, place, *kept_far([order, masks, table, *x]), ids, *kept_far(pieces)
    )


def middle_kernel(rows, part, *refs):
    me_ref, place_ref, own_ref, near_ref, far_ref, both_ref, vec_ref, x0, x1, x2, x3 = refs[:11]
    weights, (all_ref, middle_ref, normed_ref, wown_ref, w_ref, x_ref) = (
        refs[11:15],
        refs[15:],
    )
    j = pl.program_id(0)

    @pl.when(j == 0)
    def _():
        me = me_ref[0]
        for own in range(COPIES):

            @pl.when(me == own)
            def _():
                for n in range(8):
                    here = slice(n % 2 * rows, (n % 2 + 1) * rows)
                    lanes = slice(n // 2 * part, (n // 2 + 1) * part)
                    at = pl.multiple_of(place_ref[n] * rows, 16)
                    w_ref[pl.ds(at, rows), :] = jnp.concatenate(
                        [weights[own ^ b][here, lanes] for b in range(COPIES)], 1
                    )

        wown_ref[...] = w_ref[pl.ds(pl.multiple_of(me * part, 16), part), :]
        x_ref[...] = joined([x0[...], x1[...]])

    @pl.when(j == 1)
    def _():
        x_ref[...] = joined([x2[...], x3[...]])

    def unpacked(ref, order):
        return joined(
            [ref[b, :, n * part : (n + 1) * part] for b in order for n in range(COPIES)]
        )

    slots = [
        unpacked(own_ref, (0, 1)),
        unpacked(near_ref, (1, 0)),
        unpacked(far_ref, (0, 1)),
        unpacked(both_ref, (1, 0)),
    ]
    for me in range(COPIES):

        @pl.when(me_ref[0] == me)
        def _():
            all_ref[...] = jnp.concatenate([slots[me ^ n] for n in range(COPIES)], 1)

    middle = x_ref[...].astype(F32) + times(all_ref[...], w_ref[...]) + vec_ref[2:3]
    unit, _ = norm_parts(middle)
    normed = (unit * vec_ref[3:4] + vec_ref[4:5]).astype(BF16)
    length = middle_ref.shape[2]
    for core in range(2):
        middle_ref[0, core] = middle[core * length : (core + 1) * length]
        normed_ref[0, core] = normed[core * length : (core + 1) * length]


def middle_of(me, place, mixed, vec, x, weights, rows):
    length, width = x[0].shape
    part = width // COPIES
    tokens = COPIES * length
    by_slots = lambda flip: pl.BlockSpec(
        (2,) + mixed[0].shape[1:], lambda j: ((1 - j) if flip else j, 0, 0)
    )
    by_half = pl.BlockSpec((1, 2, length, width), lambda j: (j, 0, 0, 0))
    return pl.pallas_call(
        lambda *refs: middle_kernel(rows, part, *refs),
        grid=(2,),
        in_specs=[SCALARS, SCALARS]
        + [by_slots(False), by_slots(False), by_slots(True), by_slots(True), fixed(vec.shape)]
        + [fixed((length, width))] * COPIES
        + [fixed(weights[0].shape)] * COPIES,
        out_specs=[
            pl.BlockSpec((2 * length, width), lambda j: (j, 0)),
            by_half,
            by_half,
            fixed((part, width)),
        ],
        out_shape=[
            far((tokens, width), BF16),
            far((2, 2, length, width), F32),
            far((2, 2, length, width), BF16),
            far((part, width), BF16),
        ],
        scratch_shapes=[
            pltpu.VMEM((width, width), BF16),
            pltpu.VMEM((2 * length, width), BF16),
        ],
        compiler_params=params(),
        cost_estimate=cost(13),
    )(me, place, *mixed, vec, *kept_far([*x, *weights]))


def split_copies(pieces, place, up_ref, down_ref, semaphores):
    copies = []
    for number, ref in enumerate(pieces):
        for line, target in enumerate((up_ref, down_ref)):
            if target is None or (number == 7 and line == 1) or (number == 8 and line == 0):
                continue
            count = target.shape[0] // 8
            copies.append(
                pltpu.make_async_copy(
                    ref.at[pl.ds(count if line == 1 and number < 7 else 0, count)],
                    target.at[pl.ds(pl.multiple_of(place[number] * count, 16), count)],
                    semaphores.at[line, number],
                )
            )
    return copies


def feed_kernel(place_ref, normed_ref, g0, g1, g2, g3, vec_ref, *refs):
    pieces, refs = refs[:9], refs[9:]
    act_ref, dh_ref, sent_ref, kept_ref, sum_ref, up_ref, down_ref, grad_ref, semaphores = refs
    j = pl.program_id(0)

    @pl.when(j == 0)
    def _():
        copies = split_copies(pieces, place_ref, up_ref, None, semaphores)
        later = split_copies(pieces, place_ref, None, down_ref, semaphores)
        for copy in copies + later:
            copy.start()
        for copy in copies:
            copy.wait()
        sum_ref[...] = jnp.zeros_like(sum_ref)
        sum_ref[1:2] = jnp.sum(g0[...].astype(F32), 0, keepdims=True)
        grad_ref[...] = joined([g1[...], g3[...]])

    @pl.when(j == 1)
    def _():
        grad_ref[...] = joined([g0[...], g2[...]])

    normed = joined([normed_ref[0, 0], normed_ref[1, 0]])
    upward = times(normed, up_ref[...]) + vec_ref[6:7]
    sigma = jax.nn.sigmoid(GELU_SLOPE * upward)
    act = (upward * sigma).astype(BF16)
    slope = sigma + GELU_SLOPE * upward * sigma * (1.0 - sigma)

    @pl.when(j == 0)
    def _():
        for copy in split_copies(pieces, place_ref, None, down_ref, semaphores):
            copy.wait()

    low = (times_transposed(grad_ref[...], down_ref[...]) * slope).astype(BF16)
    sum_ref[0:1] += jnp.sum(low.astype(F32), 0, keepdims=True)
    back = times_transposed(low, up_ref[...]).astype(BF16)
    length = normed_ref.shape[2]
    for half in range(2):
        here = slice(half * length, (half + 1) * length)
        act_ref[half, 0] = act[here]
        dh_ref[half, 0] = low[here]

    @pl.when(j == 0)
    def _():
        for half in range(2):
            sent_ref[half] = back[half * length : (half + 1) * length]

    @pl.when(j == 1)
    def _():
        for half in range(2):
            kept_ref[half] = back[half * length : (half + 1) * length]


def feed(place, normed, grad, vec, pieces, hidden):
    _, _, length, width = normed.shape
    by_core = lambda columns: pl.BlockSpec((2, 1, length, columns), lambda j: (0, 1 - j, 0, 0))
    pair = like((2, length, width), BF16)
    return pl.pallas_call(
        feed_kernel,
        grid=(2,),
        in_specs=[SCALARS, by_core(width)]
        + [fixed((length, width))] * COPIES
        + [fixed(vec.shape)]
        + [ANYWHERE] * len(pieces),
        out_specs=[
            by_core(hidden),
            by_core(hidden),
            fixed((2, length, width)),
            fixed((2, length, width)),
            fixed((8, hidden)),
        ],
        out_shape=[
            far((2, 2, length, hidden), BF16),
            far((2, 2, length, hidden), BF16),
            pair,
            pair,
            like((8, hidden), F32),
        ],
        scratch_shapes=[
            pltpu.VMEM((width, hidden), BF16),
            pltpu.VMEM((hidden, width), BF16),
            pltpu.VMEM((2 * length, width), BF16),
            pltpu.SemaphoreType.DMA((2, 9)),
        ],
        compiler_params=params(),
        cost_estimate=cost(20),
    )(place, *kept_far([normed, *grad]), vec, *kept_far(pieces))


def down_kernel(place_ref, act_ref, *refs):
    pieces, (sent_ref, kept_ref, down_ref, semaphores) = refs[:9], refs[9:]
    j = pl.program_id(0)

    @pl.when(j == 0)
    def _():
        run_copies(split_copies(pieces, place_ref, None, down_ref, semaphores))

    value = times(joined([act_ref[0, 0], act_ref[1, 0]]), down_ref[...]).astype(BF16)
    length = act_ref.shape[2]

    @pl.when(j == 0)
    def _():
        for half in range(2):
            sent_ref[half] = value[half * length : (half + 1) * length]

    @pl.when(j == 1)
    def _():
        for half in range(2):
            kept_ref[half] = value[half * length : (half + 1) * length]


def down_of(place, act, pieces, width):
    _, _, length, hidden = act.shape
    pair = like((2, length, width), BF16)
    return pl.pallas_call(
        down_kernel,
        grid=(2,),
        in_specs=[SCALARS, pl.BlockSpec((2, 1, length, hidden), lambda j: (0, 1 - j, 0, 0))]
        + [ANYWHERE] * len(pieces),
        out_specs=[fixed((2, length, width)), fixed((2, length, width))],
        out_shape=[pair, pair],
        scratch_shapes=[pltpu.VMEM((hidden, width), BF16), pltpu.SemaphoreType.DMA((2, 9))],
        compiler_params=params(),
        cost_estimate=cost(),
    )(place, *kept_far([act, *pieces]))


def feed_grad_kernel(place_ref, normed_ref, act_ref, dh_ref, g0, g1, g2, g3, out_ref, top_ref, bottom_ref):
    i = pl.program_id(0)
    half = pl.num_programs(0) // 2
    width = normed_ref.shape[1]
    rows = width * half // 8

    def put(value, start):
        first = lax.rem(i, half) * width
        for n in range(width // 32):
            at = first + 32 * n
            shard = lax.div(at, rows)
            row = pl.multiple_of(at - shard * rows + start, 32)
            out_ref[shard, pl.ds(row, 32)] = value[32 * n : 32 * n + 32]

    @pl.when(i < half)
    def _():
        put(outer(normed_ref[...], dh_ref[...]).astype(BF16), 0)

    @pl.when(i >= half)
    def _():
        grad = joined([g0[...], g1[...], g2[...], g3[...]])
        put(outer(act_ref[...], grad).astype(BF16), rows)

    @pl.when(i == pl.num_programs(0) - 1)
    def _():
        top_ref[...] = out_ref[place_ref[7], :rows]
        bottom_ref[...] = out_ref[place_ref[7], rows:]


def feed_grads(place, normed, act, dh, grad):
    tokens, width = normed.shape
    length = grad[0].shape[0]
    block = 256
    half = width // block
    return pl.pallas_call(
        feed_grad_kernel,
        grid=(2 * half,),
        in_specs=[
            SCALARS,
            pl.BlockSpec((tokens, block), lambda i: (0, jnp.minimum(i, half - 1))),
            pl.BlockSpec((tokens, block), lambda i: (0, jnp.maximum(i - half, 0))),
            fixed(dh.shape),
        ]
        + [fixed((length, width))] * COPIES,
        out_specs=[
            fixed((8, width // 4, width)),
            fixed((width // 8, width)),
            fixed((width // 8, width)),
        ],
        out_shape=[
            far((8, width // 4, width), BF16),
            like((width // 8, width), BF16),
            like((width // 8, width), BF16),
        ],
        compiler_params=params(),
        cost_estimate=cost(),
    )(place, *kept_far([normed, act, dh, *grad]))


def ring_back_kernel(heads, size, first, *refs):
    (
        me_ref, place_ref, order_ref, mask_ref, table_ref, total_ref, middle_ref, g0, g1, x0, x1, vec_ref,
        wo_ref, qkv_ref, lse_ref, ids_ref,
    ), refs = refs[:16], refs[16:]
    pieces, refs = refs[:9], refs[9:]
    dx_ref = refs[0] if first else None
    cols_ref, grad_ref, share_ref, sums_ref, w_ref, cot_ref, all_ref, semaphores = refs[first:]
    i = pl.program_id(0)
    length, width = x0.shape
    rows = width // 8
    part = heads * size

    @pl.when(i == 0)
    def _():
        for copy in first_copies(pieces, place_ref, rows, w_ref, None, semaphores):
            copy.start()
        sums_ref[...] = jnp.zeros_like(sums_ref)

    for n, grad_ref_in in enumerate((g0, g1)):

        @pl.when(i == n)
        def _():
            cot_ref[...] = grad_ref_in[...].astype(F32)

    grad_normed = total_ref[0].astype(F32)
    unit, inverse = norm_parts(middle_ref[0, 0])
    grad_middle = cot_ref[...] + norm_back(grad_normed, unit, inverse, vec_ref[3:4])
    branch = grad_middle.astype(BF16)

    if first:

        @pl.when(i == 0)
        def _():
            dx_ref[...] = grad_middle
            sums_ref[2:3] = jnp.sum(branch.astype(F32), 0, keepdims=True)
            sums_ref[3:4] = jnp.sum(grad_normed * unit, 0, keepdims=True)
            sums_ref[4:5] = jnp.sum(grad_normed, 0, keepdims=True)

    for me in range(COPIES):

        @pl.when(me_ref[0] == me)
        def _():
            cols_ref[0] = branch[:, me * part : (me + 1) * part]

    mixed = times_transposed(branch, wo_ref[...]).astype(BF16)
    mixed = jnp.concatenate([mixed, jnp.zeros((length, 3 * LANES - part), BF16)], 1)
    query, key, value = (qkv_ref[:, 3 * n * LANES : 3 * (n + 1) * LANES] for n in range(3))
    masks = mask_ref[...].astype(BF16)
    (cosine, cosine_rest, sine, sine_rest), same = positions(ids_ref[0], table_ref[...])
    scale = size**-0.5
    lses = lse_ref[...]
    all_probs, all_lows, queries, keys, mixes = [], [], [], [], []
    for head in range(heads):
        queries.append(query * masks[head : head + 1])
        keys.append(key * masks[head : head + 1])
        mixes.append(mixed * masks[heads + head : heads + head + 1])
        scores = jnp.where(same, times_transposed(queries[-1], key) * scale, MASKED)
        probs = jnp.exp(scores - lses[:, head : head + 1])
        grad_probs = times_transposed(mixes[-1], value)
        inner = jnp.sum(probs * grad_probs, -1, keepdims=True)
        all_probs.append(probs.astype(BF16))
        all_lows.append((probs * (grad_probs - inner)).astype(BF16))
    grad_query = times(jnp.concatenate(all_lows, 1), joined(keys)) * scale
    grad_key = outer(joined(all_lows), joined(queries)) * scale
    grad_value = outer(joined(all_probs), joined(mixes)).astype(BF16)
    lane = lax.broadcasted_iota(jnp.int32, (length, LANES), 1)
    left = heads * size // 2 - LANES
    q1, q2, q_rest = tiles(grad_query, 3)
    k1, k2, k_rest = tiles(grad_key, 3)
    rest = jnp.where(lane < 2 * left, q_rest, pltpu.roll(k_rest, 2 * left, 1))
    rest = rest * cosine_rest + swapped(rest * sine_rest, lane, left)
    grad = jnp.concatenate(
        [
            q1 * cosine + q2 * sine,
            q2 * cosine - q1 * sine,
            k1 * cosine + k2 * sine,
            k2 * cosine - k1 * sine,
            rest,
        ],
        1,
    ).astype(BF16)
    here = pl.ds(pl.multiple_of(i * length, 16), length)
    all_ref[here, :] = jnp.concatenate([grad, grad_value], 1)
    natural = times_transposed(grad, order_ref[...])
    grad_ref[0, :, : 2 * part] = natural.astype(BF16)
    grad_ref[0, :, 2 * part :] = grad_value[:, :part]
    sums_ref[5:6, : 2 * part] += jnp.sum(natural, 0, keepdims=True)
    sums_ref[5:6, 2 * part : 3 * part] += jnp.sum(grad_value[:, :part].astype(F32), 0, keepdims=True)

    @pl.when(i == 1)
    def _():
        for copy in first_copies(pieces, place_ref, rows, w_ref, None, semaphores):
            copy.wait()
        share = times_transposed(all_ref[...], w_ref[...])
        for n, x_ref in enumerate((x0, x1)):
            here = share[n * length : (n + 1) * length]
            unit, _ = norm_parts(x_ref[...].astype(F32))
            sums_ref[0:1] += jnp.sum(here * unit, 0, keepdims=True)
            sums_ref[1:2] += jnp.sum(here, 0, keepdims=True)
            share_ref[n] = here.astype(BF16)


def ring_back(
    me, place, order, masks, table, total, middle, grad, x, vec, w_own, qkv, lse, ids, pieces, heads, size,
    first,
):
    length, width = x[0].shape
    part = heads * size
    core = 0 if first else 1
    by_block = lambda columns: pl.BlockSpec((length, columns), lambda i: (2 * i + core, 0))
    by_half = lambda columns: pl.BlockSpec((1, length, columns), lambda i: (i, 0, 0))
    return pl.pallas_call(
        lambda *refs: ring_back_kernel(heads, size, first, *refs),
        grid=(2,),
        in_specs=[
            SCALARS,
            SCALARS,
            fixed(order.shape),
            fixed(masks.shape),
            fixed(table.shape),
            by_half(width),
            pl.BlockSpec((1, 1, length, width), lambda i: (i, core, 0, 0)),
        ]
        + [fixed((length, width))] * 4
        + [
            fixed(vec.shape),
            fixed(w_own.shape),
            by_block(9 * LANES),
            by_block(LANES),
            pl.BlockSpec((1,) + ids.shape[1:], lambda i: (2 * i + core, 0, 0)),
        ]
        + [ANYWHERE] * len(pieces),
        out_specs=[fixed((length, width))] * first
        + [by_half(part), by_half(3 * part), fixed((2, length, width)), fixed((8, width))],
        out_shape=[far((length, width), F32)] * first
        + [
            far((2, length, part), BF16),
            far((2, length, 3 * part), BF16),
            like((2, length, width), BF16),
            like((8, width), F32),
        ],
        scratch_shapes=[
            pltpu.VMEM((width, 8 * LANES), BF16),
            pltpu.VMEM((length, width), F32),
            pltpu.VMEM((2 * length, 8 * LANES), BF16),
            pltpu.SemaphoreType.DMA((2, len(pieces))),
        ],
        compiler_params=params(),
        cost_estimate=cost(13),
    )(
        me, place, *kept_far([order, masks, table]), total,
        *kept_far([middle, grad[core], grad[2 + core], x[core], x[2 + core]]), vec,
        *kept_far([w_own, qkv, lse]), ids, *kept_far(pieces),
    )


def last_grad_kernel(
    me_ref, place_ref, normed_ref, mixed_ref, grad0_ref, grad1_ref, cols0_ref, cols1_ref, sums0_ref, sums1_ref,
    feed_ref, out_ref, top_ref, bottom_ref, line_ref, grad_ref, cols_ref, sums_ref,
):
    i = pl.program_id(0)
    width = normed_ref.shape[1]
    rows = width * pl.num_programs(0) // 8
    part = cols_ref.shape[1]

    @pl.when(i == 0)
    def _():
        length = grad0_ref.shape[1]
        for n in range(2):
            for core, grad_in, cols_in in ((0, grad0_ref, cols0_ref), (1, grad1_ref, cols1_ref)):
                here = slice((2 * n + core) * length, (2 * n + core + 1) * length)
                grad_ref[here] = grad_in[n]
                cols_ref[here] = cols_in[n]
        sums_ref[...] = sums0_ref[...] + sums1_ref[...]

    left = outer(normed_ref[...], grad_ref[...]).astype(BF16)
    right = outer(mixed_ref[...], cols_ref[...]).astype(BF16)
    value = jnp.concatenate([left, right], 1)
    for n in range(width // 32):
        at = i * width + 32 * n
        shard = lax.div(at, rows)
        row = pl.multiple_of(at - shard * rows, 32)
        out_ref[shard, pl.ds(row, 32)] = value[32 * n : 32 * n + 32]

    @pl.when(i == 0)
    def _():
        line_ref[...] = jnp.zeros_like(line_ref)
        for shard in range(8):
            here = slice(shard * rows, (shard + 1) * rows)
            for n in range(5):
                line_ref[shard, n : n + 1, :rows] = sums_ref[n : n + 1, here]
            line_ref[shard, 5:6, :rows] = feed_ref[1:2, here]
        for me in range(COPIES):

            @pl.when(me_ref[0] == me)
            def _():
                for shard in range(8):
                    line_ref[shard, 7:8, me * rows : (me + 1) * rows] = feed_ref[
                        0:1, shard * rows : (shard + 1) * rows
                    ]
                for n in range(3):
                    start = (n * COPIES + me) * part
                    for shard in range(8):
                        low = max(start, shard * 3 * rows)
                        high = min(start + part, (shard + 1) * 3 * rows)
                        if low < high:
                            line_ref[shard, 6:7, low - shard * 3 * rows : high - shard * 3 * rows] = (
                                sums_ref[5:6, n * part + low - start : n * part + high - start]
                            )

        for shard in range(8):
            out_ref[shard, rows:] = line_ref[shard].astype(BF16)

    @pl.when(i == pl.num_programs(0) - 1)
    def _():
        cut = top_ref.shape[0]
        top_ref[...] = out_ref[place_ref[7], :cut]
        bottom_ref[...] = out_ref[place_ref[7], cut:]


def last_grads(me, place, normed, mixed, grads, cols, sums, feed_sums):
    tokens, width = normed.shape
    block = 256
    rows = width // 8
    by_columns = pl.BlockSpec((tokens, block), lambda i: (0, i))
    parts, part = grads[0].shape[2], cols[0].shape[2]
    shape = (8, rows + EXTRA, parts + part)
    cut = half_of(shape[1])
    return pl.pallas_call(
        last_grad_kernel,
        grid=(width // block,),
        in_specs=[
            SCALARS,
            SCALARS,
            by_columns,
            by_columns,
            *[fixed(a.shape) for a in (*grads, *cols, *sums, feed_sums)],
        ],
        out_specs=[fixed(shape), fixed((cut, shape[2])), fixed((shape[1] - cut, shape[2]))],
        out_shape=[
            like(shape, BF16),
            like((cut, shape[2]), BF16),
            like((shape[1] - cut, shape[2]), BF16),
        ],
        scratch_shapes=[
            pltpu.VMEM((8, EXTRA, shape[2]), F32),
            pltpu.VMEM((tokens, parts), BF16),
            pltpu.VMEM((tokens, part), BF16),
            pltpu.VMEM(sums[0].shape, F32),
        ],
        compiler_params=params(),
        cost_estimate=cost(10),
    )(me, place, *kept_far([normed, mixed, *grads, *cols]), *sums, feed_sums)


def output_kernel(middle_ref, pair_ref, far_ref, vec_ref, out_ref):
    out_ref[...] = (
        middle_ref[0, 0] + pair_ref[0].astype(F32) + far_ref[...].astype(F32) + vec_ref[5:6]
    ).astype(BF16)


def output_of(middle, pair, far, vec):
    length, width = far.shape
    return pl.pallas_call(
        output_kernel,
        grid=(1,),
        in_specs=[
            fixed((1, 1, length, width)),
            fixed(pair.shape),
            fixed(far.shape),
            fixed(vec.shape),
        ],
        out_specs=fixed(far.shape),
        out_shape=like(far.shape, BF16),
        compiler_params=params(),
        cost_estimate=cost(),
    )(middle, pair, far, vec)


def last_norm_kernel(dx_ref, pair_ref, far_ref, x_ref, vec_ref, out_ref):
    grad_normed = pair_ref[0].astype(F32) + far_ref[...].astype(F32)
    unit, inverse = norm_parts(x_ref[...].astype(F32))
    out_ref[...] = (
        dx_ref[...] + norm_back(grad_normed, unit, inverse, vec_ref[0:1])
    ).astype(BF16)


def last_norm(dx, pair, far, x, vec):
    return pl.pallas_call(
        last_norm_kernel,
        in_specs=[WHOLE] * 5,
        out_specs=WHOLE,
        out_shape=like(x.shape, BF16),
        compiler_params=params(),
        cost_estimate=cost(),
    )(dx, pair, far, x, vec)


def spread_kernel(me_ref, s0, s1, s2, s3, whole_up_ref, whole_down_ref):
    slots = (s0, s1, s2, s3)
    rows = whole_up_ref.shape[0]
    step = s0.shape[0] - rows
    size = s0.shape[1] // 8
    for me in range(COPIES):

        @pl.when(me_ref[0] == me)
        def _():
            for n in range(COPIES):
                whole_down_ref[n * step : (n + 1) * step] = slots[me ^ n][rows:].astype(F32)
            for group in range(8):
                at = group * size * COPIES
                whole_up_ref[:, at : at + size * COPIES] = jnp.concatenate(
                    [
                        slots[me ^ n][:rows, group * size : (group + 1) * size]
                        for n in range(COPIES)
                    ],
                    1,
                ).astype(F32)


def spread(me, slots, rows):
    lines, width = slots[0].shape
    return pl.pallas_call(
        spread_kernel,
        in_specs=[SCALARS] + [WHOLE] * COPIES,
        out_specs=[WHOLE] * 2,
        out_shape=[
            like((rows, COPIES * width), F32),
            like((COPIES * (lines - rows), width), F32),
        ],
        compiler_params=params(),
        cost_estimate=cost(),
    )(me, *slots)


def finish_kernel(part, me_ref, s0, s1, s2, s3, whole_qkv_ref, whole_out_ref, *sum_refs):
    slots = (s0, s1, s2, s3)
    rows = whole_qkv_ref.shape[0]
    for me in range(COPIES):

        @pl.when(me_ref[0] == me)
        def _():
            for n in range(3):
                whole_qkv_ref[:, n * COPIES * part : (n + 1) * COPIES * part] = jnp.concatenate(
                    [slots[me ^ m][:rows, n * part : (n + 1) * part] for m in range(COPIES)], 1
                ).astype(F32)
            whole_out_ref[...] = jnp.concatenate(
                [slots[me ^ m][:rows, 3 * part :] for m in range(COPIES)], 1
            ).astype(F32)
            sums = sum(slots[me ^ m][rows:].astype(F32) for m in range(COPIES))
            for n, ref in enumerate(sum_refs):
                ref[...] = sums[n, : ref.shape[0]]


def finish(me, slots, part, vectors):
    lines, width = slots[0].shape
    rows = lines - EXTRA
    return pl.pallas_call(
        lambda *refs: finish_kernel(part, *refs),
        in_specs=[SCALARS] + [WHOLE] * COPIES,
        out_specs=[WHOLE] * (2 + len(vectors)),
        out_shape=[like((rows, 3 * COPIES * part), F32), like((rows, COPIES * part), F32)]
        + [like(shape, F32) for shape in vectors],
        compiler_params=params(),
        cost_estimate=cost(),
    )(me, *slots)


def slot_pairs(kept, sent):
    return (kept.astype(F32) + to_core(sent).astype(F32)).astype(BF16)


def on_eight(
    hidden_in,
    seg_ids,
    patch_rows,
    patch_cols,
    ln1_scale,
    ln1_shift,
    qkv_weight,
    qkv_bias,
    out_weight,
    out_bias,
    ln2_scale,
    ln2_shift,
    up_weight,
    up_bias,
    down_weight,
    down_bias,
    cotangent,
):
    me = lax.axis_index("rep")
    me_list = me.reshape(1).astype(jnp.int32)
    length, width = hidden_in.shape
    rows = ln1_scale.shape[0]
    size = width // HEADS
    heads = HEADS // COPIES
    part = heads * size
    hidden = up_weight.shape[1] // COPIES
    slots = ring_slots()
    vectors = (
        ln1_scale, ln1_shift, out_bias, ln2_scale, ln2_shift, down_bias, qkv_bias, up_bias,
    )

    order, masks = column_order(heads, size), head_masks(heads, size)
    table = rotary_table(heads, size)
    first = first_piece(me_list, order, qkv_weight, out_weight, vectors, part)
    ids, own_x, first = tie((jnp.concatenate([seg_ids, patch_rows, patch_cols]), hidden_in, first))
    ids = gather_rep(ids)
    own_x, ids[2] = tie((own_x, ids[2]))
    x = gather_rep(own_x)
    own_feed = second_piece(me_list, up_weight, down_weight, 8)
    x[2], own_grad = tie((x[2], cotangent))
    grad = gather_rep(own_grad)
    qkv_pieces = ring_gather(
        first, (), {1: x[2:3], 2: [own_feed], 3: x[3:] + ids[3:] + grad[2:3]}
    )
    ids = jnp.stack(ids)
    out_pieces = gather_rep(collect(qkv_pieces, rows, part))

    normed_one, qkv, lse, mixed, vec = ring_attend(
        me_list, slots, order, masks, table, x, ids, qkv_pieces, heads, size
    )
    mixed_all, middle, normed_two, w_own = middle_of(
        me_list, slots, gather_rep(mixed), vec, x, out_pieces, rows
    )
    feed_weights = ring_gather(
        own_feed, qkv_pieces[7:], {0: [mixed, out_pieces[2]], 2: [normed_two]}
    )
    act, low, sent, kept, feed_sums = feed(
        slots, normed_two, grad, vec, feed_weights, hidden
    )

    arrived = to_core(sent)
    act, arrived = tie((act, arrived))
    pair = (kept.astype(F32) + arrived.astype(F32)).astype(BF16)
    far_one, far_two = to_x(pair[1]), to_x(pair[0])

    tokens = COPIES * length
    feed_grad, feed_right, feed_left = feed_grads(
        slots, normed_two.reshape(tokens, width), act.reshape(tokens, hidden), low.reshape(tokens, hidden), grad
    )
    late, feed_grad = tie((act, feed_grad))
    sent, kept = down_of(slots, late, feed_weights, width)
    far_two, sent, kept = tie((far_two, sent, kept))
    total = (pair.astype(F32) + jnp.stack([far_one, far_two]).astype(F32)).astype(BF16)
    near = to_core(total)
    out_pair = slot_pairs(kept, sent)
    out_far = to_x(out_pair[1])
    output = output_of(middle, out_pair, out_far, vec)

    def back(values, core):
        return ring_back(
            me_list, slots, order, masks, table, values, middle, grad, x, vec, w_own, qkv, lse, ids,
            qkv_pieces, heads, size, core == 0,
        )

    grad_middle, cols, grad_qkv, kept_one, sums = back(total, 0)
    near_cols, near_qkv, sent_one, near_sums = back(near, 1)
    last, last_right, last_left = last_grads(
        me_list, slots, normed_one, mixed_all, (grad_qkv, near_qkv), (cols, near_cols), (sums, near_sums), feed_sums
    )
    feed_grad = ring_scatter(
        feed_grad, feed_right, feed_left, slots, {0: [grad_qkv], 1: [near_qkv], 2: [last]},
        [far_one], 4,
    )
    feed_slots = gather_rep(feed_grad)
    whole_up, whole_down = spread(me_list, feed_slots, rows)

    arrived = to_core(sent_one)
    pair = (kept_one.astype(F32) + arrived.astype(F32)).astype(BF16)
    far_pair = to_x(pair[1])
    grad_inputs = last_norm(grad_middle, pair, far_pair, hidden_in, vec)

    last = ring_scatter(
        last,
        last_right,
        last_left,
        slots,
        {0: [pair, out_far], 1: [far_pair], 2: [feed_grad, output], 3: [feed_slots[2], grad_inputs]},
    )
    whole_qkv, whole_out, *totals = finish(
        me_list, gather_rep(last), part, [vector.shape for vector in vectors]
    )
    return (
        output,
        grad_inputs,
        totals[0],
        totals[1],
        whole_qkv,
        totals[6],
        whole_out,
        totals[2],
        totals[3],
        totals[4],
        whole_up,
        totals[7],
        whole_down,
        totals[5],
    )


def solution(mesh):
    shards = mesh.shape["shard"]
    tokens, vector, matrix = P(("rep", "shard"), None), P("shard"), P("shard", None)
    in_specs = (
        (tokens,) * 4
        + (vector, vector, matrix, vector, matrix, vector)
        + (vector, vector, matrix, vector, matrix, vector)
        + (tokens,)
    )
    out_specs = (
        (tokens, tokens)
        + (vector, vector, matrix, vector, matrix, vector)
        + (vector, vector, matrix, vector, matrix, vector)
    )
    return jax.shard_map(
        on_eight if shards == 8 else lambda *args: on_any(shards, *args),
        mesh=mesh,
        in_specs=in_specs,
        out_specs=out_specs,
        check_vma=False,
    )
```

```python
import jax
import jax.numpy as jnp
import numpy as np
from jax import lax
from jax.experimental import pallas as pl
from jax.experimental.pallas import tpu as pltpu
from jax.sharding import PartitionSpec as P

HEADS = 16
EPSILON = 1e-06
GELU_SLOPE = 1.702
LANES = 128
MASKED = -1e30
COPIES = 4
EXTRA = 16
GRID = 32

CORE_PAIRS = [(0, 1), (1, 0), (2, 3), (3, 2)]
X_PAIRS = [(0, 2), (2, 0), (1, 3), (3, 1)]
RING = (0, 2, 4, 6, 7, 5, 3, 1)
RING_AT = tuple(RING.index(i) for i in range(8))
RIGHT = [(RING[i], RING[(i + 1) % 8]) for i in range(8)]
LEFT = [(RING[i], RING[(i - 1) % 8]) for i in range(8)]
OFFSETS = (0, -1, 1, -2, 2, -3, 3, 4, 4)

F32 = jnp.float32
BF16 = jnp.bfloat16
VMEM_LIMIT = 32 * 1024 * 1024


def norm_parts(values):
    center = values - jnp.mean(values, -1, keepdims=True)
    inverse = lax.rsqrt(jnp.mean(center * center, -1, keepdims=True) + EPSILON)
    return (center * inverse, inverse)


def norm_back(grad_normed, unit, inverse, scale):
    scaled = grad_normed * scale
    return inverse * (
        scaled
        - jnp.mean(scaled, -1, keepdims=True)
        - unit * jnp.mean(scaled * unit, -1, keepdims=True)
    )


def outer(left, right):
    return lax.dot_general(left, right, (((0,), (0,)), ((), ())), preferred_element_type=F32)


def times_transposed(left, right):
    return lax.dot_general(left, right, (((1,), (1,)), ((), ())), preferred_element_type=F32)


def times(left, right):
    return jnp.dot(left, right, preferred_element_type=F32)


def tie(values, after=()):
    values, after = tuple(values), tuple(after)
    return lax.optimization_barrier(values + after)[: len(values)]


def to_core(value):
    return lax.ppermute(value, "rep", CORE_PAIRS)


def to_x(value):
    return lax.ppermute(value, "rep", X_PAIRS)


def gather_rep(value):
    near, far = to_core(value), to_x(value)
    return [value, near, far, to_core(far)]


def reduce_pair(parts):
    low = parts.astype(BF16)
    arrived = to_core(jnp.stack([low[1], low[3]]))
    return (jnp.stack([low[0], low[2]]).astype(F32) + arrived.astype(F32)).astype(BF16)


def scatter_rep(parts):
    pair = reduce_pair(parts)
    return pair[0].astype(F32) + to_x(pair[1]).astype(F32)


def sum_rep(parts):
    pair = reduce_pair(parts)
    arrived = to_x(pair)
    total = (pair.astype(F32) + arrived[::-1].astype(F32)).astype(BF16)
    near = to_core(total)
    return jnp.stack([total[0], near[0], total[1], near[1]])


def by_owner(slots, me):
    core, far = me % 2 == 1, me // 2 == 1
    a, b, c, d = slots
    a, b, c, d = (
        jnp.where(core, b, a),
        jnp.where(core, a, b),
        jnp.where(core, d, c),
        jnp.where(core, c, d),
    )
    return [jnp.where(far, c, a), jnp.where(far, d, b), jnp.where(far, a, c), jnp.where(far, b, d)]


def gather_shards(pieces, shards):
    return [lax.all_gather(piece, "shard", axis=0) for piece in pieces]


def scatter_shards(whole, shards, rights):
    return lax.psum_scatter(whole, "shard", scatter_dimension=0, tiled=False)


def window(values, start, size):
    part = values[:, start : start + size]
    return jnp.concatenate([part, jnp.zeros((part.shape[0], LANES - size), part.dtype)], 1)


def turned(values, half, lane):
    return jnp.where(
        lane < half,
        pltpu.roll(values, LANES - half, 1),
        pltpu.roll(values, half, 1),
    )


def attend_kernel(
    heads, size, x_ref, gain_ref, shift_ref, w_ref, bias_ref, cos_ref, sin_ref, row_ref, col_ref,
    normed_ref, qkv_ref, lse_ref, out_ref,
):
    unit, _ = norm_parts(x_ref[...].astype(F32))
    normed = (unit * gain_ref[...] + shift_ref[...]).astype(BF16)
    normed_ref[...] = normed
    projected = times(normed, w_ref[...]) + bias_ref[...]
    cosine, sine = cos_ref[...], sin_ref[...]
    rows = projected.shape[0]
    lane = lax.broadcasted_iota(jnp.int32, (rows, LANES), 1)
    same = col_ref[...] == row_ref[0]
    scale = size**-0.5
    half = size // 2
    outs = []
    lses = jnp.zeros((rows, LANES), F32)
    for head in range(heads):
        query, key, value = (
            window(projected, (part * heads + head) * size, size) for part in range(3)
        )
        query = (query * cosine + turned(query, half, lane) * sine).astype(BF16)
        key = (key * cosine + turned(key, half, lane) * sine).astype(BF16)
        value = value.astype(BF16)
        for part, kept in enumerate((query, key, value)):
            at = (part * heads + head) * LANES
            qkv_ref[:, at : at + LANES] = kept
        scores = jnp.where(same, times_transposed(query, key) * scale, MASKED)
        most = jnp.max(scores, -1, keepdims=True)
        expo = jnp.exp(scores - most)
        total = jnp.sum(expo, -1, keepdims=True)
        probs = (expo * (1.0 / total)).astype(BF16)
        outs.append(times(probs, value)[:, :size])
        lses = jnp.where(lane == head, most + jnp.log(total), lses)
    lse_ref[...] = lses
    out_ref[...] = jnp.concatenate(outs, 1).astype(BF16)


def attend(x, gain, shift, weight, bias, cosine, sine, seg_rows, seg_cols, heads, size):
    tokens, width = x.shape
    length = seg_rows.shape[-1]
    part = heads * size
    by_block = lambda columns: pl.BlockSpec((length, columns), lambda i: (i, 0))
    fixed = lambda array: pl.BlockSpec(array.shape, lambda i: (0,) * array.ndim)
    return pl.pallas_call(
        lambda *refs: attend_kernel(heads, size, *refs),
        grid=(tokens // length,),
        in_specs=[
            by_block(width),
            fixed(gain),
            fixed(shift),
            fixed(weight),
            fixed(bias),
            by_block(LANES),
            by_block(LANES),
            pl.BlockSpec((1, 1, length), lambda i: (i, 0, 0)),
            by_block(1),
        ],
        out_specs=[by_block(width), by_block(3 * heads * LANES), by_block(LANES), by_block(part)],
        out_shape=[
            jax.ShapeDtypeStruct((tokens, width), BF16),
            jax.ShapeDtypeStruct((tokens, 3 * heads * LANES), BF16),
            jax.ShapeDtypeStruct((tokens, LANES), F32),
            jax.ShapeDtypeStruct((tokens, part), BF16),
        ],
        compiler_params=pltpu.CompilerParams(vmem_limit_bytes=48 * 1024 * 1024),
        cost_estimate=pl.CostEstimate(
            flops=2 * tokens * width * 3 * part + 4 * tokens * length * part,
            bytes_accessed=4 * tokens * width + weight.size * 2 + tokens * 3 * heads * LANES * 2,
            transcendentals=tokens * length * heads,
        ),
    )(x, gain, shift, weight, bias, cosine, sine, seg_rows, seg_cols)


def attend_back_kernel(
    heads, size, db_ref, wo_ref, qkv_ref, lse_ref, cos_ref, sin_ref, row_ref, col_ref, w_ref,
    x_ref, grad_ref, dn_ref, sum_ref, gain_ref, shift_ref,
):
    mixed = times_transposed(db_ref[...], wo_ref[...])
    cosine, sine = cos_ref[...], sin_ref[...]
    rows = mixed.shape[0]
    lane = lax.broadcasted_iota(jnp.int32, (rows, LANES), 1)
    same = col_ref[...] == row_ref[0]
    scale = size**-0.5
    half = size // 2
    lses = lse_ref[...]
    grads = [None] * (3 * heads)
    for head in range(heads):
        query, key, value = (
            qkv_ref[:, (part * heads + head) * LANES : (part * heads + head + 1) * LANES]
            for part in range(3)
        )
        lse = jnp.sum(jnp.where(lane == head, lses, 0.0), -1, keepdims=True)
        scores = jnp.where(same, times_transposed(query, key) * scale, MASKED)
        probs = jnp.exp(scores - lse)
        grad_mixed = window(mixed, head * size, size).astype(BF16)
        grad_probs = times_transposed(grad_mixed, value)
        grad_value = outer(probs.astype(BF16), grad_mixed)
        inner = jnp.sum(probs * grad_probs, -1, keepdims=True)
        low = (probs * (grad_probs - inner)).astype(BF16)
        grad_query = times(low, key) * scale
        grad_key = outer(low, query) * scale
        grad_query = grad_query * cosine + turned(grad_query * sine, half, lane)
        grad_key = grad_key * cosine + turned(grad_key * sine, half, lane)
        grads[head] = grad_query[:, :size]
        grads[heads + head] = grad_key[:, :size]
        grads[2 * heads + head] = grad_value[:, :size]
    grad = jnp.concatenate(grads, 1).astype(BF16)
    grad_ref[...] = grad
    grad_normed = times_transposed(grad, w_ref[...])
    dn_ref[...] = grad_normed.astype(BF16)
    unit, _ = norm_parts(x_ref[...].astype(F32))

    @pl.when(pl.program_id(0) == 0)
    def _():
        sum_ref[...] = jnp.zeros_like(sum_ref)
        gain_ref[...] = jnp.zeros_like(gain_ref)
        shift_ref[...] = jnp.zeros_like(shift_ref)

    sum_ref[...] += jnp.sum(grad.astype(F32), 0, keepdims=True)
    gain_ref[...] += jnp.sum(grad_normed * unit, 0, keepdims=True)
    shift_ref[...] += jnp.sum(grad_normed, 0, keepdims=True)


def attend_back(db, w_out, qkv, lse, cosine, sine, seg_rows, seg_cols, weight, x, heads, size):
    tokens, width = x.shape
    length = seg_rows.shape[-1]
    part = heads * size
    by_block = lambda columns: pl.BlockSpec((length, columns), lambda i: (i, 0))
    fixed = lambda shape: pl.BlockSpec(shape, lambda i: (0,) * len(shape))
    return pl.pallas_call(
        lambda *refs: attend_back_kernel(heads, size, *refs),
        grid=(tokens // length,),
        in_specs=[
            by_block(width),
            fixed(w_out.shape),
            by_block(3 * heads * LANES),
            by_block(LANES),
            by_block(LANES),
            by_block(LANES),
            pl.BlockSpec((1, 1, length), lambda i: (i, 0, 0)),
            by_block(1),
            fixed(weight.shape),
            by_block(width),
        ],
        out_specs=[
            by_block(3 * part),
            by_block(width),
            fixed((1, 3 * part)),
            fixed((1, width)),
            fixed((1, width)),
        ],
        out_shape=[
            jax.ShapeDtypeStruct((tokens, 3 * part), BF16),
            jax.ShapeDtypeStruct((tokens, width), BF16),
            jax.ShapeDtypeStruct((1, 3 * part), F32),
            jax.ShapeDtypeStruct((1, width), F32),
            jax.ShapeDtypeStruct((1, width), F32),
        ],
        compiler_params=pltpu.CompilerParams(vmem_limit_bytes=48 * 1024 * 1024),
        cost_estimate=pl.CostEstimate(
            flops=2 * tokens * width * 4 * part + 10 * tokens * length * part,
            bytes_accessed=6 * tokens * width + weight.size * 2 + tokens * 3 * heads * LANES * 2,
            transcendentals=tokens * length * heads,
        ),
    )(db, w_out, qkv, lse, cosine, sine, seg_rows, seg_cols, weight, x)


def rotary(rows, columns, size):
    quarter = size // 4
    inverse = 10000.0 ** (-4.0 * jnp.arange(quarter, dtype=F32) / size)
    angles = jnp.concatenate(
        [rows.astype(F32)[:, None] * inverse, columns.astype(F32)[:, None] * inverse], -1
    )
    cosine, sine = jnp.cos(angles), jnp.sin(angles)
    nothing = jnp.zeros((rows.shape[0], LANES - size), F32)
    return (
        jnp.concatenate([cosine, cosine, nothing], -1),
        jnp.concatenate([-sine, sine, nothing], -1),
    )


def on_any(
    shards,
    hidden_in,
    seg_ids,
    patch_rows,
    patch_cols,
    ln1_scale,
    ln1_shift,
    qkv_weight,
    qkv_bias,
    out_weight,
    out_bias,
    ln2_scale,
    ln2_shift,
    up_weight,
    up_bias,
    down_weight,
    down_bias,
    cotangent,
):
    copies = 4
    me = lax.axis_index("rep")
    length, width = hidden_in.shape
    rows = ln1_scale.shape[0]
    size = width // HEADS
    heads = HEADS // copies
    part = heads * size
    hidden = up_weight.shape[1]
    own_hidden = hidden // copies
    step = hidden // shards // copies

    def own(array, axis):
        return lax.dynamic_index_in_dim(array, me, axis, False)

    own_qkv = own(qkv_weight.reshape(rows, 3, copies, part), 2).reshape(rows, 3 * part)
    own_up = own(up_weight.reshape(rows, shards, copies, step), 2).reshape(rows, own_hidden)
    own_down = own(down_weight.reshape(copies, step, width), 0)
    own_out = own(out_weight.reshape(copies, rows // copies, width), 0)
    vectors = (
        ln1_scale, ln1_shift, out_bias, ln2_scale, ln2_shift, down_bias, qkv_bias, up_bias,
    )
    small = jnp.concatenate(vectors)
    small_rows = 8
    small = jnp.pad(small, (0, small_rows * 3 * part - small.size)).reshape(small_rows, 3 * part)
    first, up_full, out_all, down_full = gather_shards(
        [
            jnp.concatenate([own_qkv, small]),
            own_up,
            own_out,
            own_down,
        ],
        shards,
    )
    w_qkv = first[:, :rows].reshape(width, 3 * part)
    small = first[:, rows:].reshape(shards, -1)
    up_full = up_full.reshape(width, own_hidden)
    down_full = down_full.reshape(own_hidden, width)
    full = []
    at = 0
    for vector in vectors:
        full.append(small[:, at : at + vector.size].astype(F32))
        at += vector.size
    gain_one, shift_one, out_offset, gain_two, shift_two, down_offset = (
        v.reshape(1, width) for v in full[:6]
    )
    qkv_offset = own(full[6].reshape(3, copies, part), 1).reshape(1, 3 * part)
    up_offset = own(full[7].reshape(shards, copies, step), 1).reshape(1, own_hidden)

    ids = jnp.concatenate([seg_ids, patch_rows, patch_cols])
    ids = jnp.stack(gather_rep(ids))
    seg_rows, seg_cols = ids[:, :1], ids[:, 0].reshape(-1, 1)
    x_low = jnp.concatenate(gather_rep(hidden_in))
    grad_out = jnp.concatenate(gather_rep(cotangent))
    tokens = x_low.shape[0]
    cosine, sine = rotary(ids[:, 1].reshape(-1), ids[:, 2].reshape(-1), size)

    normed_one, qkv, lse, mixed = attend(
        x_low, gain_one, shift_one, w_qkv, qkv_offset, cosine, sine, seg_rows, seg_cols, heads, size
    )
    out_full = jnp.stack(by_owner(gather_rep(out_all), me), 1).reshape(width, width)
    blocks = mixed.reshape(copies, length, part)
    near, far = to_core(blocks), to_x(blocks)
    both = to_core(far)
    mixed_slots = [
        mixed,
        near[jnp.array([1, 0, 3, 2])].reshape(tokens, part),
        far[jnp.array([2, 3, 0, 1])].reshape(tokens, part),
        both[jnp.array([3, 2, 1, 0])].reshape(tokens, part),
    ]
    mixed_full = jnp.concatenate(by_owner(mixed_slots, me), 1)

    middle = x_low.astype(F32) + times(mixed_full, out_full) + out_offset
    unit_two, inverse_two = norm_parts(middle)
    normed_two = (unit_two * gain_two + shift_two).astype(BF16)
    upward = times(normed_two, up_full) + up_offset
    sigma = jax.nn.sigmoid(GELU_SLOPE * upward)
    activated = (upward * sigma).astype(BF16)
    slope = sigma + GELU_SLOPE * upward * sigma * (1.0 - sigma)

    grad_down = outer(activated, grad_out).astype(BF16)
    grad_up_low = (times_transposed(grad_out, down_full) * slope).astype(BF16)
    grad_normed_two = sum_rep(times_transposed(grad_up_low, up_full).reshape(copies, length, width))
    grad_up = outer(normed_two, grad_up_low).astype(BF16)
    grad_up_bias = jnp.sum(grad_up_low.astype(F32), 0)
    branch = scatter_rep(times(activated, down_full).reshape(copies, length, width))
    output = middle[:length] + branch + down_offset

    grad_normed_two = grad_normed_two.reshape(tokens, width).astype(F32)
    grad_middle = grad_out.astype(F32) + norm_back(
        grad_normed_two, unit_two, inverse_two, gain_two
    )
    grad_branch = grad_middle.astype(BF16)
    grad_out_w = outer(mixed_full, own(grad_branch.reshape(tokens, copies, part), 1)).astype(BF16)

    own_w_out = lax.dynamic_slice_in_dim(out_full, me * part, part, 0)
    grad_qkv_low, grad_normed_one, sum_qkv, sum_gain, sum_shift = attend_back(
        grad_branch, own_w_out, qkv, lse, cosine, sine, seg_rows, seg_cols, w_qkv, x_low, heads, size
    )
    grad_qkv = outer(normed_one, grad_qkv_low).astype(BF16)
    grad_normed_one = scatter_rep(grad_normed_one.reshape(copies, length, width))
    unit_one, inverse_one = norm_parts(hidden_in.astype(F32))
    grad_inputs = grad_middle[:length] + norm_back(grad_normed_one, unit_one, inverse_one, gain_one)

    def sum_of(values):
        return jnp.sum(values[:length], 0).reshape(shards, rows)

    def placed(values, like, axis):
        return lax.dynamic_update_index_in_dim(jnp.zeros(like, F32), values, me, axis)

    sums = [
        sum_gain.reshape(shards, rows),
        sum_shift.reshape(shards, rows),
        sum_of(grad_branch.astype(F32)),
        sum_of(grad_normed_two * unit_two),
        sum_of(grad_normed_two),
        sum_of(grad_out.astype(F32)),
        placed(sum_qkv.reshape(3, part), (3, copies, part), 1).reshape(shards, -1),
        placed(grad_up_bias.reshape(shards, step), (shards, copies, step), 1).reshape(shards, -1),
    ]
    sums = jnp.concatenate(sums, 1)
    sums = jnp.pad(sums, ((0, 0), (0, small_rows * 3 * part - sums.shape[1])))
    last = jnp.concatenate(
        [grad_qkv.reshape(shards, rows, 3 * part), sums.astype(BF16).reshape(shards, small_rows, -1)],
        1,
    )

    done_down = scatter_shards(grad_down.reshape(shards, step, width), shards, 4)
    done_up = scatter_shards(grad_up.reshape(shards, rows, own_hidden), shards, 3)
    done_out = scatter_shards(grad_out_w.reshape(shards, rows, part), shards, 4)
    done_last = scatter_shards(last, shards, 4)

    whole_down = jnp.concatenate(by_owner(gather_rep(done_down), me), 0).astype(F32)
    whole_up = jnp.stack(
        [p.reshape(rows, shards, step) for p in by_owner(gather_rep(done_up), me)], 2
    )
    whole_up = whole_up.reshape(rows, hidden).astype(F32)
    whole_out = jnp.concatenate(by_owner(gather_rep(done_out), me), 1).astype(F32)
    last_slots = gather_rep(done_last)
    whole_qkv = jnp.stack(
        [p[:rows].reshape(rows, 3, part) for p in by_owner(last_slots, me)], 2
    )
    whole_qkv = whole_qkv.reshape(rows, 3 * width).astype(F32)
    summed = sum(p[rows:].astype(F32) for p in by_owner(last_slots, me)).reshape(-1)
    totals = []
    at = 0
    for vector in vectors:
        totals.append(summed[at : at + vector.size])
        at += vector.size
    return (
        output.astype(BF16),
        grad_inputs.astype(BF16),
        totals[0],
        totals[1],
        whole_qkv,
        totals[6],
        whole_out,
        totals[2],
        totals[3],
        totals[4],
        whole_up,
        totals[7],
        whole_down,
        totals[5],
    )


def ring_slots():
    position = jnp.asarray(RING_AT, jnp.int32)[lax.axis_index("shard")]
    return jnp.asarray(RING, jnp.int32)[(position + jnp.asarray(OFFSETS, jnp.int32)) % 8]


def half_of(rows):
    return (rows // 2 + 15) // 16 * 16


def ring_gather(piece, after=(), others=None):
    right = left = piece
    if after:
        right, left = tie((piece, piece), after)
    pieces = [piece]
    for hop in range(4):
        if hop == 3:
            cut = half_of(piece.shape[0])
            right, left = right[:cut], left[cut:]
        right, left = tie(
            (lax.ppermute(right, "shard", RIGHT), lax.ppermute(left, "shard", LEFT)),
            (others or {}).get(hop, ()),
        )
        pieces += [right, left]
    return pieces


def hop_kernel(first, _, ahead_ref, behind_ref, right_ref, left_ref, to_right_ref, to_left_ref):
    i = pl.program_id(0)

    def plus(out_ref, own_ref, other_ref):
        out_ref[...] = (own_ref[0].astype(F32) + other_ref[...].astype(F32)).astype(BF16)

    def copy(out_ref, own_ref):
        out_ref[...] = own_ref[0]

    if not first:
        plus(to_right_ref, ahead_ref, right_ref)
        plus(to_left_ref, behind_ref, left_ref)
        return

    @pl.when(i < pl.num_programs(0) // 2)
    def _():
        plus(to_right_ref, ahead_ref, right_ref)
        copy(to_left_ref, behind_ref)

    @pl.when(i >= pl.num_programs(0) // 2)
    def _():
        copy(to_right_ref, ahead_ref)
        plus(to_left_ref, behind_ref, left_ref)


def hop_sums(whole, slots, right, left, hop, steps):
    _, rows, width = whole.shape
    tile = rows // steps
    half = steps // 2
    first = hop == 0
    term = lambda n: pl.BlockSpec((1, tile, width), lambda i, s: (s[n], i, 0))
    block = lambda at: pl.BlockSpec((tile, width), lambda i, s: (at(i), 0))
    same = lambda i: i
    return pl.pallas_call(
        lambda *refs: hop_kernel(first, *refs),
        grid_spec=pltpu.PrefetchScalarGridSpec(
            num_scalar_prefetch=1,
            grid=(steps,),
            in_specs=[
                term(6 - 2 * hop),
                term(5 - 2 * hop),
                block((lambda i: jnp.minimum(i, half - 1)) if first else same),
                block((lambda i: jnp.maximum(i - half, 0)) if first else same),
            ],
            out_specs=[block(same), block(same)],
        ),
        out_shape=[like((rows, width), BF16)] * 2,
        compiler_params=params(),
        cost_estimate=cost(),
    )(slots, whole, whole, right, left)


def ring_scatter(whole, right, left, slots, others=None, after=(), steps=0):
    cut = right.shape[0]

    def own(number):
        return lax.dynamic_slice(
            whole, (slots[number], 0, 0), (1,) + whole.shape[1:], allow_negative_indices=False
        )[0]

    if after:
        right, left = tie((right, left), after)
    for hop in range(4):
        waited = (others or {}).get(hop, ())
        if callable(waited):
            waited = waited(right)
        right, left = tie(
            (lax.ppermute(right, "shard", RIGHT), lax.ppermute(left, "shard", LEFT)), waited
        )
        if hop == 3:
            break
        if steps:
            right, left = hop_sums(whole, slots, right, left, hop, steps)
            continue
        ahead, behind = own(6 - 2 * hop), own(5 - 2 * hop)
        if hop == 0:
            right = jnp.concatenate([add_low(right, ahead[:cut]), ahead[cut:]])
            left = jnp.concatenate([behind[:cut], add_low(left, behind[cut:])])
        else:
            right, left = add_low(right, ahead), add_low(left, behind)
    return (right.astype(F32) + left.astype(F32) + own(0).astype(F32)).astype(BF16)


def run_copies(copies):
    for copy in copies:
        copy.start()
    for copy in copies:
        copy.wait()


ANYWHERE = pl.BlockSpec(memory_space=pl.ANY)
SCALARS = pl.BlockSpec(memory_space=pltpu.SMEM)
WHOLE = pl.BlockSpec(memory_space=pltpu.VMEM)


def params():
    return pltpu.CompilerParams(vmem_limit_bytes=VMEM_LIMIT)


def fixed(shape):
    return pl.BlockSpec(shape, lambda i: (0,) * len(shape))


def cost(microseconds=0):
    return pl.CostEstimate(flops=1, bytes_accessed=1 + microseconds * 3_690_000, transcendentals=0)


def like(shape, dtype):
    return jax.ShapeDtypeStruct(shape, dtype)


def far(shape, dtype):
    return pltpu.HBM(shape, dtype)


def kept_far(arrays):
    return [pltpu.with_memory_space_constraint(a, pltpu.HBM) for a in arrays]


def joined(slots):
    return jnp.concatenate(slots, 0)


def column_order(heads, size):
    half = size // 2
    left = heads * half - LANES
    order = np.zeros((2 * heads * size, 2 * heads * size), np.float32)
    for part in range(2):
        for head in range(heads):
            for side in range(2):
                for feature in range(half):
                    natural = (part * heads + head) * size + side * half + feature
                    at = head * half + feature
                    group = 2 * part + side
                    to = group * LANES + at if at < LANES else (4 * LANES + group * left + at - LANES)
                    order[natural, to] = 1.0
    return jnp.asarray(order, BF16)


def head_masks(heads, size):
    half = size // 2
    left = heads * half - LANES
    masks = np.zeros((2 * heads, 3 * LANES), np.float32)
    for head in range(heads):
        for lane in range(2 * LANES):
            masks[head, lane] = (lane % LANES) // half == head
        for lane in range(2 * left):
            masks[head, 2 * LANES + lane] = (LANES + lane % left) // half == head
        masks[heads + head, head * size : (head + 1) * size] = 1.0
    return jnp.asarray(masks, F32)


def rotary_table(heads, size):
    half, quarter = size // 2, size // 4
    left = heads * half - LANES
    at = np.concatenate([np.arange(LANES), LANES + np.arange(4 * left) % left]) % half
    inverse = (10000.0 ** (-4.0 * np.arange(quarter, dtype=np.float32) / size)).astype(np.float32)
    angles = np.arange(GRID, dtype=np.float32)[:, None] * inverse[at % quarter]
    sign = np.ones(2 * LANES, np.float32)
    for group in (0, 2):
        sign[LANES + group * left : LANES + (group + 1) * left] = -1.0
    both = np.concatenate([np.cos(angles), np.sin(angles) * sign], 1)
    by_row = np.concatenate([at < quarter, at < quarter])
    return jnp.asarray(np.concatenate([np.where(by_row, both, 0.0), np.where(by_row, 0.0, both)]), F32)


def positions(ids, table):
    grid = lax.broadcasted_iota(jnp.int32, (GRID, ids.shape[1]), 0)
    picks = jnp.concatenate([grid == ids[1:2], grid == ids[2:3]], 0).astype(F32)
    both = lax.dot_general(
        picks, table, (((0,), (0,)), ((), ())), precision=lax.Precision.HIGHEST,
        preferred_element_type=F32,
    )
    image = (grid[:8] == ids[0:1]).astype(F32)
    return tiles(both, 4), outer(image, image) > 0.5


def first_kernel(part, *refs):
    me_ref, order_ref, weight_ref, other_ref = refs[:4]
    vectors, out_ref = refs[4:12], refs[12]
    rows, width = out_ref.shape[0] - EXTRA, out_ref.shape[1]
    for me in range(COPIES):

        @pl.when(me_ref[0] == me)
        def _():
            parts = [
                weight_ref[:, (n * COPIES + me) * part : (n * COPIES + me + 1) * part]
                for n in range(3)
            ]
            turned = times(jnp.concatenate(parts[:2], 1), order_ref[...]).astype(BF16)
            out_ref[:rows] = jnp.concatenate(
                [turned, parts[2], other_ref[:, me * part : (me + 1) * part]], 1
            )

    lines = [v[...].astype(F32).reshape(1, -1) for v in vectors]
    lines = [jnp.concatenate(lines[:6], 1), lines[6], lines[7]]
    lines = [
        jnp.concatenate([line, jnp.zeros((1, width - line.shape[1]), F32)], 1) for line in lines
    ]
    lines.append(jnp.zeros((EXTRA - len(lines), width), F32))
    out_ref[rows:] = jnp.concatenate(lines, 0).astype(BF16)


def first_piece(me, order, weight, other, vectors, part):
    rows = weight.shape[0]
    return pl.pallas_call(
        lambda *refs: first_kernel(part, *refs),
        in_specs=[SCALARS] + [WHOLE] * 11,
        out_specs=WHOLE,
        out_shape=like((rows + EXTRA, COPIES * part), BF16),
        compiler_params=params(),
        cost_estimate=cost(),
    )(me, *kept_far([order, weight, other, *vectors]))


def collect_kernel(rows, *refs):
    pieces, (out_ref, lines_ref, semaphores) = refs[:9], refs[9:]
    lanes = lines_ref.shape[2]
    part = out_ref.shape[1] // COPIES
    copies = []
    for number, ref in enumerate(pieces):
        edge = half_of(rows + EXTRA)
        start, count = (edge, rows - edge) if number == 8 else (0, edge if number == 7 else rows)
        copies.append(
            pltpu.make_async_copy(
                ref.at[pl.ds(0, count), pl.ds(ref.shape[1] - lanes, lanes)],
                lines_ref.at[min(number, 7), pl.ds(start, count)],
                semaphores.at[number],
            )
        )
    run_copies(copies)
    for line in range(2):
        out_ref[line * rows : (line + 1) * rows] = jnp.concatenate(
            [lines_ref[2 * n + line][:, lanes - part :] for n in range(COPIES)], 1
        )


def collect(pieces, rows, part):
    lanes = -(-part // LANES) * LANES
    return pl.pallas_call(
        lambda *refs: collect_kernel(rows, *refs),
        in_specs=[ANYWHERE] * len(pieces),
        out_specs=WHOLE,
        out_shape=like((2 * rows, COPIES * part), BF16),
        scratch_shapes=[pltpu.VMEM((8, rows, lanes), BF16), pltpu.SemaphoreType.DMA((9,))],
        compiler_params=params(),
        cost_estimate=cost(),
    )(*kept_far(pieces))


def second_kernel(shards, me_ref, up_ref, down_ref, out_ref):
    rows, hidden = up_ref.shape
    step = hidden // shards // COPIES
    for me in range(COPIES):

        @pl.when(me_ref[0] == me)
        def _():
            out_ref[:rows] = jnp.concatenate(
                [
                    up_ref[:, (n * COPIES + me) * step : (n * COPIES + me + 1) * step]
                    for n in range(shards)
                ],
                1,
            )
            out_ref[rows:] = down_ref[me * step : (me + 1) * step]


def second_piece(me, up, down, shards):
    rows, hidden = up.shape
    step = hidden // shards // COPIES
    return pl.pallas_call(
        lambda *refs: second_kernel(shards, *refs),
        in_specs=[SCALARS] + [WHOLE] * 2,
        out_specs=WHOLE,
        out_shape=like((rows + step, hidden // COPIES), BF16),
        compiler_params=params(),
        cost_estimate=cost(),
    )(me, *kept_far([up, down]))


def first_copies(refs, place, rows, w_ref, small_ref, semaphores):
    cut = half_of(rows + EXTRA)
    copies = []
    for number, ref in enumerate(refs):
        slot = place[number]
        start, count = (cut, rows - cut) if number == 8 else (0, cut if number == 7 else rows)
        at = pl.multiple_of(slot * rows + start, 16)
        copies.append(
            pltpu.make_async_copy(
                ref.at[pl.ds(0, count), pl.ds(0, w_ref.shape[1])],
                w_ref.at[pl.ds(at, count)],
                semaphores.at[0, number],
            )
        )
        if number != 7 and small_ref is not None:
            copies.append(
                pltpu.make_async_copy(
                    ref.at[pl.ds(count, EXTRA)], small_ref.at[slot], semaphores.at[1, number]
                )
            )
    return copies


def vectors_of(me_ref, small_ref, order_ref, vec_ref, bias_ref, full_ref):
    shards = small_ref.shape[0]
    width = vec_ref.shape[1]
    rows = width // shards
    part = width // COPIES
    lines = [small_ref[s].astype(F32) for s in range(shards)]
    for n in range(6):
        vec_ref[n : n + 1] = jnp.concatenate(
            [line[0:1, n * rows : (n + 1) * rows] for line in lines], 1
        )
    full_ref[...] = jnp.concatenate([line[1:2, : 3 * rows] for line in lines], 1)
    vec_ref[7:8] = jnp.zeros((1, width), F32)
    bias_ref[...] = jnp.zeros_like(bias_ref)
    for me in range(COPIES):

        @pl.when(me_ref[0] == me)
        def _():
            vec_ref[6:7] = jnp.concatenate(
                [line[2:3, me * rows : (me + 1) * rows] for line in lines], 1
            )
            parts = [
                full_ref[:, (n * COPIES + me) * part : (n * COPIES + me + 1) * part] for n in range(3)
            ]
            both = jnp.broadcast_to(jnp.concatenate(parts[:2], 1), (8, 2 * part)).astype(BF16)
            bias_ref[:, : 2 * part] = times(both, order_ref[...])[:1]
            bias_ref[:, 2 * part : 3 * part] = parts[2]


def swapped(values, lane, left):
    return jnp.where(
        lane // left % 2 == 0,
        pltpu.roll(values, LANES - left, 1),
        pltpu.roll(values, left, 1),
    )


def tiles(values, count):
    return [values[:, n * LANES : (n + 1) * LANES] for n in range(count)]


def ring_attend_kernel(heads, size, *refs):
    (
        me_ref, place_ref, order_ref, mask_ref, table_ref, x0, x1, x2, x3, ids_ref,
    ), refs = refs[:10], refs[10:]
    pieces, refs = refs[:9], refs[9:]
    (
        normed_ref, qkv_ref, lse_ref, out_ref, vec_ref, w_ref, small_ref, bias_ref, full_ref, all_ref,
        project_ref, semaphores,
    ) = refs
    i = pl.program_id(0)
    length, width = x0.shape
    rows = width // 8
    part = heads * size

    @pl.when(i == 0)
    def _():
        copies = first_copies(pieces, place_ref, rows, w_ref, small_ref, semaphores)
        for copy in copies:
            copy.start()
        for copy in copies[1:14:2] + copies[-1:]:
            copy.wait()
        vectors_of(me_ref, small_ref, order_ref, vec_ref, bias_ref, full_ref)
        for slot, x_ref in enumerate((x0, x1, x2, x3)):
            unit, _ = norm_parts(x_ref[...].astype(F32))
            all_ref[slot * length : (slot + 1) * length] = (
                unit * vec_ref[0:1] + vec_ref[1:2]
            ).astype(BF16)
        for copy in copies[0:14:2] + copies[14:16]:
            copy.wait()
        project_ref[...] = times(all_ref[...], w_ref[...]) + bias_ref[...]

    here = pl.ds(pl.multiple_of(i * length, 16), length)
    normed_ref[...] = all_ref[here, :]
    q1, q2, k1, k2, rest = tiles(project_ref[here, : 5 * LANES], 5)
    value = project_ref[here, 5 * LANES :]
    lane = lax.broadcasted_iota(jnp.int32, (length, LANES), 1)
    wide = lax.broadcasted_iota(jnp.int32, (length, 3 * LANES), 1)
    (cosine, cosine_rest, sine, sine_rest), same = positions(ids_ref[0], table_ref[...])
    left = heads * size // 2 - LANES
    rest = rest * cosine_rest + swapped(rest, lane, left) * sine_rest
    query = jnp.concatenate(
        [q1 * cosine - q2 * sine, q2 * cosine + q1 * sine, jnp.where(lane < 2 * left, rest, 0.0)], 1
    ).astype(BF16)
    key = jnp.concatenate(
        [
            k1 * cosine - k2 * sine,
            k2 * cosine + k1 * sine,
            jnp.where(lane < 2 * left, pltpu.roll(rest, 2 * left, 1), 0.0),
        ],
        1,
    ).astype(BF16)
    value = jnp.where(wide < part, value, 0.0).astype(BF16)
    qkv_ref[...] = jnp.concatenate([query, key, value], 1)
    masks = mask_ref[...].astype(BF16)
    scale = size**-0.5
    all_probs, all_values = [], []
    lses = jnp.zeros((length, LANES), F32)
    for head in range(heads):
        scores = times_transposed(query * masks[head : head + 1], key)
        scores = jnp.where(same, scores * scale, MASKED)
        most = jnp.max(scores, -1, keepdims=True)
        expo = jnp.exp(scores - most)
        total = jnp.sum(expo, -1, keepdims=True)
        all_probs.append((expo * (1.0 / total)).astype(BF16))
        all_values.append(value * masks[heads + head : heads + head + 1])
        lses = jnp.where(lane == head, most + jnp.log(total), lses)
    lse_ref[...] = lses
    out = times(jnp.concatenate(all_probs, 1), joined(all_values))[:, :part].astype(BF16)
    count = out_ref.shape[1]
    out_ref[0] = jnp.concatenate([out[n * count : (n + 1) * count] for n in range(COPIES)], 1)


def ring_attend(me, place, order, masks, table, x, ids, pieces, heads, size):
    length, width = x[0].shape
    tokens = COPIES * length
    by_block = lambda columns: pl.BlockSpec((length, columns), lambda i: (i, 0))
    return pl.pallas_call(
        lambda *refs: ring_attend_kernel(heads, size, *refs),
        grid=(COPIES,),
        in_specs=[SCALARS, SCALARS, fixed(order.shape), fixed(masks.shape), fixed(table.shape)]
        + [fixed((length, width))] * COPIES
        + [pl.BlockSpec((1,) + ids.shape[1:], lambda i: (i, 0, 0))]
        + [ANYWHERE] * len(pieces),
        out_specs=[
            by_block(width),
            by_block(9 * LANES),
            by_block(LANES),
            pl.BlockSpec((1, length // COPIES, width), lambda i: (i, 0, 0)),
            fixed((8, width)),
        ],
        out_shape=[
            far((tokens, width), BF16),
            far((tokens, 9 * LANES), BF16),
            far((tokens, LANES), F32),
            like((COPIES, length // COPIES, width), BF16),
            like((8, width), F32),
        ],
        scratch_shapes=[
            pltpu.VMEM((width, 8 * LANES), BF16),
            pltpu.VMEM((8, EXTRA, width), BF16),
            pltpu.VMEM((1, 8 * LANES), F32),
            pltpu.VMEM((1, 3 * width), F32),
            pltpu.VMEM((tokens, width), BF16),
            pltpu.VMEM((tokens, 8 * LANES), F32),
            pltpu.SemaphoreType.DMA((2, len(pieces))),
        ],
        compiler_params=params(),
        cost_estimate=cost(25),
    )(
        me, place, *kept_far([order, masks, table, *x]), ids, *kept_far(pieces)
    )


def middle_kernel(rows, part, *refs):
    me_ref, place_ref, own_ref, near_ref, far_ref, both_ref, vec_ref, x0, x1, x2, x3 = refs[:11]
    weights, (all_ref, middle_ref, normed_ref, wown_ref, w_ref, x_ref) = (
        refs[11:15],
        refs[15:],
    )
    j = pl.program_id(0)

    @pl.when(j == 0)
    def _():
        me = me_ref[0]
        for own in range(COPIES):

            @pl.when(me == own)
            def _():
                for n in range(8):
                    here = slice(n % 2 * rows, (n % 2 + 1) * rows)
                    lanes = slice(n // 2 * part, (n // 2 + 1) * part)
                    at = pl.multiple_of(place_ref[n] * rows, 16)
                    w_ref[pl.ds(at, rows), :] = jnp.concatenate(
                        [weights[own ^ b][here, lanes] for b in range(COPIES)], 1
                    )

        wown_ref[...] = w_ref[pl.ds(pl.multiple_of(me * part, 16), part), :]
        x_ref[...] = joined([x0[...], x1[...]])

    @pl.when(j == 1)
    def _():
        x_ref[...] = joined([x2[...], x3[...]])

    def unpacked(ref, order):
        return joined(
            [ref[b, :, n * part : (n + 1) * part] for b in order for n in range(COPIES)]
        )

    slots = [
        unpacked(own_ref, (0, 1)),
        unpacked(near_ref, (1, 0)),
        unpacked(far_ref, (0, 1)),
        unpacked(both_ref, (1, 0)),
    ]
    for me in range(COPIES):

        @pl.when(me_ref[0] == me)
        def _():
            all_ref[...] = jnp.concatenate([slots[me ^ n] for n in range(COPIES)], 1)

    middle = x_ref[...].astype(F32) + times(all_ref[...], w_ref[...]) + vec_ref[2:3]
    unit, _ = norm_parts(middle)
    normed = (unit * vec_ref[3:4] + vec_ref[4:5]).astype(BF16)
    length = middle_ref.shape[2]
    for core in range(2):
        middle_ref[0, core] = middle[core * length : (core + 1) * length]
        normed_ref[0, core] = normed[core * length : (core + 1) * length]


def middle_of(me, place, mixed, vec, x, weights, rows):
    length, width = x[0].shape
    part = width // COPIES
    tokens = COPIES * length
    by_slots = lambda flip: pl.BlockSpec(
        (2,) + mixed[0].shape[1:], lambda j: ((1 - j) if flip else j, 0, 0)
    )
    by_half = pl.BlockSpec((1, 2, length, width), lambda j: (j, 0, 0, 0))
    return pl.pallas_call(
        lambda *refs: middle_kernel(rows, part, *refs),
        grid=(2,),
        in_specs=[SCALARS, SCALARS]
        + [by_slots(False), by_slots(False), by_slots(True), by_slots(True), fixed(vec.shape)]
        + [fixed((length, width))] * COPIES
        + [fixed(weights[0].shape)] * COPIES,
        out_specs=[
            pl.BlockSpec((2 * length, width), lambda j: (j, 0)),
            by_half,
            by_half,
            fixed((part, width)),
        ],
        out_shape=[
            far((tokens, width), BF16),
            far((2, 2, length, width), F32),
            far((2, 2, length, width), BF16),
            far((part, width), BF16),
        ],
        scratch_shapes=[
            pltpu.VMEM((width, width), BF16),
            pltpu.VMEM((2 * length, width), BF16),
        ],
        compiler_params=params(),
        cost_estimate=cost(13),
    )(me, place, *mixed, vec, *kept_far([*x, *weights]))


def split_copies(pieces, place, up_ref, down_ref, semaphores):
    copies = []
    for number, ref in enumerate(pieces):
        for line, target in enumerate((up_ref, down_ref)):
            if target is None or (number == 7 and line == 1) or (number == 8 and line == 0):
                continue
            count = target.shape[0] // 8
            copies.append(
                pltpu.make_async_copy(
                    ref.at[pl.ds(count if line == 1 and number < 7 else 0, count)],
                    target.at[pl.ds(pl.multiple_of(place[number] * count, 16), count)],
                    semaphores.at[line, number],
                )
            )
    return copies


def feed_kernel(place_ref, normed_ref, g0, g1, g2, g3, vec_ref, *refs):
    pieces, refs = refs[:9], refs[9:]
    act_ref, dh_ref, sent_ref, kept_ref, sum_ref, up_ref, down_ref, grad_ref, semaphores = refs
    j = pl.program_id(0)

    @pl.when(j == 0)
    def _():
        copies = split_copies(pieces, place_ref, up_ref, None, semaphores)
        later = split_copies(pieces, place_ref, None, down_ref, semaphores)
        for copy in copies + later:
            copy.start()
        for copy in copies:
            copy.wait()
        sum_ref[...] = jnp.zeros_like(sum_ref)
        sum_ref[1:2] = jnp.sum(g0[...].astype(F32), 0, keepdims=True)
        grad_ref[...] = joined([g1[...], g3[...]])

    @pl.when(j == 1)
    def _():
        grad_ref[...] = joined([g0[...], g2[...]])

    normed = joined([normed_ref[0, 0], normed_ref[1, 0]])
    upward = times(normed, up_ref[...]) + vec_ref[6:7]
    sigma = jax.nn.sigmoid(GELU_SLOPE * upward)
    act = (upward * sigma).astype(BF16)
    slope = sigma + GELU_SLOPE * upward * sigma * (1.0 - sigma)

    @pl.when(j == 0)
    def _():
        for copy in split_copies(pieces, place_ref, None, down_ref, semaphores):
            copy.wait()

    low = (times_transposed(grad_ref[...], down_ref[...]) * slope).astype(BF16)
    sum_ref[0:1] += jnp.sum(low.astype(F32), 0, keepdims=True)
    back = times_transposed(low, up_ref[...]).astype(BF16)
    length = normed_ref.shape[2]
    for half in range(2):
        here = slice(half * length, (half + 1) * length)
        act_ref[half, 0] = act[here]
        dh_ref[half, 0] = low[here]

    @pl.when(j == 0)
    def _():
        for half in range(2):
            sent_ref[half] = back[half * length : (half + 1) * length]

    @pl.when(j == 1)
    def _():
        for half in range(2):
            kept_ref[half] = back[half * length : (half + 1) * length]


def feed(place, normed, grad, vec, pieces, hidden):
    _, _, length, width = normed.shape
    by_core = lambda columns: pl.BlockSpec((2, 1, length, columns), lambda j: (0, 1 - j, 0, 0))
    pair = like((2, length, width), BF16)
    return pl.pallas_call(
        feed_kernel,
        grid=(2,),
        in_specs=[SCALARS, by_core(width)]
        + [fixed((length, width))] * COPIES
        + [fixed(vec.shape)]
        + [ANYWHERE] * len(pieces),
        out_specs=[
            by_core(hidden),
            by_core(hidden),
            fixed((2, length, width)),
            fixed((2, length, width)),
            fixed((8, hidden)),
        ],
        out_shape=[
            far((2, 2, length, hidden), BF16),
            far((2, 2, length, hidden), BF16),
            pair,
            pair,
            like((8, hidden), F32),
        ],
        scratch_shapes=[
            pltpu.VMEM((width, hidden), BF16),
            pltpu.VMEM((hidden, width), BF16),
            pltpu.VMEM((2 * length, width), BF16),
            pltpu.SemaphoreType.DMA((2, 9)),
        ],
        compiler_params=params(),
        cost_estimate=cost(20),
    )(place, *kept_far([normed, *grad]), vec, *kept_far(pieces))


def down_kernel(place_ref, act_ref, *refs):
    pieces, (sent_ref, kept_ref, down_ref, semaphores) = refs[:9], refs[9:]
    j = pl.program_id(0)

    @pl.when(j == 0)
    def _():
        run_copies(split_copies(pieces, place_ref, None, down_ref, semaphores))

    value = times(joined([act_ref[0, 0], act_ref[1, 0]]), down_ref[...]).astype(BF16)
    length = act_ref.shape[2]

    @pl.when(j == 0)
    def _():
        for half in range(2):
            sent_ref[half] = value[half * length : (half + 1) * length]

    @pl.when(j == 1)
    def _():
        for half in range(2):
            kept_ref[half] = value[half * length : (half + 1) * length]


def down_of(place, act, pieces, width):
    _, _, length, hidden = act.shape
    pair = like((2, length, width), BF16)
    return pl.pallas_call(
        down_kernel,
        grid=(2,),
        in_specs=[SCALARS, pl.BlockSpec((2, 1, length, hidden), lambda j: (0, 1 - j, 0, 0))]
        + [ANYWHERE] * len(pieces),
        out_specs=[fixed((2, length, width)), fixed((2, length, width))],
        out_shape=[pair, pair],
        scratch_shapes=[pltpu.VMEM((hidden, width), BF16), pltpu.SemaphoreType.DMA((2, 9))],
        compiler_params=params(),
        cost_estimate=cost(),
    )(place, *kept_far([act, *pieces]))


def feed_grad_kernel(place_ref, normed_ref, act_ref, dh_ref, g0, g1, g2, g3, out_ref, top_ref, bottom_ref):
    i = pl.program_id(0)
    half = pl.num_programs(0) // 2
    width = normed_ref.shape[1]
    rows = width * half // 8

    def put(value, start):
        first = lax.rem(i, half) * width
        for n in range(width // 32):
            at = first + 32 * n
            shard = lax.div(at, rows)
            row = pl.multiple_of(at - shard * rows + start, 32)
            out_ref[shard, pl.ds(row, 32)] = value[32 * n : 32 * n + 32]

    @pl.when(i < half)
    def _():
        put(outer(normed_ref[...], dh_ref[...]).astype(BF16), 0)

    @pl.when(i >= half)
    def _():
        grad = joined([g0[...], g1[...], g2[...], g3[...]])
        put(outer(act_ref[...], grad).astype(BF16), rows)

    @pl.when(i == pl.num_programs(0) - 1)
    def _():
        top_ref[...] = out_ref[place_ref[7], :rows]
        bottom_ref[...] = out_ref[place_ref[7], rows:]


def feed_grads(place, normed, act, dh, grad):
    tokens, width = normed.shape
    length = grad[0].shape[0]
    block = 256
    half = width // block
    return pl.pallas_call(
        feed_grad_kernel,
        grid=(2 * half,),
        in_specs=[
            SCALARS,
            pl.BlockSpec((tokens, block), lambda i: (0, jnp.minimum(i, half - 1))),
            pl.BlockSpec((tokens, block), lambda i: (0, jnp.maximum(i - half, 0))),
            fixed(dh.shape),
        ]
        + [fixed((length, width))] * COPIES,
        out_specs=[
            fixed((8, width // 4, width)),
            fixed((width // 8, width)),
            fixed((width // 8, width)),
        ],
        out_shape=[
            far((8, width // 4, width), BF16),
            like((width // 8, width), BF16),
            like((width // 8, width), BF16),
        ],
        compiler_params=params(),
        cost_estimate=cost(),
    )(place, *kept_far([normed, act, dh, *grad]))


def ring_back_kernel(heads, size, first, *refs):
    (
        me_ref, place_ref, order_ref, mask_ref, table_ref, total_ref, middle_ref, g0, g1, x0, x1, vec_ref,
        wo_ref, qkv_ref, lse_ref, ids_ref,
    ), refs = refs[:16], refs[16:]
    pieces, refs = refs[:9], refs[9:]
    dx_ref = refs[0] if first else None
    cols_ref, grad_ref, share_ref, sums_ref, w_ref, cot_ref, all_ref, semaphores = refs[first:]
    i = pl.program_id(0)
    length, width = x0.shape
    rows = width // 8
    part = heads * size

    @pl.when(i == 0)
    def _():
        for copy in first_copies(pieces, place_ref, rows, w_ref, None, semaphores):
            copy.start()
        sums_ref[...] = jnp.zeros_like(sums_ref)

    for n, grad_ref_in in enumerate((g0, g1)):

        @pl.when(i == n)
        def _():
            cot_ref[...] = grad_ref_in[...].astype(F32)

    grad_normed = total_ref[0].astype(F32)
    unit, inverse = norm_parts(middle_ref[0, 0])
    grad_middle = cot_ref[...] + norm_back(grad_normed, unit, inverse, vec_ref[3:4])
    branch = grad_middle.astype(BF16)

    if first:

        @pl.when(i == 0)
        def _():
            dx_ref[...] = grad_middle
            sums_ref[2:3] = jnp.sum(branch.astype(F32), 0, keepdims=True)
            sums_ref[3:4] = jnp.sum(grad_normed * unit, 0, keepdims=True)
            sums_ref[4:5] = jnp.sum(grad_normed, 0, keepdims=True)

    for me in range(COPIES):

        @pl.when(me_ref[0] == me)
        def _():
            cols_ref[0] = branch[:, me * part : (me + 1) * part]

    mixed = times_transposed(branch, wo_ref[...]).astype(BF16)
    mixed = jnp.concatenate([mixed, jnp.zeros((length, 3 * LANES - part), BF16)], 1)
    query, key, value = (qkv_ref[:, 3 * n * LANES : 3 * (n + 1) * LANES] for n in range(3))
    masks = mask_ref[...].astype(BF16)
    (cosine, cosine_rest, sine, sine_rest), same = positions(ids_ref[0], table_ref[...])
    scale = size**-0.5
    lses = lse_ref[...]
    all_probs, all_lows, queries, keys, mixes = [], [], [], [], []
    for head in range(heads):
        queries.append(query * masks[head : head + 1])
        keys.append(key * masks[head : head + 1])
        mixes.append(mixed * masks[heads + head : heads + head + 1])
        scores = jnp.where(same, times_transposed(queries[-1], key) * scale, MASKED)
        probs = jnp.exp(scores - lses[:, head : head + 1])
        grad_probs = times_transposed(mixes[-1], value)
        inner = jnp.sum(probs * grad_probs, -1, keepdims=True)
        all_probs.append(probs.astype(BF16))
        all_lows.append((probs * (grad_probs - inner)).astype(BF16))
    grad_query = times(jnp.concatenate(all_lows, 1), joined(keys)) * scale
    grad_key = outer(joined(all_lows), joined(queries)) * scale
    grad_value = outer(joined(all_probs), joined(mixes)).astype(BF16)
    lane = lax.broadcasted_iota(jnp.int32, (length, LANES), 1)
    left = heads * size // 2 - LANES
    q1, q2, q_rest = tiles(grad_query, 3)
    k1, k2, k_rest = tiles(grad_key, 3)
    rest = jnp.where(lane < 2 * left, q_rest, pltpu.roll(k_rest, 2 * left, 1))
    rest = rest * cosine_rest + swapped(rest * sine_rest, lane, left)
    grad = jnp.concatenate(
        [
            q1 * cosine + q2 * sine,
            q2 * cosine - q1 * sine,
            k1 * cosine + k2 * sine,
            k2 * cosine - k1 * sine,
            rest,
        ],
        1,
    ).astype(BF16)
    here = pl.ds(pl.multiple_of(i * length, 16), length)
    all_ref[here, :] = jnp.concatenate([grad, grad_value], 1)
    natural = times_transposed(grad, order_ref[...])
    grad_ref[0, :, : 2 * part] = natural.astype(BF16)
    grad_ref[0, :, 2 * part :] = grad_value[:, :part]
    sums_ref[5:6, : 2 * part] += jnp.sum(natural, 0, keepdims=True)
    sums_ref[5:6, 2 * part : 3 * part] += jnp.sum(grad_value[:, :part].astype(F32), 0, keepdims=True)

    @pl.when(i == 1)
    def _():
        for copy in first_copies(pieces, place_ref, rows, w_ref, None, semaphores):
            copy.wait()
        share = times_transposed(all_ref[...], w_ref[...])
        for n, x_ref in enumerate((x0, x1)):
            here = share[n * length : (n + 1) * length]
            unit, _ = norm_parts(x_ref[...].astype(F32))
            sums_ref[0:1] += jnp.sum(here * unit, 0, keepdims=True)
            sums_ref[1:2] += jnp.sum(here, 0, keepdims=True)
            share_ref[n] = here.astype(BF16)


def ring_back(
    me, place, order, masks, table, total, middle, grad, x, vec, w_own, qkv, lse, ids, pieces, heads, size,
    first,
):
    length, width = x[0].shape
    part = heads * size
    core = 0 if first else 1
    by_block = lambda columns: pl.BlockSpec((length, columns), lambda i: (2 * i + core, 0))
    by_half = lambda columns: pl.BlockSpec((1, length, columns), lambda i: (i, 0, 0))
    return pl.pallas_call(
        lambda *refs: ring_back_kernel(heads, size, first, *refs),
        grid=(2,),
        in_specs=[
            SCALARS,
            SCALARS,
            fixed(order.shape),
            fixed(masks.shape),
            fixed(table.shape),
            by_half(width),
            pl.BlockSpec((1, 1, length, width), lambda i: (i, core, 0, 0)),
        ]
        + [fixed((length, width))] * 4
        + [
            fixed(vec.shape),
            fixed(w_own.shape),
            by_block(9 * LANES),
            by_block(LANES),
            pl.BlockSpec((1,) + ids.shape[1:], lambda i: (2 * i + core, 0, 0)),
        ]
        + [ANYWHERE] * len(pieces),
        out_specs=[fixed((length, width))] * first
        + [by_half(part), by_half(3 * part), fixed((2, length, width)), fixed((8, width))],
        out_shape=[far((length, width), F32)] * first
        + [
            far((2, length, part), BF16),
            far((2, length, 3 * part), BF16),
            like((2, length, width), BF16),
            like((8, width), F32),
        ],
        scratch_shapes=[
            pltpu.VMEM((width, 8 * LANES), BF16),
            pltpu.VMEM((length, width), F32),
            pltpu.VMEM((2 * length, 8 * LANES), BF16),
            pltpu.SemaphoreType.DMA((2, len(pieces))),
        ],
        compiler_params=params(),
        cost_estimate=cost(13),
    )(
        me, place, *kept_far([order, masks, table]), total,
        *kept_far([middle, grad[core], grad[2 + core], x[core], x[2 + core]]), vec,
        *kept_far([w_own, qkv, lse]), ids, *kept_far(pieces),
    )


def last_grad_kernel(
    me_ref, place_ref, normed_ref, mixed_ref, grad0_ref, grad1_ref, cols0_ref, cols1_ref, sums0_ref, sums1_ref,
    feed_ref, out_ref, top_ref, bottom_ref, line_ref, grad_ref, cols_ref, sums_ref,
):
    i = pl.program_id(0)
    width = normed_ref.shape[1]
    rows = width * pl.num_programs(0) // 8
    part = cols_ref.shape[1]

    @pl.when(i == 0)
    def _():
        length = grad0_ref.shape[1]
        for n in range(2):
            for core, grad_in, cols_in in ((0, grad0_ref, cols0_ref), (1, grad1_ref, cols1_ref)):
                here = slice((2 * n + core) * length, (2 * n + core + 1) * length)
                grad_ref[here] = grad_in[n]
                cols_ref[here] = cols_in[n]
        sums_ref[...] = sums0_ref[...] + sums1_ref[...]

    left = outer(normed_ref[...], grad_ref[...]).astype(BF16)
    right = outer(mixed_ref[...], cols_ref[...]).astype(BF16)
    value = jnp.concatenate([left, right], 1)
    for n in range(width // 32):
        at = i * width + 32 * n
        shard = lax.div(at, rows)
        row = pl.multiple_of(at - shard * rows, 32)
        out_ref[shard, pl.ds(row, 32)] = value[32 * n : 32 * n + 32]

    @pl.when(i == 0)
    def _():
        line_ref[...] = jnp.zeros_like(line_ref)
        for shard in range(8):
            here = slice(shard * rows, (shard + 1) * rows)
            for n in range(5):
                line_ref[shard, n : n + 1, :rows] = sums_ref[n : n + 1, here]
            line_ref[shard, 5:6, :rows] = feed_ref[1:2, here]
        for me in range(COPIES):

            @pl.when(me_ref[0] == me)
            def _():
                for shard in range(8):
                    line_ref[shard, 7:8, me * rows : (me + 1) * rows] = feed_ref[
                        0:1, shard * rows : (shard + 1) * rows
                    ]
                for n in range(3):
                    start = (n * COPIES + me) * part
                    for shard in range(8):
                        low = max(start, shard * 3 * rows)
                        high = min(start + part, (shard + 1) * 3 * rows)
                        if low < high:
                            line_ref[shard, 6:7, low - shard * 3 * rows : high - shard * 3 * rows] = (
                                sums_ref[5:6, n * part + low - start : n * part + high - start]
                            )

        for shard in range(8):
            out_ref[shard, rows:] = line_ref[shard].astype(BF16)

    @pl.when(i == pl.num_programs(0) - 1)
    def _():
        cut = top_ref.shape[0]
        top_ref[...] = out_ref[place_ref[7], :cut]
        bottom_ref[...] = out_ref[place_ref[7], cut:]


def last_grads(me, place, normed, mixed, grads, cols, sums, feed_sums):
    tokens, width = normed.shape
    block = 256
    rows = width // 8
    by_columns = pl.BlockSpec((tokens, block), lambda i: (0, i))
    parts, part = grads[0].shape[2], cols[0].shape[2]
    shape = (8, rows + EXTRA, parts + part)
    cut = half_of(shape[1])
    return pl.pallas_call(
        last_grad_kernel,
        grid=(width // block,),
        in_specs=[
            SCALARS,
            SCALARS,
            by_columns,
            by_columns,
            *[fixed(a.shape) for a in (*grads, *cols, *sums, feed_sums)],
        ],
        out_specs=[fixed(shape), fixed((cut, shape[2])), fixed((shape[1] - cut, shape[2]))],
        out_shape=[
            like(shape, BF16),
            like((cut, shape[2]), BF16),
            like((shape[1] - cut, shape[2]), BF16),
        ],
        scratch_shapes=[
            pltpu.VMEM((8, EXTRA, shape[2]), F32),
            pltpu.VMEM((tokens, parts), BF16),
            pltpu.VMEM((tokens, part), BF16),
            pltpu.VMEM(sums[0].shape, F32),
        ],
        compiler_params=params(),
        cost_estimate=cost(10),
    )(me, place, *kept_far([normed, mixed, *grads, *cols]), *sums, feed_sums)


def output_kernel(middle_ref, pair_ref, far_ref, vec_ref, out_ref):
    out_ref[...] = (
        middle_ref[0, 0] + pair_ref[0].astype(F32) + far_ref[...].astype(F32) + vec_ref[5:6]
    ).astype(BF16)


def output_of(middle, pair, far, vec):
    length, width = far.shape
    return pl.pallas_call(
        output_kernel,
        grid=(1,),
        in_specs=[
            fixed((1, 1, length, width)),
            fixed(pair.shape),
            fixed(far.shape),
            fixed(vec.shape),
        ],
        out_specs=fixed(far.shape),
        out_shape=like(far.shape, BF16),
        compiler_params=params(),
        cost_estimate=cost(),
    )(middle, pair, far, vec)


def last_norm_kernel(dx_ref, pair_ref, far_ref, x_ref, vec_ref, out_ref):
    grad_normed = pair_ref[0].astype(F32) + far_ref[...].astype(F32)
    unit, inverse = norm_parts(x_ref[...].astype(F32))
    out_ref[...] = (
        dx_ref[...] + norm_back(grad_normed, unit, inverse, vec_ref[0:1])
    ).astype(BF16)


def last_norm(dx, pair, far, x, vec):
    return pl.pallas_call(
        last_norm_kernel,
        in_specs=[WHOLE] * 5,
        out_specs=WHOLE,
        out_shape=like(x.shape, BF16),
        compiler_params=params(),
        cost_estimate=cost(),
    )(dx, pair, far, x, vec)


def spread_kernel(me_ref, s0, s1, s2, s3, whole_up_ref, whole_down_ref):
    slots = (s0, s1, s2, s3)
    rows = whole_up_ref.shape[0]
    step = s0.shape[0] - rows
    size = s0.shape[1] // 8
    for me in range(COPIES):

        @pl.when(me_ref[0] == me)
        def _():
            for n in range(COPIES):
                whole_down_ref[n * step : (n + 1) * step] = slots[me ^ n][rows:].astype(F32)
            for group in range(8):
                at = group * size * COPIES
                whole_up_ref[:, at : at + size * COPIES] = jnp.concatenate(
                    [
                        slots[me ^ n][:rows, group * size : (group + 1) * size]
                        for n in range(COPIES)
                    ],
                    1,
                ).astype(F32)


def spread(me, slots, rows):
    lines, width = slots[0].shape
    return pl.pallas_call(
        spread_kernel,
        in_specs=[SCALARS] + [WHOLE] * COPIES,
        out_specs=[WHOLE] * 2,
        out_shape=[
            like((rows, COPIES * width), F32),
            like((COPIES * (lines - rows), width), F32),
        ],
        compiler_params=params(),
        cost_estimate=cost(),
    )(me, *slots)


def finish_kernel(part, me_ref, s0, s1, s2, s3, whole_qkv_ref, whole_out_ref, *sum_refs):
    slots = (s0, s1, s2, s3)
    rows = whole_qkv_ref.shape[0]
    for me in range(COPIES):

        @pl.when(me_ref[0] == me)
        def _():
            for n in range(3):
                whole_qkv_ref[:, n * COPIES * part : (n + 1) * COPIES * part] = jnp.concatenate(
                    [slots[me ^ m][:rows, n * part : (n + 1) * part] for m in range(COPIES)], 1
                ).astype(F32)
            whole_out_ref[...] = jnp.concatenate(
                [slots[me ^ m][:rows, 3 * part :] for m in range(COPIES)], 1
            ).astype(F32)
            sums = sum(slots[me ^ m][rows:].astype(F32) for m in range(COPIES))
            for n, ref in enumerate(sum_refs):
                ref[...] = sums[n, : ref.shape[0]]


def finish(me, slots, part, vectors):
    lines, width = slots[0].shape
    rows = lines - EXTRA
    return pl.pallas_call(
        lambda *refs: finish_kernel(part, *refs),
        in_specs=[SCALARS] + [WHOLE] * COPIES,
        out_specs=[WHOLE] * (2 + len(vectors)),
        out_shape=[like((rows, 3 * COPIES * part), F32), like((rows, COPIES * part), F32)]
        + [like(shape, F32) for shape in vectors],
        compiler_params=params(),
        cost_estimate=cost(),
    )(me, *slots)


def add_low(one, other):
    return (one.astype(F32) + other.astype(F32)).astype(BF16)


def slot_pairs(kept, sent):
    return (kept.astype(F32) + to_core(sent).astype(F32)).astype(BF16)


def on_eight(
    hidden_in,
    seg_ids,
    patch_rows,
    patch_cols,
    ln1_scale,
    ln1_shift,
    qkv_weight,
    qkv_bias,
    out_weight,
    out_bias,
    ln2_scale,
    ln2_shift,
    up_weight,
    up_bias,
    down_weight,
    down_bias,
    cotangent,
):
    me = lax.axis_index("rep")
    me_list = me.reshape(1).astype(jnp.int32)
    length, width = hidden_in.shape
    rows = ln1_scale.shape[0]
    size = width // HEADS
    heads = HEADS // COPIES
    part = heads * size
    hidden = up_weight.shape[1] // COPIES
    slots = ring_slots()
    vectors = (
        ln1_scale, ln1_shift, out_bias, ln2_scale, ln2_shift, down_bias, qkv_bias, up_bias,
    )

    order, masks = column_order(heads, size), head_masks(heads, size)
    table = rotary_table(heads, size)
    first = first_piece(me_list, order, qkv_weight, out_weight, vectors, part)
    ids, own_x, first = tie((jnp.concatenate([seg_ids, patch_rows, patch_cols]), hidden_in, first))
    ids = gather_rep(ids)
    own_x, ids[2] = tie((own_x, ids[2]))
    x = gather_rep(own_x)
    own_feed = second_piece(me_list, up_weight, down_weight, 8)
    x[2], own_grad = tie((x[2], cotangent))
    grad = gather_rep(own_grad)
    qkv_pieces = ring_gather(
        first, (), {1: x[2:3], 2: [own_feed, slots], 3: x[3:] + ids[1:] + grad[2:3]}
    )
    ids = jnp.stack(ids)
    out_pieces = gather_rep(collect(qkv_pieces, rows, part))

    normed_one, qkv, lse, mixed, vec = ring_attend(
        me_list, slots, order, masks, table, x, ids, qkv_pieces, heads, size
    )
    mixed_all, middle, normed_two, w_own = middle_of(
        me_list, slots, gather_rep(mixed), vec, x, out_pieces, rows
    )
    feed_weights = ring_gather(
        own_feed, qkv_pieces[5:7], {0: [mixed, out_pieces[2]], 2: [normed_two]}
    )
    act, low, sent, kept, feed_sums = feed(
        slots, normed_two, grad, vec, feed_weights, hidden
    )

    arrived = to_core(sent)
    act, arrived = tie((act, arrived))
    chip_own, chip_far = (add_low(kept[n], arrived[n]) for n in range(2))
    far_one, far_two = to_x(chip_far), to_x(chip_own)

    tokens = COPIES * length
    feed_grad, feed_right, feed_left = feed_grads(
        slots, normed_two.reshape(tokens, width), act.reshape(tokens, hidden), low.reshape(tokens, hidden), grad
    )
    far_one, feed_grad, feed_right, feed_left = tie((far_one, feed_grad, feed_right, feed_left))

    (late,) = tie([act], [far_one])
    sent, kept = down_of(slots, late, feed_weights, width)
    made = {}

    def back(name, values, core):
        made[name] = ring_back(
            me_list, slots, order, masks, table, values, middle, grad, x, vec, w_own, qkv, lse, ids,
            qkv_pieces, heads, size, core == 0,
        )
        return made[name]

    def first_hop(_):
        made["far_two"], made["sent"], made["kept"] = tie((far_two, sent, kept))
        return [made["far_two"], made["sent"], made["kept"]]

    def second_hop(moved):
        own, other, _ = tie((far_one, made["far_two"], moved))
        made["total"] = jnp.stack([add_low(chip_own, own), add_low(chip_far, other)])
        made["out_pair"] = slot_pairs(made["kept"], made["sent"])
        return [back("own", made["total"], 0)[2], made["out_pair"]]

    def third_hop(_):
        made["out_far"] = to_x(made["out_pair"][1])
        return [back("near", to_core(made["total"]), 1)[1], made["out_far"]]

    def fourth_hop(_):
        grad_middle, cols, grad_qkv, _, sums = made["own"]
        near_cols, near_qkv, _, near_sums = made["near"]
        made["last"] = last_grads(
            me_list, slots, normed_one, mixed_all, (grad_qkv, near_qkv), (cols, near_cols),
            (sums, near_sums), feed_sums,
        )
        return [made["last"][0]]

    feed_grad = ring_scatter(
        feed_grad, feed_right, feed_left, slots, dict(enumerate((first_hop, second_hop, third_hop, fourth_hop))),
        [far_one], 4,
    )
    feed_slots = gather_rep(feed_grad)
    whole_up, whole_down = spread(me_list, feed_slots, rows)
    output = output_of(middle, made["out_pair"], made["out_far"], vec)

    pair = slot_pairs(made["own"][3], made["near"][2])
    far_pair = to_x(pair[1])
    grad_inputs = last_norm(made["own"][0], pair, far_pair, hidden_in, vec)
    last = ring_scatter(
        *made["last"],
        slots,
        {0: [pair], 1: [feed_grad, far_pair], 2: [output], 3: [feed_slots[2], grad_inputs]},
    )
    last_far, whole_up, whole_down = tie((to_x(last), whole_up, whole_down))
    last_slots = [last, to_core(last), last_far, to_core(last_far)]
    whole_qkv, whole_out, *totals = finish(
        me_list, last_slots, part, [vector.shape for vector in vectors]
    )
    return (
        output,
        grad_inputs,
        totals[0],
        totals[1],
        whole_qkv,
        totals[6],
        whole_out,
        totals[2],
        totals[3],
        totals[4],
        whole_up,
        totals[7],
        whole_down,
        totals[5],
    )


def solution(mesh):
    shards = mesh.shape["shard"]
    tokens, vector, matrix = P(("rep", "shard"), None), P("shard"), P("shard", None)
    in_specs = (
        (tokens,) * 4
        + (vector, vector, matrix, vector, matrix, vector)
        + (vector, vector, matrix, vector, matrix, vector)
        + (tokens,)
    )
    out_specs = (
        (tokens, tokens)
        + (vector, vector, matrix, vector, matrix, vector)
        + (vector, vector, matrix, vector, matrix, vector)
    )
    return jax.shard_map(
        on_eight if shards == 8 else lambda *args: on_any(shards, *args),
        mesh=mesh,
        in_specs=in_specs,
        out_specs=out_specs,
        check_vma=False,
    )
```

```python
import jax
import jax.numpy as jnp
import numpy as np
from jax import lax
from jax.experimental import pallas as pl
from jax.experimental.pallas import tpu as pltpu
from jax.sharding import PartitionSpec as P

HEADS = 16
EPSILON = 1e-06
GELU_SLOPE = 1.702
LANES = 128
MASKED = -1e30
COPIES = 4
EXTRA = 16
GRID = 32

CORE_PAIRS = [(0, 1), (1, 0), (2, 3), (3, 2)]
X_PAIRS = [(0, 2), (2, 0), (1, 3), (3, 1)]
RING = (0, 2, 4, 6, 7, 5, 3, 1)
RING_AT = tuple(RING.index(i) for i in range(8))
RIGHT = [(RING[i], RING[(i + 1) % 8]) for i in range(8)]
LEFT = [(RING[i], RING[(i - 1) % 8]) for i in range(8)]
OFFSETS = (0, -1, 1, -2, 2, -3, 3, 4, 4)

F32 = jnp.float32
BF16 = jnp.bfloat16
VMEM_LIMIT = 32 * 1024 * 1024


def norm_parts(values):
    center = values - jnp.mean(values, -1, keepdims=True)
    inverse = lax.rsqrt(jnp.mean(center * center, -1, keepdims=True) + EPSILON)
    return (center * inverse, inverse)


def norm_back(grad_normed, unit, inverse, scale):
    scaled = grad_normed * scale
    return inverse * (
        scaled
        - jnp.mean(scaled, -1, keepdims=True)
        - unit * jnp.mean(scaled * unit, -1, keepdims=True)
    )


def outer(left, right):
    return lax.dot_general(left, right, (((0,), (0,)), ((), ())), preferred_element_type=F32)


def times_transposed(left, right):
    return lax.dot_general(left, right, (((1,), (1,)), ((), ())), preferred_element_type=F32)


def times(left, right):
    return jnp.dot(left, right, preferred_element_type=F32)


def tie(values, after=()):
    values, after = tuple(values), tuple(after)
    return lax.optimization_barrier(values + after)[: len(values)]


def to_core(value):
    return lax.ppermute(value, "rep", CORE_PAIRS)


def to_x(value):
    return lax.ppermute(value, "rep", X_PAIRS)


def gather_rep(value):
    near, far = to_core(value), to_x(value)
    return [value, near, far, to_core(far)]


def reduce_pair(parts):
    low = parts.astype(BF16)
    arrived = to_core(jnp.stack([low[1], low[3]]))
    return (jnp.stack([low[0], low[2]]).astype(F32) + arrived.astype(F32)).astype(BF16)


def scatter_rep(parts):
    pair = reduce_pair(parts)
    return pair[0].astype(F32) + to_x(pair[1]).astype(F32)


def sum_rep(parts):
    pair = reduce_pair(parts)
    arrived = to_x(pair)
    total = (pair.astype(F32) + arrived[::-1].astype(F32)).astype(BF16)
    near = to_core(total)
    return jnp.stack([total[0], near[0], total[1], near[1]])


def by_owner(slots, me):
    core, far = me % 2 == 1, me // 2 == 1
    a, b, c, d = slots
    a, b, c, d = (
        jnp.where(core, b, a),
        jnp.where(core, a, b),
        jnp.where(core, d, c),
        jnp.where(core, c, d),
    )
    return [jnp.where(far, c, a), jnp.where(far, d, b), jnp.where(far, a, c), jnp.where(far, b, d)]


def gather_shards(pieces, shards):
    return [lax.all_gather(piece, "shard", axis=0) for piece in pieces]


def scatter_shards(whole, shards, rights):
    return lax.psum_scatter(whole, "shard", scatter_dimension=0, tiled=False)


def window(values, start, size):
    part = values[:, start : start + size]
    return jnp.concatenate([part, jnp.zeros((part.shape[0], LANES - size), part.dtype)], 1)


def turned(values, half, lane):
    return jnp.where(
        lane < half,
        pltpu.roll(values, LANES - half, 1),
        pltpu.roll(values, half, 1),
    )


def attend_kernel(
    heads, size, x_ref, gain_ref, shift_ref, w_ref, bias_ref, cos_ref, sin_ref, row_ref, col_ref,
    normed_ref, qkv_ref, lse_ref, out_ref,
):
    unit, _ = norm_parts(x_ref[...].astype(F32))
    normed = (unit * gain_ref[...] + shift_ref[...]).astype(BF16)
    normed_ref[...] = normed
    projected = times(normed, w_ref[...]) + bias_ref[...]
    cosine, sine = cos_ref[...], sin_ref[...]
    rows = projected.shape[0]
    lane = lax.broadcasted_iota(jnp.int32, (rows, LANES), 1)
    same = col_ref[...] == row_ref[0]
    scale = size**-0.5
    half = size // 2
    outs = []
    lses = jnp.zeros((rows, LANES), F32)
    for head in range(heads):
        query, key, value = (
            window(projected, (part * heads + head) * size, size) for part in range(3)
        )
        query = (query * cosine + turned(query, half, lane) * sine).astype(BF16)
        key = (key * cosine + turned(key, half, lane) * sine).astype(BF16)
        value = value.astype(BF16)
        for part, kept in enumerate((query, key, value)):
            at = (part * heads + head) * LANES
            qkv_ref[:, at : at + LANES] = kept
        scores = jnp.where(same, times_transposed(query, key) * scale, MASKED)
        most = jnp.max(scores, -1, keepdims=True)
        expo = jnp.exp(scores - most)
        total = jnp.sum(expo, -1, keepdims=True)
        probs = (expo * (1.0 / total)).astype(BF16)
        outs.append(times(probs, value)[:, :size])
        lses = jnp.where(lane == head, most + jnp.log(total), lses)
    lse_ref[...] = lses
    out_ref[...] = jnp.concatenate(outs, 1).astype(BF16)


def attend(x, gain, shift, weight, bias, cosine, sine, seg_rows, seg_cols, heads, size):
    tokens, width = x.shape
    length = seg_rows.shape[-1]
    part = heads * size
    by_block = lambda columns: pl.BlockSpec((length, columns), lambda i: (i, 0))
    fixed = lambda array: pl.BlockSpec(array.shape, lambda i: (0,) * array.ndim)
    return pl.pallas_call(
        lambda *refs: attend_kernel(heads, size, *refs),
        grid=(tokens // length,),
        in_specs=[
            by_block(width),
            fixed(gain),
            fixed(shift),
            fixed(weight),
            fixed(bias),
            by_block(LANES),
            by_block(LANES),
            pl.BlockSpec((1, 1, length), lambda i: (i, 0, 0)),
            by_block(1),
        ],
        out_specs=[by_block(width), by_block(3 * heads * LANES), by_block(LANES), by_block(part)],
        out_shape=[
            jax.ShapeDtypeStruct((tokens, width), BF16),
            jax.ShapeDtypeStruct((tokens, 3 * heads * LANES), BF16),
            jax.ShapeDtypeStruct((tokens, LANES), F32),
            jax.ShapeDtypeStruct((tokens, part), BF16),
        ],
        compiler_params=pltpu.CompilerParams(vmem_limit_bytes=48 * 1024 * 1024),
        cost_estimate=pl.CostEstimate(
            flops=2 * tokens * width * 3 * part + 4 * tokens * length * part,
            bytes_accessed=4 * tokens * width + weight.size * 2 + tokens * 3 * heads * LANES * 2,
            transcendentals=tokens * length * heads,
        ),
    )(x, gain, shift, weight, bias, cosine, sine, seg_rows, seg_cols)


def attend_back_kernel(
    heads, size, db_ref, wo_ref, qkv_ref, lse_ref, cos_ref, sin_ref, row_ref, col_ref, w_ref,
    x_ref, grad_ref, dn_ref, sum_ref, gain_ref, shift_ref,
):
    mixed = times_transposed(db_ref[...], wo_ref[...])
    cosine, sine = cos_ref[...], sin_ref[...]
    rows = mixed.shape[0]
    lane = lax.broadcasted_iota(jnp.int32, (rows, LANES), 1)
    same = col_ref[...] == row_ref[0]
    scale = size**-0.5
    half = size // 2
    lses = lse_ref[...]
    grads = [None] * (3 * heads)
    for head in range(heads):
        query, key, value = (
            qkv_ref[:, (part * heads + head) * LANES : (part * heads + head + 1) * LANES]
            for part in range(3)
        )
        lse = jnp.sum(jnp.where(lane == head, lses, 0.0), -1, keepdims=True)
        scores = jnp.where(same, times_transposed(query, key) * scale, MASKED)
        probs = jnp.exp(scores - lse)
        grad_mixed = window(mixed, head * size, size).astype(BF16)
        grad_probs = times_transposed(grad_mixed, value)
        grad_value = outer(probs.astype(BF16), grad_mixed)
        inner = jnp.sum(probs * grad_probs, -1, keepdims=True)
        low = (probs * (grad_probs - inner)).astype(BF16)
        grad_query = times(low, key) * scale
        grad_key = outer(low, query) * scale
        grad_query = grad_query * cosine + turned(grad_query * sine, half, lane)
        grad_key = grad_key * cosine + turned(grad_key * sine, half, lane)
        grads[head] = grad_query[:, :size]
        grads[heads + head] = grad_key[:, :size]
        grads[2 * heads + head] = grad_value[:, :size]
    grad = jnp.concatenate(grads, 1).astype(BF16)
    grad_ref[...] = grad
    grad_normed = times_transposed(grad, w_ref[...])
    dn_ref[...] = grad_normed.astype(BF16)
    unit, _ = norm_parts(x_ref[...].astype(F32))

    @pl.when(pl.program_id(0) == 0)
    def _():
        sum_ref[...] = jnp.zeros_like(sum_ref)
        gain_ref[...] = jnp.zeros_like(gain_ref)
        shift_ref[...] = jnp.zeros_like(shift_ref)

    sum_ref[...] += jnp.sum(grad.astype(F32), 0, keepdims=True)
    gain_ref[...] += jnp.sum(grad_normed * unit, 0, keepdims=True)
    shift_ref[...] += jnp.sum(grad_normed, 0, keepdims=True)


def attend_back(db, w_out, qkv, lse, cosine, sine, seg_rows, seg_cols, weight, x, heads, size):
    tokens, width = x.shape
    length = seg_rows.shape[-1]
    part = heads * size
    by_block = lambda columns: pl.BlockSpec((length, columns), lambda i: (i, 0))
    fixed = lambda shape: pl.BlockSpec(shape, lambda i: (0,) * len(shape))
    return pl.pallas_call(
        lambda *refs: attend_back_kernel(heads, size, *refs),
        grid=(tokens // length,),
        in_specs=[
            by_block(width),
            fixed(w_out.shape),
            by_block(3 * heads * LANES),
            by_block(LANES),
            by_block(LANES),
            by_block(LANES),
            pl.BlockSpec((1, 1, length), lambda i: (i, 0, 0)),
            by_block(1),
            fixed(weight.shape),
            by_block(width),
        ],
        out_specs=[
            by_block(3 * part),
            by_block(width),
            fixed((1, 3 * part)),
            fixed((1, width)),
            fixed((1, width)),
        ],
        out_shape=[
            jax.ShapeDtypeStruct((tokens, 3 * part), BF16),
            jax.ShapeDtypeStruct((tokens, width), BF16),
            jax.ShapeDtypeStruct((1, 3 * part), F32),
            jax.ShapeDtypeStruct((1, width), F32),
            jax.ShapeDtypeStruct((1, width), F32),
        ],
        compiler_params=pltpu.CompilerParams(vmem_limit_bytes=48 * 1024 * 1024),
        cost_estimate=pl.CostEstimate(
            flops=2 * tokens * width * 4 * part + 10 * tokens * length * part,
            bytes_accessed=6 * tokens * width + weight.size * 2 + tokens * 3 * heads * LANES * 2,
            transcendentals=tokens * length * heads,
        ),
    )(db, w_out, qkv, lse, cosine, sine, seg_rows, seg_cols, weight, x)


def rotary(rows, columns, size):
    quarter = size // 4
    inverse = 10000.0 ** (-4.0 * jnp.arange(quarter, dtype=F32) / size)
    angles = jnp.concatenate(
        [rows.astype(F32)[:, None] * inverse, columns.astype(F32)[:, None] * inverse], -1
    )
    cosine, sine = jnp.cos(angles), jnp.sin(angles)
    nothing = jnp.zeros((rows.shape[0], LANES - size), F32)
    return (
        jnp.concatenate([cosine, cosine, nothing], -1),
        jnp.concatenate([-sine, sine, nothing], -1),
    )


def on_any(
    shards,
    hidden_in,
    seg_ids,
    patch_rows,
    patch_cols,
    ln1_scale,
    ln1_shift,
    qkv_weight,
    qkv_bias,
    out_weight,
    out_bias,
    ln2_scale,
    ln2_shift,
    up_weight,
    up_bias,
    down_weight,
    down_bias,
    cotangent,
):
    copies = 4
    me = lax.axis_index("rep")
    length, width = hidden_in.shape
    rows = ln1_scale.shape[0]
    size = width // HEADS
    heads = HEADS // copies
    part = heads * size
    hidden = up_weight.shape[1]
    own_hidden = hidden // copies
    step = hidden // shards // copies

    def own(array, axis):
        return lax.dynamic_index_in_dim(array, me, axis, False)

    own_qkv = own(qkv_weight.reshape(rows, 3, copies, part), 2).reshape(rows, 3 * part)
    own_up = own(up_weight.reshape(rows, shards, copies, step), 2).reshape(rows, own_hidden)
    own_down = own(down_weight.reshape(copies, step, width), 0)
    own_out = own(out_weight.reshape(copies, rows // copies, width), 0)
    vectors = (
        ln1_scale, ln1_shift, out_bias, ln2_scale, ln2_shift, down_bias, qkv_bias, up_bias,
    )
    small = jnp.concatenate(vectors)
    small_rows = 8
    small = jnp.pad(small, (0, small_rows * 3 * part - small.size)).reshape(small_rows, 3 * part)
    first, up_full, out_all, down_full = gather_shards(
        [
            jnp.concatenate([own_qkv, small]),
            own_up,
            own_out,
            own_down,
        ],
        shards,
    )
    w_qkv = first[:, :rows].reshape(width, 3 * part)
    small = first[:, rows:].reshape(shards, -1)
    up_full = up_full.reshape(width, own_hidden)
    down_full = down_full.reshape(own_hidden, width)
    full = []
    at = 0
    for vector in vectors:
        full.append(small[:, at : at + vector.size].astype(F32))
        at += vector.size
    gain_one, shift_one, out_offset, gain_two, shift_two, down_offset = (
        v.reshape(1, width) for v in full[:6]
    )
    qkv_offset = own(full[6].reshape(3, copies, part), 1).reshape(1, 3 * part)
    up_offset = own(full[7].reshape(shards, copies, step), 1).reshape(1, own_hidden)

    ids = jnp.concatenate([seg_ids, patch_rows, patch_cols])
    ids = jnp.stack(gather_rep(ids))
    seg_rows, seg_cols = ids[:, :1], ids[:, 0].reshape(-1, 1)
    x_low = jnp.concatenate(gather_rep(hidden_in))
    grad_out = jnp.concatenate(gather_rep(cotangent))
    tokens = x_low.shape[0]
    cosine, sine = rotary(ids[:, 1].reshape(-1), ids[:, 2].reshape(-1), size)

    normed_one, qkv, lse, mixed = attend(
        x_low, gain_one, shift_one, w_qkv, qkv_offset, cosine, sine, seg_rows, seg_cols, heads, size
    )
    out_full = jnp.stack(by_owner(gather_rep(out_all), me), 1).reshape(width, width)
    blocks = mixed.reshape(copies, length, part)
    near, far = to_core(blocks), to_x(blocks)
    both = to_core(far)
    mixed_slots = [
        mixed,
        near[jnp.array([1, 0, 3, 2])].reshape(tokens, part),
        far[jnp.array([2, 3, 0, 1])].reshape(tokens, part),
        both[jnp.array([3, 2, 1, 0])].reshape(tokens, part),
    ]
    mixed_full = jnp.concatenate(by_owner(mixed_slots, me), 1)

    middle = x_low.astype(F32) + times(mixed_full, out_full) + out_offset
    unit_two, inverse_two = norm_parts(middle)
    normed_two = (unit_two * gain_two + shift_two).astype(BF16)
    upward = times(normed_two, up_full) + up_offset
    sigma = jax.nn.sigmoid(GELU_SLOPE * upward)
    activated = (upward * sigma).astype(BF16)
    slope = sigma + GELU_SLOPE * upward * sigma * (1.0 - sigma)

    grad_down = outer(activated, grad_out).astype(BF16)
    grad_up_low = (times_transposed(grad_out, down_full) * slope).astype(BF16)
    grad_normed_two = sum_rep(times_transposed(grad_up_low, up_full).reshape(copies, length, width))
    grad_up = outer(normed_two, grad_up_low).astype(BF16)
    grad_up_bias = jnp.sum(grad_up_low.astype(F32), 0)
    branch = scatter_rep(times(activated, down_full).reshape(copies, length, width))
    output = middle[:length] + branch + down_offset

    grad_normed_two = grad_normed_two.reshape(tokens, width).astype(F32)
    grad_middle = grad_out.astype(F32) + norm_back(
        grad_normed_two, unit_two, inverse_two, gain_two
    )
    grad_branch = grad_middle.astype(BF16)
    grad_out_w = outer(mixed_full, own(grad_branch.reshape(tokens, copies, part), 1)).astype(BF16)

    own_w_out = lax.dynamic_slice_in_dim(out_full, me * part, part, 0)
    grad_qkv_low, grad_normed_one, sum_qkv, sum_gain, sum_shift = attend_back(
        grad_branch, own_w_out, qkv, lse, cosine, sine, seg_rows, seg_cols, w_qkv, x_low, heads, size
    )
    grad_qkv = outer(normed_one, grad_qkv_low).astype(BF16)
    grad_normed_one = scatter_rep(grad_normed_one.reshape(copies, length, width))
    unit_one, inverse_one = norm_parts(hidden_in.astype(F32))
    grad_inputs = grad_middle[:length] + norm_back(grad_normed_one, unit_one, inverse_one, gain_one)

    def sum_of(values):
        return jnp.sum(values[:length], 0).reshape(shards, rows)

    def placed(values, like, axis):
        return lax.dynamic_update_index_in_dim(jnp.zeros(like, F32), values, me, axis)

    sums = [
        sum_gain.reshape(shards, rows),
        sum_shift.reshape(shards, rows),
        sum_of(grad_branch.astype(F32)),
        sum_of(grad_normed_two * unit_two),
        sum_of(grad_normed_two),
        sum_of(grad_out.astype(F32)),
        placed(sum_qkv.reshape(3, part), (3, copies, part), 1).reshape(shards, -1),
        placed(grad_up_bias.reshape(shards, step), (shards, copies, step), 1).reshape(shards, -1),
    ]
    sums = jnp.concatenate(sums, 1)
    sums = jnp.pad(sums, ((0, 0), (0, small_rows * 3 * part - sums.shape[1])))
    last = jnp.concatenate(
        [grad_qkv.reshape(shards, rows, 3 * part), sums.astype(BF16).reshape(shards, small_rows, -1)],
        1,
    )

    done_down = scatter_shards(grad_down.reshape(shards, step, width), shards, 4)
    done_up = scatter_shards(grad_up.reshape(shards, rows, own_hidden), shards, 3)
    done_out = scatter_shards(grad_out_w.reshape(shards, rows, part), shards, 4)
    done_last = scatter_shards(last, shards, 4)

    whole_down = jnp.concatenate(by_owner(gather_rep(done_down), me), 0).astype(F32)
    whole_up = jnp.stack(
        [p.reshape(rows, shards, step) for p in by_owner(gather_rep(done_up), me)], 2
    )
    whole_up = whole_up.reshape(rows, hidden).astype(F32)
    whole_out = jnp.concatenate(by_owner(gather_rep(done_out), me), 1).astype(F32)
    last_slots = gather_rep(done_last)
    whole_qkv = jnp.stack(
        [p[:rows].reshape(rows, 3, part) for p in by_owner(last_slots, me)], 2
    )
    whole_qkv = whole_qkv.reshape(rows, 3 * width).astype(F32)
    summed = sum(p[rows:].astype(F32) for p in by_owner(last_slots, me)).reshape(-1)
    totals = []
    at = 0
    for vector in vectors:
        totals.append(summed[at : at + vector.size])
        at += vector.size
    return (
        output.astype(BF16),
        grad_inputs.astype(BF16),
        totals[0],
        totals[1],
        whole_qkv,
        totals[6],
        whole_out,
        totals[2],
        totals[3],
        totals[4],
        whole_up,
        totals[7],
        whole_down,
        totals[5],
    )


def ring_slots():
    position = jnp.asarray(RING_AT, jnp.int32)[lax.axis_index("shard")]
    return jnp.asarray(RING, jnp.int32)[(position + jnp.asarray(OFFSETS, jnp.int32)) % 8]


def half_of(rows):
    return (rows // 2 + 15) // 16 * 16


def ring_gather(piece, after=(), others=None):
    right = left = piece
    if after:
        right, left = tie((piece, piece), after)
    pieces = [piece]
    for hop in range(4):
        if hop == 3:
            cut = half_of(piece.shape[0])
            right, left = right[:cut], left[cut:]
        right, left = tie(
            (lax.ppermute(right, "shard", RIGHT), lax.ppermute(left, "shard", LEFT)),
            (others or {}).get(hop, ()),
        )
        pieces += [right, left]
    return pieces


def hop_kernel(first, _, ahead_ref, behind_ref, right_ref, left_ref, to_right_ref, to_left_ref):
    i = pl.program_id(0)

    def plus(out_ref, own_ref, other_ref):
        out_ref[...] = (own_ref[0].astype(F32) + other_ref[...].astype(F32)).astype(BF16)

    def copy(out_ref, own_ref):
        out_ref[...] = own_ref[0]

    if not first:
        plus(to_right_ref, ahead_ref, right_ref)
        plus(to_left_ref, behind_ref, left_ref)
        return

    @pl.when(i < pl.num_programs(0) // 2)
    def _():
        plus(to_right_ref, ahead_ref, right_ref)
        copy(to_left_ref, behind_ref)

    @pl.when(i >= pl.num_programs(0) // 2)
    def _():
        copy(to_right_ref, ahead_ref)
        plus(to_left_ref, behind_ref, left_ref)


def hop_sums(whole, slots, right, left, hop, steps):
    _, rows, width = whole.shape
    tile = rows // steps
    half = steps // 2
    first = hop == 0
    term = lambda n: pl.BlockSpec((1, tile, width), lambda i, s: (s[n], i, 0))
    block = lambda at: pl.BlockSpec((tile, width), lambda i, s: (at(i), 0))
    same = lambda i: i
    return pl.pallas_call(
        lambda *refs: hop_kernel(first, *refs),
        grid_spec=pltpu.PrefetchScalarGridSpec(
            num_scalar_prefetch=1,
            grid=(steps,),
            in_specs=[
                term(6 - 2 * hop),
                term(5 - 2 * hop),
                block((lambda i: jnp.minimum(i, half - 1)) if first else same),
                block((lambda i: jnp.maximum(i - half, 0)) if first else same),
            ],
            out_specs=[block(same), block(same)],
        ),
        out_shape=[like((rows, width), BF16)] * 2,
        compiler_params=params(),
        cost_estimate=cost(),
    )(slots, whole, whole, right, left)


def ring_scatter(whole, right, left, slots, others=None, after=(), steps=0):
    cut = right.shape[0]

    def own(number):
        return lax.dynamic_slice(
            whole, (slots[number], 0, 0), (1,) + whole.shape[1:], allow_negative_indices=False
        )[0]

    if after:
        right, left = tie((right, left), after)
    for hop in range(4):
        waited = (others or {}).get(hop, ())
        if callable(waited):
            waited = waited(right)
        right, left = tie(
            (lax.ppermute(right, "shard", RIGHT), lax.ppermute(left, "shard", LEFT)), waited
        )
        if hop == 3:
            break
        if steps:
            right, left = hop_sums(whole, slots, right, left, hop, steps)
            continue
        ahead, behind = own(6 - 2 * hop), own(5 - 2 * hop)
        if hop == 0:
            right = jnp.concatenate([add_low(right, ahead[:cut]), ahead[cut:]])
            left = jnp.concatenate([behind[:cut], add_low(left, behind[cut:])])
        else:
            right, left = add_low(right, ahead), add_low(left, behind)
    return (right.astype(F32) + left.astype(F32) + own(0).astype(F32)).astype(BF16)


def run_copies(copies):
    for copy in copies:
        copy.start()
    for copy in copies:
        copy.wait()


ANYWHERE = pl.BlockSpec(memory_space=pl.ANY)
SCALARS = pl.BlockSpec(memory_space=pltpu.SMEM)
WHOLE = pl.BlockSpec(memory_space=pltpu.VMEM)


def params():
    return pltpu.CompilerParams(vmem_limit_bytes=VMEM_LIMIT)


def fixed(shape):
    return pl.BlockSpec(shape, lambda i: (0,) * len(shape))


def cost(microseconds=0):
    return pl.CostEstimate(flops=1, bytes_accessed=1 + microseconds * 3_690_000, transcendentals=0)


def like(shape, dtype):
    return jax.ShapeDtypeStruct(shape, dtype)


def far(shape, dtype):
    return pltpu.HBM(shape, dtype)


def kept_far(arrays):
    return [pltpu.with_memory_space_constraint(a, pltpu.HBM) for a in arrays]


def joined(slots):
    return jnp.concatenate(slots, 0)


def column_order(heads, size):
    half = size // 2
    left = heads * half - LANES
    order = np.zeros((2 * heads * size, 2 * heads * size), np.float32)
    for part in range(2):
        for head in range(heads):
            for side in range(2):
                for feature in range(half):
                    natural = (part * heads + head) * size + side * half + feature
                    at = head * half + feature
                    group = 2 * part + side
                    to = group * LANES + at if at < LANES else (4 * LANES + group * left + at - LANES)
                    order[natural, to] = 1.0
    return jnp.asarray(order, BF16)


def head_masks(heads, size):
    half = size // 2
    left = heads * half - LANES
    masks = np.zeros((2 * heads, 3 * LANES), np.float32)
    for head in range(heads):
        for lane in range(2 * LANES):
            masks[head, lane] = (lane % LANES) // half == head
        for lane in range(2 * left):
            masks[head, 2 * LANES + lane] = (LANES + lane % left) // half == head
        masks[heads + head, head * size : (head + 1) * size] = 1.0
    return jnp.asarray(masks, F32)


def rotary_table(heads, size):
    half, quarter = size // 2, size // 4
    left = heads * half - LANES
    at = np.concatenate([np.arange(LANES), LANES + np.arange(4 * left) % left]) % half
    inverse = (10000.0 ** (-4.0 * np.arange(quarter, dtype=np.float32) / size)).astype(np.float32)
    angles = np.arange(GRID, dtype=np.float32)[:, None] * inverse[at % quarter]
    sign = np.ones(2 * LANES, np.float32)
    for group in (0, 2):
        sign[LANES + group * left : LANES + (group + 1) * left] = -1.0
    both = np.concatenate([np.cos(angles), np.sin(angles) * sign], 1)
    by_row = np.concatenate([at < quarter, at < quarter])
    return jnp.asarray(np.concatenate([np.where(by_row, both, 0.0), np.where(by_row, 0.0, both)]), F32)


def positions(ids, table):
    grid = lax.broadcasted_iota(jnp.int32, (GRID, ids.shape[1]), 0)
    picks = jnp.concatenate([grid == ids[1:2], grid == ids[2:3]], 0).astype(F32)
    both = lax.dot_general(
        picks, table, (((0,), (0,)), ((), ())), precision=lax.Precision.HIGHEST,
        preferred_element_type=F32,
    )
    image = (grid[:8] == ids[0:1]).astype(F32)
    return tiles(both, 4), outer(image, image) > 0.5


def first_kernel(part, *refs):
    me_ref, order_ref, weight_ref, other_ref = refs[:4]
    vectors, out_ref = refs[4:12], refs[12]
    rows, width = out_ref.shape[0] - EXTRA, out_ref.shape[1]
    for me in range(COPIES):

        @pl.when(me_ref[0] == me)
        def _():
            parts = [
                weight_ref[:, (n * COPIES + me) * part : (n * COPIES + me + 1) * part]
                for n in range(3)
            ]
            turned = times(jnp.concatenate(parts[:2], 1), order_ref[...]).astype(BF16)
            out_ref[:rows] = jnp.concatenate(
                [turned, parts[2], other_ref[:, me * part : (me + 1) * part]], 1
            )

    lines = [v[...].astype(F32).reshape(1, -1) for v in vectors]
    lines = [jnp.concatenate(lines[:6], 1), lines[6], lines[7]]
    lines = [
        jnp.concatenate([line, jnp.zeros((1, width - line.shape[1]), F32)], 1) for line in lines
    ]
    lines.append(jnp.zeros((EXTRA - len(lines), width), F32))
    out_ref[rows:] = jnp.concatenate(lines, 0).astype(BF16)


def first_piece(me, order, weight, other, vectors, part):
    rows = weight.shape[0]
    return pl.pallas_call(
        lambda *refs: first_kernel(part, *refs),
        in_specs=[SCALARS] + [WHOLE] * 11,
        out_specs=WHOLE,
        out_shape=like((rows + EXTRA, COPIES * part), BF16),
        compiler_params=params(),
        cost_estimate=cost(),
    )(me, *kept_far([order, weight, other, *vectors]))


def collect_kernel(rows, *refs):
    pieces, (out_ref, lines_ref, semaphores) = refs[:9], refs[9:]
    lanes = lines_ref.shape[2]
    part = out_ref.shape[1] // COPIES
    copies = []
    for number, ref in enumerate(pieces):
        edge = half_of(rows + EXTRA)
        start, count = (edge, rows - edge) if number == 8 else (0, edge if number == 7 else rows)
        copies.append(
            pltpu.make_async_copy(
                ref.at[pl.ds(0, count), pl.ds(ref.shape[1] - lanes, lanes)],
                lines_ref.at[min(number, 7), pl.ds(start, count)],
                semaphores.at[number],
            )
        )
    run_copies(copies)
    for line in range(2):
        out_ref[line * rows : (line + 1) * rows] = jnp.concatenate(
            [lines_ref[2 * n + line][:, lanes - part :] for n in range(COPIES)], 1
        )


def collect(pieces, rows, part):
    lanes = -(-part // LANES) * LANES
    return pl.pallas_call(
        lambda *refs: collect_kernel(rows, *refs),
        in_specs=[ANYWHERE] * len(pieces),
        out_specs=WHOLE,
        out_shape=like((2 * rows, COPIES * part), BF16),
        scratch_shapes=[pltpu.VMEM((8, rows, lanes), BF16), pltpu.SemaphoreType.DMA((9,))],
        compiler_params=params(),
        cost_estimate=cost(),
    )(*kept_far(pieces))


def second_kernel(shards, me_ref, up_ref, down_ref, out_ref):
    rows, hidden = up_ref.shape
    step = hidden // shards // COPIES
    for me in range(COPIES):

        @pl.when(me_ref[0] == me)
        def _():
            out_ref[:rows] = jnp.concatenate(
                [
                    up_ref[:, (n * COPIES + me) * step : (n * COPIES + me + 1) * step]
                    for n in range(shards)
                ],
                1,
            )
            out_ref[rows:] = down_ref[me * step : (me + 1) * step]


def second_piece(me, up, down, shards):
    rows, hidden = up.shape
    step = hidden // shards // COPIES
    return pl.pallas_call(
        lambda *refs: second_kernel(shards, *refs),
        in_specs=[SCALARS] + [WHOLE] * 2,
        out_specs=WHOLE,
        out_shape=like((rows + step, hidden // COPIES), BF16),
        compiler_params=params(),
        cost_estimate=cost(),
    )(me, *kept_far([up, down]))


def first_copies(refs, place, rows, w_ref, small_ref, semaphores):
    cut = half_of(rows + EXTRA)
    copies = []
    for number, ref in enumerate(refs):
        slot = place[number]
        start, count = (cut, rows - cut) if number == 8 else (0, cut if number == 7 else rows)
        at = pl.multiple_of(slot * rows + start, 16)
        copies.append(
            pltpu.make_async_copy(
                ref.at[pl.ds(0, count), pl.ds(0, w_ref.shape[1])],
                w_ref.at[pl.ds(at, count)],
                semaphores.at[0, number],
            )
        )
        if number != 7 and small_ref is not None:
            copies.append(
                pltpu.make_async_copy(
                    ref.at[pl.ds(count, EXTRA)], small_ref.at[slot], semaphores.at[1, number]
                )
            )
    return copies


def vectors_of(me_ref, small_ref, order_ref, vec_ref, bias_ref, full_ref):
    shards = small_ref.shape[0]
    width = vec_ref.shape[1]
    rows = width // shards
    part = width // COPIES
    lines = [small_ref[s].astype(F32) for s in range(shards)]
    for n in range(6):
        vec_ref[n : n + 1] = jnp.concatenate(
            [line[0:1, n * rows : (n + 1) * rows] for line in lines], 1
        )
    full_ref[...] = jnp.concatenate([line[1:2, : 3 * rows] for line in lines], 1)
    vec_ref[7:8] = jnp.zeros((1, width), F32)
    bias_ref[...] = jnp.zeros_like(bias_ref)
    for me in range(COPIES):

        @pl.when(me_ref[0] == me)
        def _():
            vec_ref[6:7] = jnp.concatenate(
                [line[2:3, me * rows : (me + 1) * rows] for line in lines], 1
            )
            parts = [
                full_ref[:, (n * COPIES + me) * part : (n * COPIES + me + 1) * part] for n in range(3)
            ]
            both = jnp.broadcast_to(jnp.concatenate(parts[:2], 1), (8, 2 * part)).astype(BF16)
            bias_ref[:, : 2 * part] = times(both, order_ref[...])[:1]
            bias_ref[:, 2 * part : 3 * part] = parts[2]


def swapped(values, lane, left):
    return jnp.where(
        lane // left % 2 == 0,
        pltpu.roll(values, LANES - left, 1),
        pltpu.roll(values, left, 1),
    )


def tiles(values, count):
    return [values[:, n * LANES : (n + 1) * LANES] for n in range(count)]


def ring_attend_kernel(heads, size, *refs):
    (
        me_ref, place_ref, order_ref, mask_ref, table_ref, x0, x1, x2, x3, ids_ref,
    ), refs = refs[:10], refs[10:]
    pieces, refs = refs[:9], refs[9:]
    (
        normed_ref, qkv_ref, lse_ref, out_ref, vec_ref, w_ref, small_ref, bias_ref, full_ref, all_ref,
        project_ref, semaphores,
    ) = refs
    i = pl.program_id(0)
    length, width = x0.shape
    rows = width // 8
    part = heads * size

    @pl.when(i == 0)
    def _():
        copies = first_copies(pieces, place_ref, rows, w_ref, small_ref, semaphores)
        for copy in copies:
            copy.start()
        for copy in copies[1:14:2] + copies[-1:]:
            copy.wait()
        vectors_of(me_ref, small_ref, order_ref, vec_ref, bias_ref, full_ref)
        for slot, x_ref in enumerate((x0, x1, x2, x3)):
            unit, _ = norm_parts(x_ref[...].astype(F32))
            all_ref[slot * length : (slot + 1) * length] = (
                unit * vec_ref[0:1] + vec_ref[1:2]
            ).astype(BF16)
        for copy in copies[0:14:2] + copies[14:16]:
            copy.wait()
        project_ref[...] = times(all_ref[...], w_ref[...]) + bias_ref[...]

    here = pl.ds(pl.multiple_of(i * length, 16), length)
    normed_ref[...] = all_ref[here, :]
    q1, q2, k1, k2, rest = tiles(project_ref[here, : 5 * LANES], 5)
    value = project_ref[here, 5 * LANES :]
    lane = lax.broadcasted_iota(jnp.int32, (length, LANES), 1)
    wide = lax.broadcasted_iota(jnp.int32, (length, 3 * LANES), 1)
    (cosine, cosine_rest, sine, sine_rest), same = positions(ids_ref[0], table_ref[...])
    left = heads * size // 2 - LANES
    rest = rest * cosine_rest + swapped(rest, lane, left) * sine_rest
    query = jnp.concatenate(
        [q1 * cosine - q2 * sine, q2 * cosine + q1 * sine, jnp.where(lane < 2 * left, rest, 0.0)], 1
    ).astype(BF16)
    key = jnp.concatenate(
        [
            k1 * cosine - k2 * sine,
            k2 * cosine + k1 * sine,
            jnp.where(lane < 2 * left, pltpu.roll(rest, 2 * left, 1), 0.0),
        ],
        1,
    ).astype(BF16)
    value = jnp.where(wide < part, value, 0.0).astype(BF16)
    qkv_ref[...] = jnp.concatenate([query, key, value], 1)
    masks = mask_ref[...].astype(BF16)
    scale = size**-0.5
    all_probs, all_values = [], []
    lses = jnp.zeros((length, LANES), F32)
    for head in range(heads):
        scores = times_transposed(query * masks[head : head + 1], key)
        scores = jnp.where(same, scores * scale, MASKED)
        most = jnp.max(scores, -1, keepdims=True)
        expo = jnp.exp(scores - most)
        total = jnp.sum(expo, -1, keepdims=True)
        all_probs.append((expo * (1.0 / total)).astype(BF16))
        all_values.append(value * masks[heads + head : heads + head + 1])
        lses = jnp.where(lane == head, most + jnp.log(total), lses)
    lse_ref[...] = lses
    out = times(jnp.concatenate(all_probs, 1), joined(all_values))[:, :part].astype(BF16)
    count = out_ref.shape[1]
    out_ref[0] = jnp.concatenate([out[n * count : (n + 1) * count] for n in range(COPIES)], 1)


def ring_attend(me, place, order, masks, table, x, ids, pieces, heads, size):
    length, width = x[0].shape
    tokens = COPIES * length
    by_block = lambda columns: pl.BlockSpec((length, columns), lambda i: (i, 0))
    return pl.pallas_call(
        lambda *refs: ring_attend_kernel(heads, size, *refs),
        grid=(COPIES,),
        in_specs=[SCALARS, SCALARS, fixed(order.shape), fixed(masks.shape), fixed(table.shape)]
        + [fixed((length, width))] * COPIES
        + [pl.BlockSpec((1,) + ids.shape[1:], lambda i: (i, 0, 0))]
        + [ANYWHERE] * len(pieces),
        out_specs=[
            by_block(width),
            by_block(9 * LANES),
            by_block(LANES),
            pl.BlockSpec((1, length // COPIES, width), lambda i: (i, 0, 0)),
            fixed((8, width)),
        ],
        out_shape=[
            far((tokens, width), BF16),
            far((tokens, 9 * LANES), BF16),
            far((tokens, LANES), F32),
            like((COPIES, length // COPIES, width), BF16),
            like((8, width), F32),
        ],
        scratch_shapes=[
            pltpu.VMEM((width, 8 * LANES), BF16),
            pltpu.VMEM((8, EXTRA, width), BF16),
            pltpu.VMEM((1, 8 * LANES), F32),
            pltpu.VMEM((1, 3 * width), F32),
            pltpu.VMEM((tokens, width), BF16),
            pltpu.VMEM((tokens, 8 * LANES), F32),
            pltpu.SemaphoreType.DMA((2, len(pieces))),
        ],
        compiler_params=params(),
        cost_estimate=cost(25),
    )(
        me, place, *kept_far([order, masks, table, *x]), ids, *kept_far(pieces)
    )


def middle_kernel(rows, part, *refs):
    me_ref, place_ref, own_ref, near_ref, far_ref, both_ref, vec_ref, x0, x1, x2, x3 = refs[:11]
    weights, (all_ref, middle_ref, normed_ref, wown_ref, w_ref, x_ref) = (
        refs[11:15],
        refs[15:],
    )
    j = pl.program_id(0)

    @pl.when(j == 0)
    def _():
        me = me_ref[0]
        for own in range(COPIES):

            @pl.when(me == own)
            def _():
                for n in range(8):
                    here = slice(n % 2 * rows, (n % 2 + 1) * rows)
                    lanes = slice(n // 2 * part, (n // 2 + 1) * part)
                    at = pl.multiple_of(place_ref[n] * rows, 16)
                    w_ref[pl.ds(at, rows), :] = jnp.concatenate(
                        [weights[own ^ b][here, lanes] for b in range(COPIES)], 1
                    )

        wown_ref[...] = w_ref[pl.ds(pl.multiple_of(me * part, 16), part), :]
        x_ref[...] = joined([x0[...], x1[...]])

    @pl.when(j == 1)
    def _():
        x_ref[...] = joined([x2[...], x3[...]])

    def unpacked(ref, order):
        return joined(
            [ref[b, :, n * part : (n + 1) * part] for b in order for n in range(COPIES)]
        )

    slots = [
        unpacked(own_ref, (0, 1)),
        unpacked(near_ref, (1, 0)),
        unpacked(far_ref, (0, 1)),
        unpacked(both_ref, (1, 0)),
    ]
    for me in range(COPIES):

        @pl.when(me_ref[0] == me)
        def _():
            all_ref[...] = jnp.concatenate([slots[me ^ n] for n in range(COPIES)], 1)

    middle = x_ref[...].astype(F32) + times(all_ref[...], w_ref[...]) + vec_ref[2:3]
    unit, _ = norm_parts(middle)
    normed = (unit * vec_ref[3:4] + vec_ref[4:5]).astype(BF16)
    length = middle_ref.shape[2]
    for core in range(2):
        middle_ref[0, core] = middle[core * length : (core + 1) * length]
        normed_ref[0, core] = normed[core * length : (core + 1) * length]


def middle_of(me, place, mixed, vec, x, weights, rows):
    length, width = x[0].shape
    part = width // COPIES
    tokens = COPIES * length
    by_slots = lambda flip: pl.BlockSpec(
        (2,) + mixed[0].shape[1:], lambda j: ((1 - j) if flip else j, 0, 0)
    )
    by_half = pl.BlockSpec((1, 2, length, width), lambda j: (j, 0, 0, 0))
    return pl.pallas_call(
        lambda *refs: middle_kernel(rows, part, *refs),
        grid=(2,),
        in_specs=[SCALARS, SCALARS]
        + [by_slots(False), by_slots(False), by_slots(True), by_slots(True), fixed(vec.shape)]
        + [fixed((length, width))] * COPIES
        + [fixed(weights[0].shape)] * COPIES,
        out_specs=[
            pl.BlockSpec((2 * length, width), lambda j: (j, 0)),
            by_half,
            by_half,
            fixed((part, width)),
        ],
        out_shape=[
            far((tokens, width), BF16),
            far((2, 2, length, width), F32),
            far((2, 2, length, width), BF16),
            far((part, width), BF16),
        ],
        scratch_shapes=[
            pltpu.VMEM((width, width), BF16),
            pltpu.VMEM((2 * length, width), BF16),
        ],
        compiler_params=params(),
        cost_estimate=cost(13),
    )(me, place, *mixed, vec, *kept_far([*x, *weights]))


def split_copies(pieces, place, up_ref, down_ref, semaphores):
    copies = []
    for number, ref in enumerate(pieces):
        for line, target in enumerate((up_ref, down_ref)):
            if target is None or (number == 7 and line == 1) or (number == 8 and line == 0):
                continue
            count = target.shape[0] // 8
            copies.append(
                pltpu.make_async_copy(
                    ref.at[pl.ds(count if line == 1 and number < 7 else 0, count)],
                    target.at[pl.ds(pl.multiple_of(place[number] * count, 16), count)],
                    semaphores.at[line, number],
                )
            )
    return copies


def feed_kernel(place_ref, normed_ref, g0, g1, g2, g3, vec_ref, *refs):
    pieces, refs = refs[:9], refs[9:]
    act_ref, dh_ref, sent_ref, kept_ref, sum_ref, up_ref, down_ref, grad_ref, semaphores = refs
    j = pl.program_id(0)

    @pl.when(j == 0)
    def _():
        copies = split_copies(pieces, place_ref, up_ref, None, semaphores)
        later = split_copies(pieces, place_ref, None, down_ref, semaphores)
        for copy in copies + later:
            copy.start()
        for copy in copies:
            copy.wait()
        sum_ref[...] = jnp.zeros_like(sum_ref)
        sum_ref[1:2] = jnp.sum(g0[...].astype(F32), 0, keepdims=True)
        grad_ref[...] = joined([g1[...], g3[...]])

    @pl.when(j == 1)
    def _():
        grad_ref[...] = joined([g0[...], g2[...]])

    normed = joined([normed_ref[0, 0], normed_ref[1, 0]])
    upward = times(normed, up_ref[...]) + vec_ref[6:7]
    sigma = jax.nn.sigmoid(GELU_SLOPE * upward)
    act = (upward * sigma).astype(BF16)
    slope = sigma + GELU_SLOPE * upward * sigma * (1.0 - sigma)

    @pl.when(j == 0)
    def _():
        for copy in split_copies(pieces, place_ref, None, down_ref, semaphores):
            copy.wait()

    low = (times_transposed(grad_ref[...], down_ref[...]) * slope).astype(BF16)
    sum_ref[0:1] += jnp.sum(low.astype(F32), 0, keepdims=True)
    back = times_transposed(low, up_ref[...]).astype(BF16)
    length = normed_ref.shape[2]
    for half in range(2):
        here = slice(half * length, (half + 1) * length)
        act_ref[half, 0] = act[here]
        dh_ref[half, 0] = low[here]

    @pl.when(j == 0)
    def _():
        for half in range(2):
            sent_ref[half] = back[half * length : (half + 1) * length]

    @pl.when(j == 1)
    def _():
        for half in range(2):
            kept_ref[half] = back[half * length : (half + 1) * length]


def feed(place, normed, grad, vec, pieces, hidden):
    _, _, length, width = normed.shape
    by_core = lambda columns: pl.BlockSpec((2, 1, length, columns), lambda j: (0, 1 - j, 0, 0))
    pair = like((2, length, width), BF16)
    return pl.pallas_call(
        feed_kernel,
        grid=(2,),
        in_specs=[SCALARS, by_core(width)]
        + [fixed((length, width))] * COPIES
        + [fixed(vec.shape)]
        + [ANYWHERE] * len(pieces),
        out_specs=[
            by_core(hidden),
            by_core(hidden),
            fixed((2, length, width)),
            fixed((2, length, width)),
            fixed((8, hidden)),
        ],
        out_shape=[
            far((2, 2, length, hidden), BF16),
            far((2, 2, length, hidden), BF16),
            pair,
            pair,
            like((8, hidden), F32),
        ],
        scratch_shapes=[
            pltpu.VMEM((width, hidden), BF16),
            pltpu.VMEM((hidden, width), BF16),
            pltpu.VMEM((2 * length, width), BF16),
            pltpu.SemaphoreType.DMA((2, 9)),
        ],
        compiler_params=params(),
        cost_estimate=cost(20),
    )(place, *kept_far([normed, *grad]), vec, *kept_far(pieces))


def down_kernel(place_ref, act_ref, *refs):
    pieces, (sent_ref, kept_ref, down_ref, semaphores) = refs[:9], refs[9:]
    j = pl.program_id(0)

    @pl.when(j == 0)
    def _():
        run_copies(split_copies(pieces, place_ref, None, down_ref, semaphores))

    value = times(joined([act_ref[0, 0], act_ref[1, 0]]), down_ref[...]).astype(BF16)
    length = act_ref.shape[2]

    @pl.when(j == 0)
    def _():
        for half in range(2):
            sent_ref[half] = value[half * length : (half + 1) * length]

    @pl.when(j == 1)
    def _():
        for half in range(2):
            kept_ref[half] = value[half * length : (half + 1) * length]


def down_of(place, act, pieces, width):
    _, _, length, hidden = act.shape
    pair = like((2, length, width), BF16)
    return pl.pallas_call(
        down_kernel,
        grid=(2,),
        in_specs=[SCALARS, pl.BlockSpec((2, 1, length, hidden), lambda j: (0, 1 - j, 0, 0))]
        + [ANYWHERE] * len(pieces),
        out_specs=[fixed((2, length, width)), fixed((2, length, width))],
        out_shape=[pair, pair],
        scratch_shapes=[pltpu.VMEM((hidden, width), BF16), pltpu.SemaphoreType.DMA((2, 9))],
        compiler_params=params(),
        cost_estimate=cost(),
    )(place, *kept_far([act, *pieces]))


def feed_grad_kernel(place_ref, normed_ref, act_ref, dh_ref, g0, g1, g2, g3, out_ref, top_ref, bottom_ref):
    i = pl.program_id(0)
    half = pl.num_programs(0) // 2
    width = normed_ref.shape[1]
    rows = width * half // 8

    def put(value, start):
        first = lax.rem(i, half) * width
        for n in range(width // 32):
            at = first + 32 * n
            shard = lax.div(at, rows)
            row = pl.multiple_of(at - shard * rows + start, 32)
            out_ref[shard, pl.ds(row, 32)] = value[32 * n : 32 * n + 32]

    @pl.when(i < half)
    def _():
        put(outer(normed_ref[...], dh_ref[...]).astype(BF16), 0)

    @pl.when(i >= half)
    def _():
        grad = joined([g0[...], g1[...], g2[...], g3[...]])
        put(outer(act_ref[...], grad).astype(BF16), rows)

    @pl.when(i == pl.num_programs(0) - 1)
    def _():
        top_ref[...] = out_ref[place_ref[7], :rows]
        bottom_ref[...] = out_ref[place_ref[7], rows:]


def feed_grads(place, normed, act, dh, grad):
    tokens, width = normed.shape
    length = grad[0].shape[0]
    block = 256
    half = width // block
    return pl.pallas_call(
        feed_grad_kernel,
        grid=(2 * half,),
        in_specs=[
            SCALARS,
            pl.BlockSpec((tokens, block), lambda i: (0, jnp.minimum(i, half - 1))),
            pl.BlockSpec((tokens, block), lambda i: (0, jnp.maximum(i - half, 0))),
            fixed(dh.shape),
        ]
        + [fixed((length, width))] * COPIES,
        out_specs=[
            fixed((8, width // 4, width)),
            fixed((width // 8, width)),
            fixed((width // 8, width)),
        ],
        out_shape=[
            far((8, width // 4, width), BF16),
            like((width // 8, width), BF16),
            like((width // 8, width), BF16),
        ],
        compiler_params=params(),
        cost_estimate=cost(),
    )(place, *kept_far([normed, act, dh, *grad]))


def ring_back_kernel(heads, size, first, *refs):
    (
        me_ref, place_ref, order_ref, mask_ref, table_ref, total_ref, middle_ref, g0, g1, x0, x1, vec_ref,
        wo_ref, qkv_ref, lse_ref, ids_ref,
    ), refs = refs[:16], refs[16:]
    pieces, refs = refs[:9], refs[9:]
    dx_ref = refs[0] if first else None
    cols_ref, grad_ref, share_ref, sums_ref, w_ref, cot_ref, all_ref, semaphores = refs[first:]
    i = pl.program_id(0)
    length, width = x0.shape
    rows = width // 8
    part = heads * size

    @pl.when(i == 0)
    def _():
        for copy in first_copies(pieces, place_ref, rows, w_ref, None, semaphores):
            copy.start()
        sums_ref[...] = jnp.zeros_like(sums_ref)

    for n, grad_ref_in in enumerate((g0, g1)):

        @pl.when(i == n)
        def _():
            cot_ref[...] = grad_ref_in[...].astype(F32)

    grad_normed = total_ref[0].astype(F32)
    unit, inverse = norm_parts(middle_ref[0, 0])
    grad_middle = cot_ref[...] + norm_back(grad_normed, unit, inverse, vec_ref[3:4])
    branch = grad_middle.astype(BF16)

    if first:

        @pl.when(i == 0)
        def _():
            dx_ref[...] = grad_middle
            sums_ref[2:3] = jnp.sum(branch.astype(F32), 0, keepdims=True)
            sums_ref[3:4] = jnp.sum(grad_normed * unit, 0, keepdims=True)
            sums_ref[4:5] = jnp.sum(grad_normed, 0, keepdims=True)

    for me in range(COPIES):

        @pl.when(me_ref[0] == me)
        def _():
            cols_ref[0] = branch[:, me * part : (me + 1) * part]

    mixed = times_transposed(branch, wo_ref[...]).astype(BF16)
    mixed = jnp.concatenate([mixed, jnp.zeros((length, 3 * LANES - part), BF16)], 1)
    query, key, value = (qkv_ref[:, 3 * n * LANES : 3 * (n + 1) * LANES] for n in range(3))
    masks = mask_ref[...].astype(BF16)
    (cosine, cosine_rest, sine, sine_rest), same = positions(ids_ref[0], table_ref[...])
    scale = size**-0.5
    lses = lse_ref[...]
    all_probs, all_lows, queries, keys, mixes = [], [], [], [], []
    for head in range(heads):
        queries.append(query * masks[head : head + 1])
        keys.append(key * masks[head : head + 1])
        mixes.append(mixed * masks[heads + head : heads + head + 1])
        scores = jnp.where(same, times_transposed(queries[-1], key) * scale, MASKED)
        probs = jnp.exp(scores - lses[:, head : head + 1])
        grad_probs = times_transposed(mixes[-1], value)
        inner = jnp.sum(probs * grad_probs, -1, keepdims=True)
        all_probs.append(probs.astype(BF16))
        all_lows.append((probs * (grad_probs - inner)).astype(BF16))
    grad_query = times(jnp.concatenate(all_lows, 1), joined(keys)) * scale
    grad_key = outer(joined(all_lows), joined(queries)) * scale
    grad_value = outer(joined(all_probs), joined(mixes)).astype(BF16)
    lane = lax.broadcasted_iota(jnp.int32, (length, LANES), 1)
    left = heads * size // 2 - LANES
    q1, q2, q_rest = tiles(grad_query, 3)
    k1, k2, k_rest = tiles(grad_key, 3)
    rest = jnp.where(lane < 2 * left, q_rest, pltpu.roll(k_rest, 2 * left, 1))
    rest = rest * cosine_rest + swapped(rest * sine_rest, lane, left)
    grad = jnp.concatenate(
        [
            q1 * cosine + q2 * sine,
            q2 * cosine - q1 * sine,
            k1 * cosine + k2 * sine,
            k2 * cosine - k1 * sine,
            rest,
        ],
        1,
    ).astype(BF16)
    here = pl.ds(pl.multiple_of(i * length, 16), length)
    all_ref[here, :] = jnp.concatenate([grad, grad_value], 1)
    natural = times_transposed(grad, order_ref[...])
    grad_ref[0, :, : 2 * part] = natural.astype(BF16)
    grad_ref[0, :, 2 * part :] = grad_value[:, :part]
    sums_ref[5:6, : 2 * part] += jnp.sum(natural, 0, keepdims=True)
    sums_ref[5:6, 2 * part : 3 * part] += jnp.sum(grad_value[:, :part].astype(F32), 0, keepdims=True)

    @pl.when(i == 1)
    def _():
        for copy in first_copies(pieces, place_ref, rows, w_ref, None, semaphores):
            copy.wait()
        share = times_transposed(all_ref[...], w_ref[...])
        for n, x_ref in enumerate((x0, x1)):
            here = share[n * length : (n + 1) * length]
            unit, _ = norm_parts(x_ref[...].astype(F32))
            sums_ref[0:1] += jnp.sum(here * unit, 0, keepdims=True)
            sums_ref[1:2] += jnp.sum(here, 0, keepdims=True)
            share_ref[n] = here.astype(BF16)


def ring_back(
    me, place, order, masks, table, total, middle, grad, x, vec, w_own, qkv, lse, ids, pieces, heads, size,
    first,
):
    length, width = x[0].shape
    part = heads * size
    core = 0 if first else 1
    by_block = lambda columns: pl.BlockSpec((length, columns), lambda i: (2 * i + core, 0))
    by_half = lambda columns: pl.BlockSpec((1, length, columns), lambda i: (i, 0, 0))
    return pl.pallas_call(
        lambda *refs: ring_back_kernel(heads, size, first, *refs),
        grid=(2,),
        in_specs=[
            SCALARS,
            SCALARS,
            fixed(order.shape),
            fixed(masks.shape),
            fixed(table.shape),
            by_half(width),
            pl.BlockSpec((1, 1, length, width), lambda i: (i, core, 0, 0)),
        ]
        + [fixed((length, width))] * 4
        + [
            fixed(vec.shape),
            fixed(w_own.shape),
            by_block(9 * LANES),
            by_block(LANES),
            pl.BlockSpec((1,) + ids.shape[1:], lambda i: (2 * i + core, 0, 0)),
        ]
        + [ANYWHERE] * len(pieces),
        out_specs=[fixed((length, width))] * first
        + [by_half(part), by_half(3 * part), fixed((2, length, width)), fixed((8, width))],
        out_shape=[far((length, width), F32)] * first
        + [
            far((2, length, part), BF16),
            far((2, length, 3 * part), BF16),
            like((2, length, width), BF16),
            like((8, width), F32),
        ],
        scratch_shapes=[
            pltpu.VMEM((width, 8 * LANES), BF16),
            pltpu.VMEM((length, width), F32),
            pltpu.VMEM((2 * length, 8 * LANES), BF16),
            pltpu.SemaphoreType.DMA((2, len(pieces))),
        ],
        compiler_params=params(),
        cost_estimate=cost(13),
    )(
        me, place, *kept_far([order, masks, table]), total,
        *kept_far([middle, grad[core], grad[2 + core], x[core], x[2 + core]]), vec,
        *kept_far([w_own, qkv, lse]), ids, *kept_far(pieces),
    )


def last_grad_kernel(
    me_ref, place_ref, normed_ref, mixed_ref, grad0_ref, grad1_ref, cols0_ref, cols1_ref, sums0_ref, sums1_ref,
    feed_ref, out_ref, top_ref, bottom_ref, line_ref, grad_ref, cols_ref, sums_ref,
):
    i = pl.program_id(0)
    width = normed_ref.shape[1]
    rows = width * pl.num_programs(0) // 8
    part = cols_ref.shape[1]

    @pl.when(i == 0)
    def _():
        length = grad0_ref.shape[1]
        for n in range(2):
            for core, grad_in, cols_in in ((0, grad0_ref, cols0_ref), (1, grad1_ref, cols1_ref)):
                here = slice((2 * n + core) * length, (2 * n + core + 1) * length)
                grad_ref[here] = grad_in[n]
                cols_ref[here] = cols_in[n]
        sums_ref[...] = sums0_ref[...] + sums1_ref[...]

    left = outer(normed_ref[...], grad_ref[...]).astype(BF16)
    right = outer(mixed_ref[...], cols_ref[...]).astype(BF16)
    value = jnp.concatenate([left, right], 1)
    for n in range(width // 32):
        at = i * width + 32 * n
        shard = lax.div(at, rows)
        row = pl.multiple_of(at - shard * rows, 32)
        out_ref[shard, pl.ds(row, 32)] = value[32 * n : 32 * n + 32]

    @pl.when(i == 0)
    def _():
        line_ref[...] = jnp.zeros_like(line_ref)
        for shard in range(8):
            here = slice(shard * rows, (shard + 1) * rows)
            for n in range(5):
                line_ref[shard, n : n + 1, :rows] = sums_ref[n : n + 1, here]
            line_ref[shard, 5:6, :rows] = feed_ref[1:2, here]
        for me in range(COPIES):

            @pl.when(me_ref[0] == me)
            def _():
                for shard in range(8):
                    line_ref[shard, 7:8, me * rows : (me + 1) * rows] = feed_ref[
                        0:1, shard * rows : (shard + 1) * rows
                    ]
                for n in range(3):
                    start = (n * COPIES + me) * part
                    for shard in range(8):
                        low = max(start, shard * 3 * rows)
                        high = min(start + part, (shard + 1) * 3 * rows)
                        if low < high:
                            line_ref[shard, 6:7, low - shard * 3 * rows : high - shard * 3 * rows] = (
                                sums_ref[5:6, n * part + low - start : n * part + high - start]
                            )

        for shard in range(8):
            out_ref[shard, rows:] = line_ref[shard].astype(BF16)

    @pl.when(i == pl.num_programs(0) - 1)
    def _():
        cut = top_ref.shape[0]
        top_ref[...] = out_ref[place_ref[7], :cut]
        bottom_ref[...] = out_ref[place_ref[7], cut:]


def last_grads(me, place, normed, mixed, grads, cols, sums, feed_sums):
    tokens, width = normed.shape
    block = 256
    rows = width // 8
    by_columns = pl.BlockSpec((tokens, block), lambda i: (0, i))
    parts, part = grads[0].shape[2], cols[0].shape[2]
    shape = (8, rows + EXTRA, parts + part)
    cut = half_of(shape[1])
    return pl.pallas_call(
        last_grad_kernel,
        grid=(width // block,),
        in_specs=[
            SCALARS,
            SCALARS,
            by_columns,
            by_columns,
            *[fixed(a.shape) for a in (*grads, *cols, *sums, feed_sums)],
        ],
        out_specs=[fixed(shape), fixed((cut, shape[2])), fixed((shape[1] - cut, shape[2]))],
        out_shape=[
            like(shape, BF16),
            like((cut, shape[2]), BF16),
            like((shape[1] - cut, shape[2]), BF16),
        ],
        scratch_shapes=[
            pltpu.VMEM((8, EXTRA, shape[2]), F32),
            pltpu.VMEM((tokens, parts), BF16),
            pltpu.VMEM((tokens, part), BF16),
            pltpu.VMEM(sums[0].shape, F32),
        ],
        compiler_params=params(),
        cost_estimate=cost(10),
    )(me, place, *kept_far([normed, mixed, *grads, *cols]), *sums, feed_sums)


def output_kernel(middle_ref, pair_ref, far_ref, vec_ref, out_ref):
    out_ref[...] = (
        middle_ref[0, 0] + pair_ref[0].astype(F32) + far_ref[...].astype(F32) + vec_ref[5:6]
    ).astype(BF16)


def output_of(middle, pair, far, vec):
    length, width = far.shape
    return pl.pallas_call(
        output_kernel,
        grid=(1,),
        in_specs=[
            fixed((1, 1, length, width)),
            fixed(pair.shape),
            fixed(far.shape),
            fixed(vec.shape),
        ],
        out_specs=fixed(far.shape),
        out_shape=like(far.shape, BF16),
        compiler_params=params(),
        cost_estimate=cost(),
    )(middle, pair, far, vec)


def last_norm_kernel(dx_ref, pair_ref, far_ref, x_ref, vec_ref, out_ref):
    grad_normed = pair_ref[0].astype(F32) + far_ref[...].astype(F32)
    unit, inverse = norm_parts(x_ref[...].astype(F32))
    out_ref[...] = (
        dx_ref[...] + norm_back(grad_normed, unit, inverse, vec_ref[0:1])
    ).astype(BF16)


def last_norm(dx, pair, far, x, vec):
    return pl.pallas_call(
        last_norm_kernel,
        in_specs=[WHOLE] * 5,
        out_specs=WHOLE,
        out_shape=like(x.shape, BF16),
        compiler_params=params(),
        cost_estimate=cost(),
    )(dx, pair, far, x, vec)


def spread_kernel(me_ref, s0, s1, s2, s3, whole_up_ref, whole_down_ref):
    slots = (s0, s1, s2, s3)
    rows = whole_up_ref.shape[0]
    step = s0.shape[0] - rows
    size = s0.shape[1] // 8
    for me in range(COPIES):

        @pl.when(me_ref[0] == me)
        def _():
            for n in range(COPIES):
                whole_down_ref[n * step : (n + 1) * step] = slots[me ^ n][rows:].astype(F32)
            for group in range(8):
                at = group * size * COPIES
                whole_up_ref[:, at : at + size * COPIES] = jnp.concatenate(
                    [
                        slots[me ^ n][:rows, group * size : (group + 1) * size]
                        for n in range(COPIES)
                    ],
                    1,
                ).astype(F32)


def spread(me, slots, rows):
    lines, width = slots[0].shape
    return pl.pallas_call(
        spread_kernel,
        in_specs=[SCALARS] + [WHOLE] * COPIES,
        out_specs=[WHOLE] * 2,
        out_shape=[
            like((rows, COPIES * width), F32),
            like((COPIES * (lines - rows), width), F32),
        ],
        compiler_params=params(),
        cost_estimate=cost(),
    )(me, *slots)


def finish_kernel(part, me_ref, s0, s1, s2, s3, whole_qkv_ref, whole_out_ref, *sum_refs):
    slots = (s0, s1, s2, s3)
    rows = whole_qkv_ref.shape[0]
    for me in range(COPIES):

        @pl.when(me_ref[0] == me)
        def _():
            for n in range(3):
                whole_qkv_ref[:, n * COPIES * part : (n + 1) * COPIES * part] = jnp.concatenate(
                    [slots[me ^ m][:rows, n * part : (n + 1) * part] for m in range(COPIES)], 1
                ).astype(F32)
            whole_out_ref[...] = jnp.concatenate(
                [slots[me ^ m][:rows, 3 * part :] for m in range(COPIES)], 1
            ).astype(F32)
            sums = sum(slots[me ^ m][rows:].astype(F32) for m in range(COPIES))
            for n, ref in enumerate(sum_refs):
                ref[...] = sums[n, : ref.shape[0]]


def finish(me, slots, part, vectors):
    lines, width = slots[0].shape
    rows = lines - EXTRA
    return pl.pallas_call(
        lambda *refs: finish_kernel(part, *refs),
        in_specs=[SCALARS] + [WHOLE] * COPIES,
        out_specs=[WHOLE] * (2 + len(vectors)),
        out_shape=[like((rows, 3 * COPIES * part), F32), like((rows, COPIES * part), F32)]
        + [like(shape, F32) for shape in vectors],
        compiler_params=params(),
        cost_estimate=cost(),
    )(me, *slots)


def add_low(one, other):
    return (one.astype(F32) + other.astype(F32)).astype(BF16)


def slot_pairs(kept, sent):
    return (kept.astype(F32) + to_core(sent).astype(F32)).astype(BF16)


def on_eight(
    hidden_in,
    seg_ids,
    patch_rows,
    patch_cols,
    ln1_scale,
    ln1_shift,
    qkv_weight,
    qkv_bias,
    out_weight,
    out_bias,
    ln2_scale,
    ln2_shift,
    up_weight,
    up_bias,
    down_weight,
    down_bias,
    cotangent,
):
    me = lax.axis_index("rep")
    me_list = me.reshape(1).astype(jnp.int32)
    length, width = hidden_in.shape
    rows = ln1_scale.shape[0]
    size = width // HEADS
    heads = HEADS // COPIES
    part = heads * size
    hidden = up_weight.shape[1] // COPIES
    slots = ring_slots()
    vectors = (
        ln1_scale, ln1_shift, out_bias, ln2_scale, ln2_shift, down_bias, qkv_bias, up_bias,
    )

    order, masks = column_order(heads, size), head_masks(heads, size)
    table = rotary_table(heads, size)
    first = first_piece(me_list, order, qkv_weight, out_weight, vectors, part)
    ids, own_x, first = tie((jnp.concatenate([seg_ids, patch_rows, patch_cols]), hidden_in, first))
    ids = gather_rep(ids)
    own_x, ids[2] = tie((own_x, ids[2]))
    x = gather_rep(own_x)
    own_feed = second_piece(me_list, up_weight, down_weight, 8)
    x[2], own_grad = tie((x[2], cotangent))
    grad = gather_rep(own_grad)
    qkv_pieces = ring_gather(
        first, (), {1: x[2:3], 2: [own_feed, slots] + x[1:2] + grad[2:3], 3: x[3:] + ids[1:] + grad[1:2]}
    )
    ids = jnp.stack(ids)
    out_pieces = gather_rep(collect(qkv_pieces, rows, part))

    normed_one, qkv, lse, mixed, vec = ring_attend(
        me_list, slots, order, masks, table, x, ids, qkv_pieces, heads, size
    )
    mixed_all, middle, normed_two, w_own = middle_of(
        me_list, slots, gather_rep(mixed), vec, x, out_pieces, rows
    )
    feed_weights = ring_gather(
        own_feed, qkv_pieces[5:7], {1: [mixed, out_pieces[2]], 3: [normed_two]}
    )
    act, low, sent, kept, feed_sums = feed(
        slots, normed_two, grad, vec, feed_weights, hidden
    )

    arrived = to_core(sent)
    act, arrived = tie((act, arrived))
    chip_own, chip_far = (add_low(kept[n], arrived[n]) for n in range(2))
    far_one, far_two = to_x(chip_far), to_x(chip_own)

    tokens = COPIES * length
    feed_grad, feed_right, feed_left = feed_grads(
        slots, normed_two.reshape(tokens, width), act.reshape(tokens, hidden), low.reshape(tokens, hidden), grad
    )
    far_one, feed_grad, feed_right, feed_left = tie((far_one, feed_grad, feed_right, feed_left))

    (late,) = tie([act], [far_one])
    sent, kept = down_of(slots, late, feed_weights, width)
    made = {}

    def back(name, values, core):
        made[name] = ring_back(
            me_list, slots, order, masks, table, values, middle, grad, x, vec, w_own, qkv, lse, ids,
            qkv_pieces, heads, size, core == 0,
        )
        return made[name]

    def first_hop(_):
        made["far_two"], made["sent"], made["kept"] = tie((far_two, sent, kept))
        return [made["far_two"], made["sent"], made["kept"]]

    def second_hop(moved):
        own, other, _ = tie((far_one, made["far_two"], moved))
        made["total"] = jnp.stack([add_low(chip_own, own), add_low(chip_far, other)])
        made["out_pair"] = slot_pairs(made["kept"], made["sent"])
        return [back("own", made["total"], 0)[2], made["out_pair"]]

    def third_hop(_):
        made["out_far"] = to_x(made["out_pair"][1])
        return [back("near", to_core(made["total"]), 1)[1], made["out_far"]]

    def fourth_hop(_):
        grad_middle, cols, grad_qkv, _, sums = made["own"]
        near_cols, near_qkv, _, near_sums = made["near"]
        made["last"] = last_grads(
            me_list, slots, normed_one, mixed_all, (grad_qkv, near_qkv), (cols, near_cols),
            (sums, near_sums), feed_sums,
        )
        return [made["last"][0]]

    feed_grad = ring_scatter(
        feed_grad, feed_right, feed_left, slots, dict(enumerate((first_hop, second_hop, third_hop, fourth_hop))),
        [far_one], 4,
    )
    feed_slots = gather_rep(feed_grad)
    whole_up, whole_down = spread(me_list, feed_slots, rows)
    output = output_of(middle, made["out_pair"], made["out_far"], vec)

    pair = slot_pairs(made["own"][3], made["near"][2])
    far_pair = to_x(pair[1])
    grad_inputs = last_norm(made["own"][0], pair, far_pair, hidden_in, vec)
    last = ring_scatter(
        *made["last"],
        slots,
        {0: [pair], 1: [feed_grad, far_pair], 2: [output], 3: [feed_slots[2], grad_inputs]},
    )
    last_far, whole_up, whole_down = tie((to_x(last), whole_up, whole_down))
    last_slots = [last, to_core(last), last_far, to_core(last_far)]
    whole_qkv, whole_out, *totals = finish(
        me_list, last_slots, part, [vector.shape for vector in vectors]
    )
    return (
        output,
        grad_inputs,
        totals[0],
        totals[1],
        whole_qkv,
        totals[6],
        whole_out,
        totals[2],
        totals[3],
        totals[4],
        whole_up,
        totals[7],
        whole_down,
        totals[5],
    )


def solution(mesh):
    shards = mesh.shape["shard"]
    tokens, vector, matrix = P(("rep", "shard"), None), P("shard"), P("shard", None)
    in_specs = (
        (tokens,) * 4
        + (vector, vector, matrix, vector, matrix, vector)
        + (vector, vector, matrix, vector, matrix, vector)
        + (tokens,)
    )
    out_specs = (
        (tokens, tokens)
        + (vector, vector, matrix, vector, matrix, vector)
        + (vector, vector, matrix, vector, matrix, vector)
    )
    return jax.shard_map(
        on_eight if shards == 8 else lambda *args: on_any(shards, *args),
        mesh=mesh,
        in_specs=in_specs,
        out_specs=out_specs,
        check_vma=False,
    )
```

```python
import jax
import jax.numpy as jnp
import numpy as np
from jax import lax
from jax.experimental import pallas as pl
from jax.experimental.pallas import tpu as pltpu
from jax.sharding import PartitionSpec as P

HEADS = 16
EPSILON = 1e-06
GELU_SLOPE = 1.702
LANES = 128
MASKED = -1e30
COPIES = 4
EXTRA = 16
GRID = 32

CORE_PAIRS = [(0, 1), (1, 0), (2, 3), (3, 2)]
X_PAIRS = [(0, 2), (2, 0), (1, 3), (3, 1)]
RING = (0, 2, 4, 6, 7, 5, 3, 1)
RING_AT = tuple(RING.index(i) for i in range(8))
RIGHT = [(RING[i], RING[(i + 1) % 8]) for i in range(8)]
LEFT = [(RING[i], RING[(i - 1) % 8]) for i in range(8)]
OFFSETS = (0, -1, 1, -2, 2, -3, 3, 4, 4)

F32 = jnp.float32
BF16 = jnp.bfloat16
VMEM_LIMIT = 32 * 1024 * 1024


def norm_parts(values):
    center = values - jnp.mean(values, -1, keepdims=True)
    inverse = lax.rsqrt(jnp.mean(center * center, -1, keepdims=True) + EPSILON)
    return (center * inverse, inverse)


def norm_back(grad_normed, unit, inverse, scale):
    scaled = grad_normed * scale
    return inverse * (
        scaled
        - jnp.mean(scaled, -1, keepdims=True)
        - unit * jnp.mean(scaled * unit, -1, keepdims=True)
    )


def outer(left, right):
    return lax.dot_general(left, right, (((0,), (0,)), ((), ())), preferred_element_type=F32)


def times_transposed(left, right):
    return lax.dot_general(left, right, (((1,), (1,)), ((), ())), preferred_element_type=F32)


def times(left, right):
    return jnp.dot(left, right, preferred_element_type=F32)


def tie(values, after=()):
    values, after = tuple(values), tuple(after)
    return lax.optimization_barrier(values + after)[: len(values)]


def to_core(value):
    return lax.ppermute(value, "rep", CORE_PAIRS)


def to_x(value):
    return lax.ppermute(value, "rep", X_PAIRS)


def gather_rep(value):
    near, far = to_core(value), to_x(value)
    return [value, near, far, to_core(far)]


def reduce_pair(parts):
    low = parts.astype(BF16)
    arrived = to_core(jnp.stack([low[1], low[3]]))
    return (jnp.stack([low[0], low[2]]).astype(F32) + arrived.astype(F32)).astype(BF16)


def scatter_rep(parts):
    pair = reduce_pair(parts)
    return pair[0].astype(F32) + to_x(pair[1]).astype(F32)


def sum_rep(parts):
    pair = reduce_pair(parts)
    arrived = to_x(pair)
    total = (pair.astype(F32) + arrived[::-1].astype(F32)).astype(BF16)
    near = to_core(total)
    return jnp.stack([total[0], near[0], total[1], near[1]])


def by_owner(slots, me):
    core, far = me % 2 == 1, me // 2 == 1
    a, b, c, d = slots
    a, b, c, d = (
        jnp.where(core, b, a),
        jnp.where(core, a, b),
        jnp.where(core, d, c),
        jnp.where(core, c, d),
    )
    return [jnp.where(far, c, a), jnp.where(far, d, b), jnp.where(far, a, c), jnp.where(far, b, d)]


def gather_shards(pieces, shards):
    return [lax.all_gather(piece, "shard", axis=0) for piece in pieces]


def scatter_shards(whole, shards, rights):
    return lax.psum_scatter(whole, "shard", scatter_dimension=0, tiled=False)


def window(values, start, size):
    part = values[:, start : start + size]
    return jnp.concatenate([part, jnp.zeros((part.shape[0], LANES - size), part.dtype)], 1)


def turned(values, half, lane):
    return jnp.where(
        lane < half,
        pltpu.roll(values, LANES - half, 1),
        pltpu.roll(values, half, 1),
    )


def attend_kernel(
    heads, size, x_ref, gain_ref, shift_ref, w_ref, bias_ref, cos_ref, sin_ref, row_ref, col_ref,
    normed_ref, qkv_ref, lse_ref, out_ref,
):
    unit, _ = norm_parts(x_ref[...].astype(F32))
    normed = (unit * gain_ref[...] + shift_ref[...]).astype(BF16)
    normed_ref[...] = normed
    projected = times(normed, w_ref[...]) + bias_ref[...]
    cosine, sine = cos_ref[...], sin_ref[...]
    rows = projected.shape[0]
    lane = lax.broadcasted_iota(jnp.int32, (rows, LANES), 1)
    same = col_ref[...] == row_ref[0]
    scale = size**-0.5
    half = size // 2
    outs = []
    lses = jnp.zeros((rows, LANES), F32)
    for head in range(heads):
        query, key, value = (
            window(projected, (part * heads + head) * size, size) for part in range(3)
        )
        query = (query * cosine + turned(query, half, lane) * sine).astype(BF16)
        key = (key * cosine + turned(key, half, lane) * sine).astype(BF16)
        value = value.astype(BF16)
        for part, kept in enumerate((query, key, value)):
            at = (part * heads + head) * LANES
            qkv_ref[:, at : at + LANES] = kept
        scores = jnp.where(same, times_transposed(query, key) * scale, MASKED)
        most = jnp.max(scores, -1, keepdims=True)
        expo = jnp.exp(scores - most)
        total = jnp.sum(expo, -1, keepdims=True)
        probs = (expo * (1.0 / total)).astype(BF16)
        outs.append(times(probs, value)[:, :size])
        lses = jnp.where(lane == head, most + jnp.log(total), lses)
    lse_ref[...] = lses
    out_ref[...] = jnp.concatenate(outs, 1).astype(BF16)


def attend(x, gain, shift, weight, bias, cosine, sine, seg_rows, seg_cols, heads, size):
    tokens, width = x.shape
    length = seg_rows.shape[-1]
    part = heads * size
    by_block = lambda columns: pl.BlockSpec((length, columns), lambda i: (i, 0))
    fixed = lambda array: pl.BlockSpec(array.shape, lambda i: (0,) * array.ndim)
    return pl.pallas_call(
        lambda *refs: attend_kernel(heads, size, *refs),
        grid=(tokens // length,),
        in_specs=[
            by_block(width),
            fixed(gain),
            fixed(shift),
            fixed(weight),
            fixed(bias),
            by_block(LANES),
            by_block(LANES),
            pl.BlockSpec((1, 1, length), lambda i: (i, 0, 0)),
            by_block(1),
        ],
        out_specs=[by_block(width), by_block(3 * heads * LANES), by_block(LANES), by_block(part)],
        out_shape=[
            jax.ShapeDtypeStruct((tokens, width), BF16),
            jax.ShapeDtypeStruct((tokens, 3 * heads * LANES), BF16),
            jax.ShapeDtypeStruct((tokens, LANES), F32),
            jax.ShapeDtypeStruct((tokens, part), BF16),
        ],
        compiler_params=pltpu.CompilerParams(vmem_limit_bytes=48 * 1024 * 1024),
        cost_estimate=pl.CostEstimate(
            flops=2 * tokens * width * 3 * part + 4 * tokens * length * part,
            bytes_accessed=4 * tokens * width + weight.size * 2 + tokens * 3 * heads * LANES * 2,
            transcendentals=tokens * length * heads,
        ),
    )(x, gain, shift, weight, bias, cosine, sine, seg_rows, seg_cols)


def attend_back_kernel(
    heads, size, db_ref, wo_ref, qkv_ref, lse_ref, cos_ref, sin_ref, row_ref, col_ref, w_ref,
    x_ref, grad_ref, dn_ref, sum_ref, gain_ref, shift_ref,
):
    mixed = times_transposed(db_ref[...], wo_ref[...])
    cosine, sine = cos_ref[...], sin_ref[...]
    rows = mixed.shape[0]
    lane = lax.broadcasted_iota(jnp.int32, (rows, LANES), 1)
    same = col_ref[...] == row_ref[0]
    scale = size**-0.5
    half = size // 2
    lses = lse_ref[...]
    grads = [None] * (3 * heads)
    for head in range(heads):
        query, key, value = (
            qkv_ref[:, (part * heads + head) * LANES : (part * heads + head + 1) * LANES]
            for part in range(3)
        )
        lse = jnp.sum(jnp.where(lane == head, lses, 0.0), -1, keepdims=True)
        scores = jnp.where(same, times_transposed(query, key) * scale, MASKED)
        probs = jnp.exp(scores - lse)
        grad_mixed = window(mixed, head * size, size).astype(BF16)
        grad_probs = times_transposed(grad_mixed, value)
        grad_value = outer(probs.astype(BF16), grad_mixed)
        inner = jnp.sum(probs * grad_probs, -1, keepdims=True)
        low = (probs * (grad_probs - inner)).astype(BF16)
        grad_query = times(low, key) * scale
        grad_key = outer(low, query) * scale
        grad_query = grad_query * cosine + turned(grad_query * sine, half, lane)
        grad_key = grad_key * cosine + turned(grad_key * sine, half, lane)
        grads[head] = grad_query[:, :size]
        grads[heads + head] = grad_key[:, :size]
        grads[2 * heads + head] = grad_value[:, :size]
    grad = jnp.concatenate(grads, 1).astype(BF16)
    grad_ref[...] = grad
    grad_normed = times_transposed(grad, w_ref[...])
    dn_ref[...] = grad_normed.astype(BF16)
    unit, _ = norm_parts(x_ref[...].astype(F32))

    @pl.when(pl.program_id(0) == 0)
    def _():
        sum_ref[...] = jnp.zeros_like(sum_ref)
        gain_ref[...] = jnp.zeros_like(gain_ref)
        shift_ref[...] = jnp.zeros_like(shift_ref)

    sum_ref[...] += jnp.sum(grad.astype(F32), 0, keepdims=True)
    gain_ref[...] += jnp.sum(grad_normed * unit, 0, keepdims=True)
    shift_ref[...] += jnp.sum(grad_normed, 0, keepdims=True)


def attend_back(db, w_out, qkv, lse, cosine, sine, seg_rows, seg_cols, weight, x, heads, size):
    tokens, width = x.shape
    length = seg_rows.shape[-1]
    part = heads * size
    by_block = lambda columns: pl.BlockSpec((length, columns), lambda i: (i, 0))
    fixed = lambda shape: pl.BlockSpec(shape, lambda i: (0,) * len(shape))
    return pl.pallas_call(
        lambda *refs: attend_back_kernel(heads, size, *refs),
        grid=(tokens // length,),
        in_specs=[
            by_block(width),
            fixed(w_out.shape),
            by_block(3 * heads * LANES),
            by_block(LANES),
            by_block(LANES),
            by_block(LANES),
            pl.BlockSpec((1, 1, length), lambda i: (i, 0, 0)),
            by_block(1),
            fixed(weight.shape),
            by_block(width),
        ],
        out_specs=[
            by_block(3 * part),
            by_block(width),
            fixed((1, 3 * part)),
            fixed((1, width)),
            fixed((1, width)),
        ],
        out_shape=[
            jax.ShapeDtypeStruct((tokens, 3 * part), BF16),
            jax.ShapeDtypeStruct((tokens, width), BF16),
            jax.ShapeDtypeStruct((1, 3 * part), F32),
            jax.ShapeDtypeStruct((1, width), F32),
            jax.ShapeDtypeStruct((1, width), F32),
        ],
        compiler_params=pltpu.CompilerParams(vmem_limit_bytes=48 * 1024 * 1024),
        cost_estimate=pl.CostEstimate(
            flops=2 * tokens * width * 4 * part + 10 * tokens * length * part,
            bytes_accessed=6 * tokens * width + weight.size * 2 + tokens * 3 * heads * LANES * 2,
            transcendentals=tokens * length * heads,
        ),
    )(db, w_out, qkv, lse, cosine, sine, seg_rows, seg_cols, weight, x)


def rotary(rows, columns, size):
    quarter = size // 4
    inverse = 10000.0 ** (-4.0 * jnp.arange(quarter, dtype=F32) / size)
    angles = jnp.concatenate(
        [rows.astype(F32)[:, None] * inverse, columns.astype(F32)[:, None] * inverse], -1
    )
    cosine, sine = jnp.cos(angles), jnp.sin(angles)
    nothing = jnp.zeros((rows.shape[0], LANES - size), F32)
    return (
        jnp.concatenate([cosine, cosine, nothing], -1),
        jnp.concatenate([-sine, sine, nothing], -1),
    )


def on_any(
    shards,
    hidden_in,
    seg_ids,
    patch_rows,
    patch_cols,
    ln1_scale,
    ln1_shift,
    qkv_weight,
    qkv_bias,
    out_weight,
    out_bias,
    ln2_scale,
    ln2_shift,
    up_weight,
    up_bias,
    down_weight,
    down_bias,
    cotangent,
):
    copies = 4
    me = lax.axis_index("rep")
    length, width = hidden_in.shape
    rows = ln1_scale.shape[0]
    size = width // HEADS
    heads = HEADS // copies
    part = heads * size
    hidden = up_weight.shape[1]
    own_hidden = hidden // copies
    step = hidden // shards // copies

    def own(array, axis):
        return lax.dynamic_index_in_dim(array, me, axis, False)

    own_qkv = own(qkv_weight.reshape(rows, 3, copies, part), 2).reshape(rows, 3 * part)
    own_up = own(up_weight.reshape(rows, shards, copies, step), 2).reshape(rows, own_hidden)
    own_down = own(down_weight.reshape(copies, step, width), 0)
    own_out = own(out_weight.reshape(copies, rows // copies, width), 0)
    vectors = (
        ln1_scale, ln1_shift, out_bias, ln2_scale, ln2_shift, down_bias, qkv_bias, up_bias,
    )
    small = jnp.concatenate(vectors)
    small_rows = 8
    small = jnp.pad(small, (0, small_rows * 3 * part - small.size)).reshape(small_rows, 3 * part)
    first, up_full, out_all, down_full = gather_shards(
        [
            jnp.concatenate([own_qkv, small]),
            own_up,
            own_out,
            own_down,
        ],
        shards,
    )
    w_qkv = first[:, :rows].reshape(width, 3 * part)
    small = first[:, rows:].reshape(shards, -1)
    up_full = up_full.reshape(width, own_hidden)
    down_full = down_full.reshape(own_hidden, width)
    full = []
    at = 0
    for vector in vectors:
        full.append(small[:, at : at + vector.size].astype(F32))
        at += vector.size
    gain_one, shift_one, out_offset, gain_two, shift_two, down_offset = (
        v.reshape(1, width) for v in full[:6]
    )
    qkv_offset = own(full[6].reshape(3, copies, part), 1).reshape(1, 3 * part)
    up_offset = own(full[7].reshape(shards, copies, step), 1).reshape(1, own_hidden)

    ids = jnp.concatenate([seg_ids, patch_rows, patch_cols])
    ids = jnp.stack(gather_rep(ids))
    seg_rows, seg_cols = ids[:, :1], ids[:, 0].reshape(-1, 1)
    x_low = jnp.concatenate(gather_rep(hidden_in))
    grad_out = jnp.concatenate(gather_rep(cotangent))
    tokens = x_low.shape[0]
    cosine, sine = rotary(ids[:, 1].reshape(-1), ids[:, 2].reshape(-1), size)

    normed_one, qkv, lse, mixed = attend(
        x_low, gain_one, shift_one, w_qkv, qkv_offset, cosine, sine, seg_rows, seg_cols, heads, size
    )
    out_full = jnp.stack(by_owner(gather_rep(out_all), me), 1).reshape(width, width)
    blocks = mixed.reshape(copies, length, part)
    near, far = to_core(blocks), to_x(blocks)
    both = to_core(far)
    mixed_slots = [
        mixed,
        near[jnp.array([1, 0, 3, 2])].reshape(tokens, part),
        far[jnp.array([2, 3, 0, 1])].reshape(tokens, part),
        both[jnp.array([3, 2, 1, 0])].reshape(tokens, part),
    ]
    mixed_full = jnp.concatenate(by_owner(mixed_slots, me), 1)

    middle = x_low.astype(F32) + times(mixed_full, out_full) + out_offset
    unit_two, inverse_two = norm_parts(middle)
    normed_two = (unit_two * gain_two + shift_two).astype(BF16)
    upward = times(normed_two, up_full) + up_offset
    sigma = jax.nn.sigmoid(GELU_SLOPE * upward)
    activated = (upward * sigma).astype(BF16)
    slope = sigma + GELU_SLOPE * upward * sigma * (1.0 - sigma)

    grad_down = outer(activated, grad_out).astype(BF16)
    grad_up_low = (times_transposed(grad_out, down_full) * slope).astype(BF16)
    grad_normed_two = sum_rep(times_transposed(grad_up_low, up_full).reshape(copies, length, width))
    grad_up = outer(normed_two, grad_up_low).astype(BF16)
    grad_up_bias = jnp.sum(grad_up_low.astype(F32), 0)
    branch = scatter_rep(times(activated, down_full).reshape(copies, length, width))
    output = middle[:length] + branch + down_offset

    grad_normed_two = grad_normed_two.reshape(tokens, width).astype(F32)
    grad_middle = grad_out.astype(F32) + norm_back(
        grad_normed_two, unit_two, inverse_two, gain_two
    )
    grad_branch = grad_middle.astype(BF16)
    grad_out_w = outer(mixed_full, own(grad_branch.reshape(tokens, copies, part), 1)).astype(BF16)

    own_w_out = lax.dynamic_slice_in_dim(out_full, me * part, part, 0)
    grad_qkv_low, grad_normed_one, sum_qkv, sum_gain, sum_shift = attend_back(
        grad_branch, own_w_out, qkv, lse, cosine, sine, seg_rows, seg_cols, w_qkv, x_low, heads, size
    )
    grad_qkv = outer(normed_one, grad_qkv_low).astype(BF16)
    grad_normed_one = scatter_rep(grad_normed_one.reshape(copies, length, width))
    unit_one, inverse_one = norm_parts(hidden_in.astype(F32))
    grad_inputs = grad_middle[:length] + norm_back(grad_normed_one, unit_one, inverse_one, gain_one)

    def sum_of(values):
        return jnp.sum(values[:length], 0).reshape(shards, rows)

    def placed(values, like, axis):
        return lax.dynamic_update_index_in_dim(jnp.zeros(like, F32), values, me, axis)

    sums = [
        sum_gain.reshape(shards, rows),
        sum_shift.reshape(shards, rows),
        sum_of(grad_branch.astype(F32)),
        sum_of(grad_normed_two * unit_two),
        sum_of(grad_normed_two),
        sum_of(grad_out.astype(F32)),
        placed(sum_qkv.reshape(3, part), (3, copies, part), 1).reshape(shards, -1),
        placed(grad_up_bias.reshape(shards, step), (shards, copies, step), 1).reshape(shards, -1),
    ]
    sums = jnp.concatenate(sums, 1)
    sums = jnp.pad(sums, ((0, 0), (0, small_rows * 3 * part - sums.shape[1])))
    last = jnp.concatenate(
        [grad_qkv.reshape(shards, rows, 3 * part), sums.astype(BF16).reshape(shards, small_rows, -1)],
        1,
    )

    done_down = scatter_shards(grad_down.reshape(shards, step, width), shards, 4)
    done_up = scatter_shards(grad_up.reshape(shards, rows, own_hidden), shards, 3)
    done_out = scatter_shards(grad_out_w.reshape(shards, rows, part), shards, 4)
    done_last = scatter_shards(last, shards, 4)

    whole_down = jnp.concatenate(by_owner(gather_rep(done_down), me), 0).astype(F32)
    whole_up = jnp.stack(
        [p.reshape(rows, shards, step) for p in by_owner(gather_rep(done_up), me)], 2
    )
    whole_up = whole_up.reshape(rows, hidden).astype(F32)
    whole_out = jnp.concatenate(by_owner(gather_rep(done_out), me), 1).astype(F32)
    last_slots = gather_rep(done_last)
    whole_qkv = jnp.stack(
        [p[:rows].reshape(rows, 3, part) for p in by_owner(last_slots, me)], 2
    )
    whole_qkv = whole_qkv.reshape(rows, 3 * width).astype(F32)
    summed = sum(p[rows:].astype(F32) for p in by_owner(last_slots, me)).reshape(-1)
    totals = []
    at = 0
    for vector in vectors:
        totals.append(summed[at : at + vector.size])
        at += vector.size
    return (
        output.astype(BF16),
        grad_inputs.astype(BF16),
        totals[0],
        totals[1],
        whole_qkv,
        totals[6],
        whole_out,
        totals[2],
        totals[3],
        totals[4],
        whole_up,
        totals[7],
        whole_down,
        totals[5],
    )


def ring_slots():
    position = jnp.asarray(RING_AT, jnp.int32)[lax.axis_index("shard")]
    return jnp.asarray(RING, jnp.int32)[(position + jnp.asarray(OFFSETS, jnp.int32)) % 8]


def half_of(rows):
    return (rows // 2 + 15) // 16 * 16


def ring_gather(piece, after=(), others=None):
    right = left = piece
    if after:
        right, left = tie((piece, piece), after)
    pieces = [piece]
    for hop in range(4):
        if hop == 3:
            cut = half_of(piece.shape[0])
            right, left = right[:cut], left[cut:]
        right, left = tie(
            (lax.ppermute(right, "shard", RIGHT), lax.ppermute(left, "shard", LEFT)),
            (others or {}).get(hop, ()),
        )
        pieces += [right, left]
    return pieces


def hop_kernel(first, _, ahead_ref, behind_ref, right_ref, left_ref, to_right_ref, to_left_ref):
    i = pl.program_id(0)

    def plus(out_ref, own_ref, other_ref):
        out_ref[...] = (own_ref[0].astype(F32) + other_ref[...].astype(F32)).astype(BF16)

    def copy(out_ref, own_ref):
        out_ref[...] = own_ref[0]

    if not first:
        plus(to_right_ref, ahead_ref, right_ref)
        plus(to_left_ref, behind_ref, left_ref)
        return

    if right_ref.shape != to_right_ref.shape:
        cut = right_ref.shape[0]
        to_right_ref[:cut] = add_low(ahead_ref[0, :cut], right_ref[...])
        to_right_ref[cut:] = ahead_ref[0, cut:]
        to_left_ref[:cut] = behind_ref[0, :cut]
        to_left_ref[cut:] = add_low(behind_ref[0, cut:], left_ref[...])
        return

    @pl.when(i < pl.num_programs(0) // 2)
    def _():
        plus(to_right_ref, ahead_ref, right_ref)
        copy(to_left_ref, behind_ref)

    @pl.when(i >= pl.num_programs(0) // 2)
    def _():
        copy(to_right_ref, ahead_ref)
        plus(to_left_ref, behind_ref, left_ref)


def hop_sums(whole, slots, right, left, hop, steps):
    _, rows, width = whole.shape
    tile = rows // steps
    half = steps // 2
    first = hop == 0
    term = lambda n: pl.BlockSpec((1, tile, width), lambda i, s: (s[n], i, 0))
    block = lambda at: pl.BlockSpec((tile, width), lambda i, s: (at(i), 0))
    same = lambda i: i
    return pl.pallas_call(
        lambda *refs: hop_kernel(first, *refs),
        grid_spec=pltpu.PrefetchScalarGridSpec(
            num_scalar_prefetch=1,
            grid=(steps,),
            in_specs=[
                term(6 - 2 * hop),
                term(5 - 2 * hop),
                *(
                    [pl.BlockSpec(v.shape, lambda i, s: (0, 0)) for v in (right, left)]
                    if steps == 1
                    else [
                        block((lambda i: jnp.minimum(i, half - 1)) if first else same),
                        block((lambda i: jnp.maximum(i - half, 0)) if first else same),
                    ]
                ),
            ],
            out_specs=[block(same), block(same)],
        ),
        out_shape=[like((rows, width), BF16)] * 2,
        compiler_params=params(),
        cost_estimate=cost(),
    )(slots, whole, whole, right, left)


def ring_scatter(whole, right, left, slots, others=None, after=(), steps=0):
    cut = right.shape[0]

    def own(number):
        return lax.dynamic_slice(
            whole, (slots[number], 0, 0), (1,) + whole.shape[1:], allow_negative_indices=False
        )[0]

    if after:
        right, left = tie((right, left), after)
    for hop in range(4):
        waited = (others or {}).get(hop, ())
        if callable(waited):
            waited = waited(right)
        right, left = tie(
            (lax.ppermute(right, "shard", RIGHT), lax.ppermute(left, "shard", LEFT)), waited
        )
        if hop == 3:
            break
        if steps > 1 or (steps and hop):
            right, left = hop_sums(whole, slots, right, left, hop, steps)
            continue
        ahead, behind = own(6 - 2 * hop), own(5 - 2 * hop)
        if hop == 0:
            right = jnp.concatenate([add_low(right, ahead[:cut]), ahead[cut:]])
            left = jnp.concatenate([behind[:cut], add_low(left, behind[cut:])])
        else:
            right, left = add_low(right, ahead), add_low(left, behind)
    return (right.astype(F32) + left.astype(F32) + own(0).astype(F32)).astype(BF16)


def run_copies(copies):
    for copy in copies:
        copy.start()
    for copy in copies:
        copy.wait()


ANYWHERE = pl.BlockSpec(memory_space=pl.ANY)
SCALARS = pl.BlockSpec(memory_space=pltpu.SMEM)
WHOLE = pl.BlockSpec(memory_space=pltpu.VMEM)


def params():
    return pltpu.CompilerParams(vmem_limit_bytes=VMEM_LIMIT)


def fixed(shape):
    return pl.BlockSpec(shape, lambda i: (0,) * len(shape))


def cost(microseconds=0):
    return pl.CostEstimate(flops=1, bytes_accessed=1 + microseconds * 3_690_000, transcendentals=0)


def like(shape, dtype):
    return jax.ShapeDtypeStruct(shape, dtype)


def far(shape, dtype):
    return pltpu.HBM(shape, dtype)


def kept_far(arrays):
    return [pltpu.with_memory_space_constraint(a, pltpu.HBM) for a in arrays]


def joined(slots):
    return jnp.concatenate(slots, 0)


def column_order(heads, size):
    half = size // 2
    left = heads * half - LANES
    order = np.zeros((2 * heads * size, 2 * heads * size), np.float32)
    for part in range(2):
        for head in range(heads):
            for side in range(2):
                for feature in range(half):
                    natural = (part * heads + head) * size + side * half + feature
                    at = head * half + feature
                    group = 2 * part + side
                    to = group * LANES + at if at < LANES else (4 * LANES + group * left + at - LANES)
                    order[natural, to] = 1.0
    return jnp.asarray(order, BF16)


def head_masks(heads, size):
    half = size // 2
    left = heads * half - LANES
    masks = np.zeros((2 * heads, 3 * LANES), np.float32)
    for head in range(heads):
        for lane in range(2 * LANES):
            masks[head, lane] = (lane % LANES) // half == head
        for lane in range(2 * left):
            masks[head, 2 * LANES + lane] = (LANES + lane % left) // half == head
        masks[heads + head, head * size : (head + 1) * size] = 1.0
    return jnp.asarray(masks, F32)


def rotary_table(heads, size):
    half, quarter = size // 2, size // 4
    left = heads * half - LANES
    at = np.concatenate([np.arange(LANES), LANES + np.arange(4 * left) % left]) % half
    inverse = (10000.0 ** (-4.0 * np.arange(quarter, dtype=np.float32) / size)).astype(np.float32)
    angles = np.arange(GRID, dtype=np.float32)[:, None] * inverse[at % quarter]
    sign = np.ones(2 * LANES, np.float32)
    for group in (0, 2):
        sign[LANES + group * left : LANES + (group + 1) * left] = -1.0
    both = np.concatenate([np.cos(angles), np.sin(angles) * sign], 1)
    by_row = np.concatenate([at < quarter, at < quarter])
    return jnp.asarray(np.concatenate([np.where(by_row, both, 0.0), np.where(by_row, 0.0, both)]), F32)


def positions(ids, table):
    grid = lax.broadcasted_iota(jnp.int32, (GRID, ids.shape[1]), 0)
    picks = jnp.concatenate([grid == ids[1:2], grid == ids[2:3]], 0).astype(F32)
    both = lax.dot_general(
        picks, table, (((0,), (0,)), ((), ())), precision=lax.Precision.HIGHEST,
        preferred_element_type=F32,
    )
    image = (grid[:8] == ids[0:1]).astype(F32)
    return tiles(both, 4), outer(image, image) > 0.5


def first_kernel(part, *refs):
    me_ref, order_ref, weight_ref, other_ref = refs[:4]
    vectors, out_ref = refs[4:12], refs[12]
    rows, width = out_ref.shape[0] - EXTRA, out_ref.shape[1]
    for me in range(COPIES):

        @pl.when(me_ref[0] == me)
        def _():
            parts = [
                weight_ref[:, (n * COPIES + me) * part : (n * COPIES + me + 1) * part]
                for n in range(3)
            ]
            turned = times(jnp.concatenate(parts[:2], 1), order_ref[...]).astype(BF16)
            out_ref[:rows] = jnp.concatenate(
                [turned, parts[2], other_ref[:, me * part : (me + 1) * part]], 1
            )

    lines = [v[...].astype(F32).reshape(1, -1) for v in vectors]
    lines = [jnp.concatenate(lines[:6], 1), lines[6], lines[7]]
    lines = [
        jnp.concatenate([line, jnp.zeros((1, width - line.shape[1]), F32)], 1) for line in lines
    ]
    lines.append(jnp.zeros((EXTRA - len(lines), width), F32))
    out_ref[rows:] = jnp.concatenate(lines, 0).astype(BF16)


def first_piece(me, order, weight, other, vectors, part):
    rows = weight.shape[0]
    return pl.pallas_call(
        lambda *refs: first_kernel(part, *refs),
        in_specs=[SCALARS] + [WHOLE] * 11,
        out_specs=WHOLE,
        out_shape=like((rows + EXTRA, COPIES * part), BF16),
        compiler_params=params(),
        cost_estimate=cost(),
    )(me, *kept_far([order, weight, other, *vectors]))


def collect_kernel(rows, *refs):
    pieces, (out_ref, lines_ref, semaphores) = refs[:9], refs[9:]
    lanes = lines_ref.shape[2]
    part = out_ref.shape[1] // COPIES
    copies = []
    for number, ref in enumerate(pieces):
        edge = half_of(rows + EXTRA)
        start, count = (edge, rows - edge) if number == 8 else (0, edge if number == 7 else rows)
        copies.append(
            pltpu.make_async_copy(
                ref.at[pl.ds(0, count), pl.ds(ref.shape[1] - lanes, lanes)],
                lines_ref.at[min(number, 7), pl.ds(start, count)],
                semaphores.at[number],
            )
        )
    run_copies(copies)
    for line in range(2):
        out_ref[line * rows : (line + 1) * rows] = jnp.concatenate(
            [lines_ref[2 * n + line][:, lanes - part :] for n in range(COPIES)], 1
        )


def collect(pieces, rows, part):
    lanes = -(-part // LANES) * LANES
    return pl.pallas_call(
        lambda *refs: collect_kernel(rows, *refs),
        in_specs=[ANYWHERE] * len(pieces),
        out_specs=WHOLE,
        out_shape=like((2 * rows, COPIES * part), BF16),
        scratch_shapes=[pltpu.VMEM((8, rows, lanes), BF16), pltpu.SemaphoreType.DMA((9,))],
        compiler_params=params(),
        cost_estimate=cost(),
    )(*kept_far(pieces))


def second_kernel(shards, me_ref, up_ref, down_ref, out_ref):
    rows, hidden = up_ref.shape
    step = hidden // shards // COPIES
    for me in range(COPIES):

        @pl.when(me_ref[0] == me)
        def _():
            out_ref[:rows] = jnp.concatenate(
                [
                    up_ref[:, (n * COPIES + me) * step : (n * COPIES + me + 1) * step]
                    for n in range(shards)
                ],
                1,
            )
            out_ref[rows:] = down_ref[me * step : (me + 1) * step]


def second_piece(me, up, down, shards):
    rows, hidden = up.shape
    step = hidden // shards // COPIES
    return pl.pallas_call(
        lambda *refs: second_kernel(shards, *refs),
        in_specs=[SCALARS] + [WHOLE] * 2,
        out_specs=WHOLE,
        out_shape=like((rows + step, hidden // COPIES), BF16),
        compiler_params=params(),
        cost_estimate=cost(),
    )(me, *kept_far([up, down]))


def first_copies(refs, place, rows, w_ref, small_ref, semaphores):
    cut = half_of(rows + EXTRA)
    copies = []
    for number, ref in enumerate(refs):
        slot = place[number]
        start, count = (cut, rows - cut) if number == 8 else (0, cut if number == 7 else rows)
        at = pl.multiple_of(slot * rows + start, 16)
        copies.append(
            pltpu.make_async_copy(
                ref.at[pl.ds(0, count), pl.ds(0, w_ref.shape[1])],
                w_ref.at[pl.ds(at, count)],
                semaphores.at[0, number],
            )
        )
        if number != 7 and small_ref is not None:
            copies.append(
                pltpu.make_async_copy(
                    ref.at[pl.ds(count, EXTRA)], small_ref.at[slot], semaphores.at[1, number]
                )
            )
    return copies


def vectors_of(me_ref, small_ref, order_ref, vec_ref, bias_ref, full_ref):
    shards = small_ref.shape[0]
    width = vec_ref.shape[1]
    rows = width // shards
    part = width // COPIES
    lines = [small_ref[s].astype(F32) for s in range(shards)]
    for n in range(6):
        vec_ref[n : n + 1] = jnp.concatenate(
            [line[0:1, n * rows : (n + 1) * rows] for line in lines], 1
        )
    full_ref[...] = jnp.concatenate([line[1:2, : 3 * rows] for line in lines], 1)
    vec_ref[7:8] = jnp.zeros((1, width), F32)
    bias_ref[...] = jnp.zeros_like(bias_ref)
    for me in range(COPIES):

        @pl.when(me_ref[0] == me)
        def _():
            vec_ref[6:7] = jnp.concatenate(
                [line[2:3, me * rows : (me + 1) * rows] for line in lines], 1
            )
            parts = [
                full_ref[:, (n * COPIES + me) * part : (n * COPIES + me + 1) * part] for n in range(3)
            ]
            both = jnp.broadcast_to(jnp.concatenate(parts[:2], 1), (8, 2 * part)).astype(BF16)
            bias_ref[:, : 2 * part] = times(both, order_ref[...])[:1]
            bias_ref[:, 2 * part : 3 * part] = parts[2]


def swapped(values, lane, left):
    return jnp.where(
        lane // left % 2 == 0,
        pltpu.roll(values, LANES - left, 1),
        pltpu.roll(values, left, 1),
    )


def tiles(values, count):
    return [values[:, n * LANES : (n + 1) * LANES] for n in range(count)]


def ring_attend_kernel(heads, size, *refs):
    (
        me_ref, place_ref, order_ref, mask_ref, table_ref, x0, x1, x2, x3, ids_ref,
    ), refs = refs[:10], refs[10:]
    pieces, refs = refs[:9], refs[9:]
    (
        normed_ref, qkv_ref, lse_ref, out_ref, vec_ref, w_ref, small_ref, bias_ref, full_ref, all_ref,
        project_ref, semaphores,
    ) = refs
    i = pl.program_id(0)
    length, width = x0.shape
    rows = width // 8
    part = heads * size

    @pl.when(i == 0)
    def _():
        copies = first_copies(pieces, place_ref, rows, w_ref, small_ref, semaphores)
        for copy in copies:
            copy.start()
        for copy in copies[1:14:2] + copies[-1:]:
            copy.wait()
        vectors_of(me_ref, small_ref, order_ref, vec_ref, bias_ref, full_ref)
        for slot, x_ref in enumerate((x0, x1, x2, x3)):
            unit, _ = norm_parts(x_ref[...].astype(F32))
            all_ref[slot * length : (slot + 1) * length] = (
                unit * vec_ref[0:1] + vec_ref[1:2]
            ).astype(BF16)
        for copy in copies[0:14:2] + copies[14:16]:
            copy.wait()
        project_ref[...] = times(all_ref[...], w_ref[...]) + bias_ref[...]

    here = pl.ds(pl.multiple_of(i * length, 16), length)
    normed_ref[...] = all_ref[here, :]
    q1, q2, k1, k2, rest = tiles(project_ref[here, : 5 * LANES], 5)
    value = project_ref[here, 5 * LANES :]
    lane = lax.broadcasted_iota(jnp.int32, (length, LANES), 1)
    wide = lax.broadcasted_iota(jnp.int32, (length, 3 * LANES), 1)
    (cosine, cosine_rest, sine, sine_rest), same = positions(ids_ref[0], table_ref[...])
    left = heads * size // 2 - LANES
    rest = rest * cosine_rest + swapped(rest, lane, left) * sine_rest
    query = jnp.concatenate(
        [q1 * cosine - q2 * sine, q2 * cosine + q1 * sine, jnp.where(lane < 2 * left, rest, 0.0)], 1
    ).astype(BF16)
    key = jnp.concatenate(
        [
            k1 * cosine - k2 * sine,
            k2 * cosine + k1 * sine,
            jnp.where(lane < 2 * left, pltpu.roll(rest, 2 * left, 1), 0.0),
        ],
        1,
    ).astype(BF16)
    value = jnp.where(wide < part, value, 0.0).astype(BF16)
    qkv_ref[...] = jnp.concatenate([query, key, value], 1)
    masks = mask_ref[...].astype(BF16)
    scale = size**-0.5
    all_probs, all_values = [], []
    lses = jnp.zeros((length, LANES), F32)
    for head in range(heads):
        scores = times_transposed(query * masks[head : head + 1], key)
        scores = jnp.where(same, scores * scale, MASKED)
        most = jnp.max(scores, -1, keepdims=True)
        expo = jnp.exp(scores - most)
        total = jnp.sum(expo, -1, keepdims=True)
        all_probs.append((expo * (1.0 / total)).astype(BF16))
        all_values.append(value * masks[heads + head : heads + head + 1])
        lses = jnp.where(lane == head, most + jnp.log(total), lses)
    lse_ref[...] = lses
    out = times(jnp.concatenate(all_probs, 1), joined(all_values))[:, :part].astype(BF16)
    count = out_ref.shape[1]
    out_ref[0] = jnp.concatenate([out[n * count : (n + 1) * count] for n in range(COPIES)], 1)


def ring_attend(me, place, order, masks, table, x, ids, pieces, heads, size):
    length, width = x[0].shape
    tokens = COPIES * length
    by_block = lambda columns: pl.BlockSpec((length, columns), lambda i: (i, 0))
    return pl.pallas_call(
        lambda *refs: ring_attend_kernel(heads, size, *refs),
        grid=(COPIES,),
        in_specs=[SCALARS, SCALARS, fixed(order.shape), fixed(masks.shape), fixed(table.shape)]
        + [fixed((length, width))] * COPIES
        + [pl.BlockSpec((1,) + ids.shape[1:], lambda i: (i, 0, 0))]
        + [ANYWHERE] * len(pieces),
        out_specs=[
            by_block(width),
            by_block(9 * LANES),
            by_block(LANES),
            pl.BlockSpec((1, length // COPIES, width), lambda i: (i, 0, 0)),
            fixed((8, width)),
        ],
        out_shape=[
            far((tokens, width), BF16),
            far((tokens, 9 * LANES), BF16),
            far((tokens, LANES), F32),
            like((COPIES, length // COPIES, width), BF16),
            like((8, width), F32),
        ],
        scratch_shapes=[
            pltpu.VMEM((width, 8 * LANES), BF16),
            pltpu.VMEM((8, EXTRA, width), BF16),
            pltpu.VMEM((1, 8 * LANES), F32),
            pltpu.VMEM((1, 3 * width), F32),
            pltpu.VMEM((tokens, width), BF16),
            pltpu.VMEM((tokens, 8 * LANES), F32),
            pltpu.SemaphoreType.DMA((2, len(pieces))),
        ],
        compiler_params=params(),
        cost_estimate=cost(25),
    )(
        me, place, *kept_far([order, masks, table, *x]), ids, *kept_far(pieces)
    )


def middle_kernel(rows, part, *refs):
    me_ref, place_ref, own_ref, near_ref, far_ref, both_ref, vec_ref, x0, x1, x2, x3 = refs[:11]
    weights, (all_ref, middle_ref, normed_ref, wown_ref, w_ref, x_ref) = (
        refs[11:15],
        refs[15:],
    )
    j = pl.program_id(0)

    @pl.when(j == 0)
    def _():
        me = me_ref[0]
        for own in range(COPIES):

            @pl.when(me == own)
            def _():
                for n in range(8):
                    here = slice(n % 2 * rows, (n % 2 + 1) * rows)
                    lanes = slice(n // 2 * part, (n // 2 + 1) * part)
                    at = pl.multiple_of(place_ref[n] * rows, 16)
                    w_ref[pl.ds(at, rows), :] = jnp.concatenate(
                        [weights[own ^ b][here, lanes] for b in range(COPIES)], 1
                    )

        wown_ref[...] = w_ref[pl.ds(pl.multiple_of(me * part, 16), part), :]
        x_ref[...] = joined([x0[...], x1[...]])

    @pl.when(j == 1)
    def _():
        x_ref[...] = joined([x2[...], x3[...]])

    def unpacked(ref, order):
        return joined(
            [ref[b, :, n * part : (n + 1) * part] for b in order for n in range(COPIES)]
        )

    slots = [
        unpacked(own_ref, (0, 1)),
        unpacked(near_ref, (1, 0)),
        unpacked(far_ref, (0, 1)),
        unpacked(both_ref, (1, 0)),
    ]
    for me in range(COPIES):

        @pl.when(me_ref[0] == me)
        def _():
            all_ref[...] = jnp.concatenate([slots[me ^ n] for n in range(COPIES)], 1)

    middle = x_ref[...].astype(F32) + times(all_ref[...], w_ref[...]) + vec_ref[2:3]
    unit, _ = norm_parts(middle)
    normed = (unit * vec_ref[3:4] + vec_ref[4:5]).astype(BF16)
    length = middle_ref.shape[2]
    for core in range(2):
        middle_ref[0, core] = middle[core * length : (core + 1) * length]
        normed_ref[0, core] = normed[core * length : (core + 1) * length]


def middle_of(me, place, mixed, vec, x, weights, rows):
    length, width = x[0].shape
    part = width // COPIES
    tokens = COPIES * length
    by_slots = lambda flip: pl.BlockSpec(
        (2,) + mixed[0].shape[1:], lambda j: ((1 - j) if flip else j, 0, 0)
    )
    by_half = pl.BlockSpec((1, 2, length, width), lambda j: (j, 0, 0, 0))
    return pl.pallas_call(
        lambda *refs: middle_kernel(rows, part, *refs),
        grid=(2,),
        in_specs=[SCALARS, SCALARS]
        + [by_slots(False), by_slots(False), by_slots(True), by_slots(True), fixed(vec.shape)]
        + [fixed((length, width))] * COPIES
        + [fixed(weights[0].shape)] * COPIES,
        out_specs=[
            pl.BlockSpec((2 * length, width), lambda j: (j, 0)),
            by_half,
            by_half,
            fixed((part, width)),
        ],
        out_shape=[
            far((tokens, width), BF16),
            far((2, 2, length, width), F32),
            far((2, 2, length, width), BF16),
            far((part, width), BF16),
        ],
        scratch_shapes=[
            pltpu.VMEM((width, width), BF16),
            pltpu.VMEM((2 * length, width), BF16),
        ],
        compiler_params=params(),
        cost_estimate=cost(13),
    )(me, place, *mixed, vec, *kept_far([*x, *weights]))


def split_copies(pieces, place, up_ref, down_ref, semaphores):
    copies = []
    for number, ref in enumerate(pieces):
        for line, target in enumerate((up_ref, down_ref)):
            if target is None or (number == 7 and line == 1) or (number == 8 and line == 0):
                continue
            count = target.shape[0] // 8
            copies.append(
                pltpu.make_async_copy(
                    ref.at[pl.ds(count if line == 1 and number < 7 else 0, count)],
                    target.at[pl.ds(pl.multiple_of(place[number] * count, 16), count)],
                    semaphores.at[line, number],
                )
            )
    return copies


def feed_kernel(place_ref, normed_ref, g0, g1, g2, g3, vec_ref, *refs):
    pieces, refs = refs[:9], refs[9:]
    act_ref, dh_ref, sent_ref, kept_ref, sum_ref, up_ref, down_ref, grad_ref, semaphores = refs
    j = pl.program_id(0)

    @pl.when(j == 0)
    def _():
        copies = split_copies(pieces, place_ref, up_ref, None, semaphores)
        later = split_copies(pieces, place_ref, None, down_ref, semaphores)
        for copy in copies + later:
            copy.start()
        for copy in copies:
            copy.wait()
        sum_ref[...] = jnp.zeros_like(sum_ref)
        sum_ref[1:2] = jnp.sum(g0[...].astype(F32), 0, keepdims=True)
        grad_ref[...] = joined([g1[...], g3[...]])

    @pl.when(j == 1)
    def _():
        grad_ref[...] = joined([g0[...], g2[...]])

    normed = joined([normed_ref[0, 0], normed_ref[1, 0]])
    upward = times(normed, up_ref[...]) + vec_ref[6:7]
    sigma = jax.nn.sigmoid(GELU_SLOPE * upward)
    act = (upward * sigma).astype(BF16)
    slope = sigma + GELU_SLOPE * upward * sigma * (1.0 - sigma)

    @pl.when(j == 0)
    def _():
        for copy in split_copies(pieces, place_ref, None, down_ref, semaphores):
            copy.wait()

    low = (times_transposed(grad_ref[...], down_ref[...]) * slope).astype(BF16)
    sum_ref[0:1] += jnp.sum(low.astype(F32), 0, keepdims=True)
    back = times_transposed(low, up_ref[...]).astype(BF16)
    length = normed_ref.shape[2]
    for half in range(2):
        here = slice(half * length, (half + 1) * length)
        act_ref[half, 0] = act[here]
        dh_ref[half, 0] = low[here]

    @pl.when(j == 0)
    def _():
        for half in range(2):
            sent_ref[half] = back[half * length : (half + 1) * length]

    @pl.when(j == 1)
    def _():
        for half in range(2):
            kept_ref[half] = back[half * length : (half + 1) * length]


def feed(place, normed, grad, vec, pieces, hidden):
    _, _, length, width = normed.shape
    by_core = lambda columns: pl.BlockSpec((2, 1, length, columns), lambda j: (0, 1 - j, 0, 0))
    pair = like((2, length, width), BF16)
    return pl.pallas_call(
        feed_kernel,
        grid=(2,),
        in_specs=[SCALARS, by_core(width)]
        + [fixed((length, width))] * COPIES
        + [fixed(vec.shape)]
        + [ANYWHERE] * len(pieces),
        out_specs=[
            by_core(hidden),
            by_core(hidden),
            fixed((2, length, width)),
            fixed((2, length, width)),
            fixed((8, hidden)),
        ],
        out_shape=[
            far((2, 2, length, hidden), BF16),
            far((2, 2, length, hidden), BF16),
            pair,
            pair,
            like((8, hidden), F32),
        ],
        scratch_shapes=[
            pltpu.VMEM((width, hidden), BF16),
            pltpu.VMEM((hidden, width), BF16),
            pltpu.VMEM((2 * length, width), BF16),
            pltpu.SemaphoreType.DMA((2, 9)),
        ],
        compiler_params=params(),
        cost_estimate=cost(20),
    )(place, *kept_far([normed, *grad]), vec, *kept_far(pieces))


def down_kernel(place_ref, act_ref, *refs):
    pieces, (sent_ref, kept_ref, down_ref, semaphores) = refs[:9], refs[9:]
    j = pl.program_id(0)

    @pl.when(j == 0)
    def _():
        run_copies(split_copies(pieces, place_ref, None, down_ref, semaphores))

    value = times(joined([act_ref[0, 0], act_ref[1, 0]]), down_ref[...]).astype(BF16)
    length = act_ref.shape[2]

    @pl.when(j == 0)
    def _():
        for half in range(2):
            sent_ref[half] = value[half * length : (half + 1) * length]

    @pl.when(j == 1)
    def _():
        for half in range(2):
            kept_ref[half] = value[half * length : (half + 1) * length]


def down_of(place, act, pieces, width):
    _, _, length, hidden = act.shape
    pair = like((2, length, width), BF16)
    return pl.pallas_call(
        down_kernel,
        grid=(2,),
        in_specs=[SCALARS, pl.BlockSpec((2, 1, length, hidden), lambda j: (0, 1 - j, 0, 0))]
        + [ANYWHERE] * len(pieces),
        out_specs=[fixed((2, length, width)), fixed((2, length, width))],
        out_shape=[pair, pair],
        scratch_shapes=[pltpu.VMEM((hidden, width), BF16), pltpu.SemaphoreType.DMA((2, 9))],
        compiler_params=params(),
        cost_estimate=cost(),
    )(place, *kept_far([act, *pieces]))


def feed_grad_kernel(place_ref, normed_ref, act_ref, dh_ref, g0, g1, g2, g3, out_ref, top_ref, bottom_ref):
    i = pl.program_id(0)
    half = pl.num_programs(0) // 2
    width = normed_ref.shape[1]
    rows = width * half // 8

    def put(value, start):
        first = lax.rem(i, half) * width
        for n in range(width // 32):
            at = first + 32 * n
            shard = lax.div(at, rows)
            row = pl.multiple_of(at - shard * rows + start, 32)
            out_ref[shard, pl.ds(row, 32)] = value[32 * n : 32 * n + 32]

    @pl.when(i < half)
    def _():
        put(outer(normed_ref[...], dh_ref[...]).astype(BF16), 0)

    @pl.when(i >= half)
    def _():
        grad = joined([g0[...], g1[...], g2[...], g3[...]])
        put(outer(act_ref[...], grad).astype(BF16), rows)

    @pl.when(i == pl.num_programs(0) - 1)
    def _():
        top_ref[...] = out_ref[place_ref[7], :rows]
        bottom_ref[...] = out_ref[place_ref[7], rows:]


def feed_grads(place, normed, act, dh, grad):
    tokens, width = normed.shape
    length = grad[0].shape[0]
    block = 256
    half = width // block
    return pl.pallas_call(
        feed_grad_kernel,
        grid=(2 * half,),
        in_specs=[
            SCALARS,
            pl.BlockSpec((tokens, block), lambda i: (0, jnp.minimum(i, half - 1))),
            pl.BlockSpec((tokens, block), lambda i: (0, jnp.maximum(i - half, 0))),
            fixed(dh.shape),
        ]
        + [fixed((length, width))] * COPIES,
        out_specs=[
            fixed((8, width // 4, width)),
            fixed((width // 8, width)),
            fixed((width // 8, width)),
        ],
        out_shape=[
            far((8, width // 4, width), BF16),
            like((width // 8, width), BF16),
            like((width // 8, width), BF16),
        ],
        compiler_params=params(),
        cost_estimate=cost(),
    )(place, *kept_far([normed, act, dh, *grad]))


def ring_back_kernel(heads, size, first, *refs):
    (
        me_ref, place_ref, order_ref, mask_ref, table_ref, total_ref, middle_ref, g0, g1, x0, x1, vec_ref,
        wo_ref, qkv_ref, lse_ref, ids_ref,
    ), refs = refs[:16], refs[16:]
    pieces, refs = refs[:9], refs[9:]
    dx_ref = refs[0] if first else None
    cols_ref, grad_ref, share_ref, sums_ref, w_ref, cot_ref, all_ref, semaphores = refs[first:]
    i = pl.program_id(0)
    length, width = x0.shape
    rows = width // 8
    part = heads * size

    @pl.when(i == 0)
    def _():
        for copy in first_copies(pieces, place_ref, rows, w_ref, None, semaphores):
            copy.start()
        sums_ref[...] = jnp.zeros_like(sums_ref)

    for n, grad_ref_in in enumerate((g0, g1)):

        @pl.when(i == n)
        def _():
            cot_ref[...] = grad_ref_in[...].astype(F32)

    grad_normed = total_ref[0].astype(F32)
    unit, inverse = norm_parts(middle_ref[0, 0])
    grad_middle = cot_ref[...] + norm_back(grad_normed, unit, inverse, vec_ref[3:4])
    branch = grad_middle.astype(BF16)

    if first:

        @pl.when(i == 0)
        def _():
            dx_ref[...] = grad_middle
            sums_ref[2:3] = jnp.sum(branch.astype(F32), 0, keepdims=True)
            sums_ref[3:4] = jnp.sum(grad_normed * unit, 0, keepdims=True)
            sums_ref[4:5] = jnp.sum(grad_normed, 0, keepdims=True)

    for me in range(COPIES):

        @pl.when(me_ref[0] == me)
        def _():
            cols_ref[0] = branch[:, me * part : (me + 1) * part]

    mixed = times_transposed(branch, wo_ref[...]).astype(BF16)
    mixed = jnp.concatenate([mixed, jnp.zeros((length, 3 * LANES - part), BF16)], 1)
    query, key, value = (qkv_ref[:, 3 * n * LANES : 3 * (n + 1) * LANES] for n in range(3))
    masks = mask_ref[...].astype(BF16)
    (cosine, cosine_rest, sine, sine_rest), same = positions(ids_ref[0], table_ref[...])
    scale = size**-0.5
    lses = lse_ref[...]
    all_probs, all_lows, queries, keys, mixes = [], [], [], [], []
    for head in range(heads):
        queries.append(query * masks[head : head + 1])
        keys.append(key * masks[head : head + 1])
        mixes.append(mixed * masks[heads + head : heads + head + 1])
        scores = jnp.where(same, times_transposed(queries[-1], key) * scale, MASKED)
        probs = jnp.exp(scores - lses[:, head : head + 1])
        grad_probs = times_transposed(mixes[-1], value)
        inner = jnp.sum(probs * grad_probs, -1, keepdims=True)
        all_probs.append(probs.astype(BF16))
        all_lows.append((probs * (grad_probs - inner)).astype(BF16))
    grad_query = times(jnp.concatenate(all_lows, 1), joined(keys)) * scale
    grad_key = outer(joined(all_lows), joined(queries)) * scale
    grad_value = outer(joined(all_probs), joined(mixes)).astype(BF16)
    lane = lax.broadcasted_iota(jnp.int32, (length, LANES), 1)
    left = heads * size // 2 - LANES
    q1, q2, q_rest = tiles(grad_query, 3)
    k1, k2, k_rest = tiles(grad_key, 3)
    rest = jnp.where(lane < 2 * left, q_rest, pltpu.roll(k_rest, 2 * left, 1))
    rest = rest * cosine_rest + swapped(rest * sine_rest, lane, left)
    grad = jnp.concatenate(
        [
            q1 * cosine + q2 * sine,
            q2 * cosine - q1 * sine,
            k1 * cosine + k2 * sine,
            k2 * cosine - k1 * sine,
            rest,
        ],
        1,
    ).astype(BF16)
    here = pl.ds(pl.multiple_of(i * length, 16), length)
    all_ref[here, :] = jnp.concatenate([grad, grad_value], 1)
    natural = times_transposed(grad, order_ref[...])
    grad_ref[0, :, : 2 * part] = natural.astype(BF16)
    grad_ref[0, :, 2 * part :] = grad_value[:, :part]
    sums_ref[5:6, : 2 * part] += jnp.sum(natural, 0, keepdims=True)
    sums_ref[5:6, 2 * part : 3 * part] += jnp.sum(grad_value[:, :part].astype(F32), 0, keepdims=True)

    @pl.when(i == 1)
    def _():
        for copy in first_copies(pieces, place_ref, rows, w_ref, None, semaphores):
            copy.wait()
        share = times_transposed(all_ref[...], w_ref[...])
        for n, x_ref in enumerate((x0, x1)):
            here = share[n * length : (n + 1) * length]
            unit, _ = norm_parts(x_ref[...].astype(F32))
            sums_ref[0:1] += jnp.sum(here * unit, 0, keepdims=True)
            sums_ref[1:2] += jnp.sum(here, 0, keepdims=True)
            share_ref[n] = here.astype(BF16)


def ring_back(
    me, place, order, masks, table, total, middle, grad, x, vec, w_own, qkv, lse, ids, pieces, heads, size,
    first,
):
    length, width = x[0].shape
    part = heads * size
    core = 0 if first else 1
    by_block = lambda columns: pl.BlockSpec((length, columns), lambda i: (2 * i + core, 0))
    by_half = lambda columns: pl.BlockSpec((1, length, columns), lambda i: (i, 0, 0))
    return pl.pallas_call(
        lambda *refs: ring_back_kernel(heads, size, first, *refs),
        grid=(2,),
        in_specs=[
            SCALARS,
            SCALARS,
            fixed(order.shape),
            fixed(masks.shape),
            fixed(table.shape),
            by_half(width),
            pl.BlockSpec((1, 1, length, width), lambda i: (i, core, 0, 0)),
        ]
        + [fixed((length, width))] * 4
        + [
            fixed(vec.shape),
            fixed(w_own.shape),
            by_block(9 * LANES),
            by_block(LANES),
            pl.BlockSpec((1,) + ids.shape[1:], lambda i: (2 * i + core, 0, 0)),
        ]
        + [ANYWHERE] * len(pieces),
        out_specs=[fixed((length, width))] * first
        + [by_half(part), by_half(3 * part), fixed((2, length, width)), fixed((8, width))],
        out_shape=[far((length, width), F32)] * first
        + [
            far((2, length, part), BF16),
            far((2, length, 3 * part), BF16),
            like((2, length, width), BF16),
            like((8, width), F32),
        ],
        scratch_shapes=[
            pltpu.VMEM((width, 8 * LANES), BF16),
            pltpu.VMEM((length, width), F32),
            pltpu.VMEM((2 * length, 8 * LANES), BF16),
            pltpu.SemaphoreType.DMA((2, len(pieces))),
        ],
        compiler_params=params(),
        cost_estimate=cost(13),
    )(
        me, place, *kept_far([order, masks, table]), total,
        *kept_far([middle, grad[core], grad[2 + core], x[core], x[2 + core]]), vec,
        *kept_far([w_own, qkv, lse]), ids, *kept_far(pieces),
    )


def last_grad_kernel(
    me_ref, place_ref, normed_ref, mixed_ref, grad0_ref, grad1_ref, cols0_ref, cols1_ref, sums0_ref, sums1_ref,
    feed_ref, out_ref, top_ref, bottom_ref, line_ref, grad_ref, cols_ref, sums_ref,
):
    i = pl.program_id(0)
    width = normed_ref.shape[1]
    rows = width * pl.num_programs(0) // 8
    part = cols_ref.shape[1]

    @pl.when(i == 0)
    def _():
        length = grad0_ref.shape[1]
        for n in range(2):
            for core, grad_in, cols_in in ((0, grad0_ref, cols0_ref), (1, grad1_ref, cols1_ref)):
                here = slice((2 * n + core) * length, (2 * n + core + 1) * length)
                grad_ref[here] = grad_in[n]
                cols_ref[here] = cols_in[n]
        sums_ref[...] = sums0_ref[...] + sums1_ref[...]

    left = outer(normed_ref[...], grad_ref[...]).astype(BF16)
    right = outer(mixed_ref[...], cols_ref[...]).astype(BF16)
    value = jnp.concatenate([left, right], 1)
    for n in range(width // 32):
        at = i * width + 32 * n
        shard = lax.div(at, rows)
        row = pl.multiple_of(at - shard * rows, 32)
        out_ref[shard, pl.ds(row, 32)] = value[32 * n : 32 * n + 32]

    @pl.when(i == 0)
    def _():
        line_ref[...] = jnp.zeros_like(line_ref)
        for shard in range(8):
            here = slice(shard * rows, (shard + 1) * rows)
            for n in range(5):
                line_ref[shard, n : n + 1, :rows] = sums_ref[n : n + 1, here]
            line_ref[shard, 5:6, :rows] = feed_ref[1:2, here]
        for me in range(COPIES):

            @pl.when(me_ref[0] == me)
            def _():
                for shard in range(8):
                    line_ref[shard, 7:8, me * rows : (me + 1) * rows] = feed_ref[
                        0:1, shard * rows : (shard + 1) * rows
                    ]
                for n in range(3):
                    start = (n * COPIES + me) * part
                    for shard in range(8):
                        low = max(start, shard * 3 * rows)
                        high = min(start + part, (shard + 1) * 3 * rows)
                        if low < high:
                            line_ref[shard, 6:7, low - shard * 3 * rows : high - shard * 3 * rows] = (
                                sums_ref[5:6, n * part + low - start : n * part + high - start]
                            )

        for shard in range(8):
            out_ref[shard, rows:] = line_ref[shard].astype(BF16)

    @pl.when(i == pl.num_programs(0) - 1)
    def _():
        cut = top_ref.shape[0]
        top_ref[...] = out_ref[place_ref[7], :cut]
        bottom_ref[...] = out_ref[place_ref[7], cut:]


def last_grads(me, place, normed, mixed, grads, cols, sums, feed_sums):
    tokens, width = normed.shape
    block = 256
    rows = width // 8
    by_columns = pl.BlockSpec((tokens, block), lambda i: (0, i))
    parts, part = grads[0].shape[2], cols[0].shape[2]
    shape = (8, rows + EXTRA, parts + part)
    cut = half_of(shape[1])
    return pl.pallas_call(
        last_grad_kernel,
        grid=(width // block,),
        in_specs=[
            SCALARS,
            SCALARS,
            by_columns,
            by_columns,
            *[fixed(a.shape) for a in (*grads, *cols, *sums, feed_sums)],
        ],
        out_specs=[fixed(shape), fixed((cut, shape[2])), fixed((shape[1] - cut, shape[2]))],
        out_shape=[
            like(shape, BF16),
            like((cut, shape[2]), BF16),
            like((shape[1] - cut, shape[2]), BF16),
        ],
        scratch_shapes=[
            pltpu.VMEM((8, EXTRA, shape[2]), F32),
            pltpu.VMEM((tokens, parts), BF16),
            pltpu.VMEM((tokens, part), BF16),
            pltpu.VMEM(sums[0].shape, F32),
        ],
        compiler_params=params(),
        cost_estimate=cost(10),
    )(me, place, *kept_far([normed, mixed, *grads, *cols]), *sums, feed_sums)


def output_kernel(middle_ref, pair_ref, far_ref, vec_ref, out_ref):
    out_ref[...] = (
        middle_ref[0, 0] + pair_ref[0].astype(F32) + far_ref[...].astype(F32) + vec_ref[5:6]
    ).astype(BF16)


def output_of(middle, pair, far, vec):
    length, width = far.shape
    return pl.pallas_call(
        output_kernel,
        grid=(1,),
        in_specs=[
            fixed((1, 1, length, width)),
            fixed(pair.shape),
            fixed(far.shape),
            fixed(vec.shape),
        ],
        out_specs=fixed(far.shape),
        out_shape=like(far.shape, BF16),
        compiler_params=params(),
        cost_estimate=cost(),
    )(middle, pair, far, vec)


def last_norm_kernel(dx_ref, pair_ref, far_ref, x_ref, vec_ref, out_ref):
    grad_normed = pair_ref[0].astype(F32) + far_ref[...].astype(F32)
    unit, inverse = norm_parts(x_ref[...].astype(F32))
    out_ref[...] = (
        dx_ref[...] + norm_back(grad_normed, unit, inverse, vec_ref[0:1])
    ).astype(BF16)


def last_norm(dx, pair, far, x, vec):
    return pl.pallas_call(
        last_norm_kernel,
        in_specs=[WHOLE] * 5,
        out_specs=WHOLE,
        out_shape=like(x.shape, BF16),
        compiler_params=params(),
        cost_estimate=cost(),
    )(dx, pair, far, x, vec)


def spread_kernel(me_ref, s0, s1, s2, s3, whole_up_ref, whole_down_ref):
    slots = (s0, s1, s2, s3)
    rows = whole_up_ref.shape[0]
    step = s0.shape[0] - rows
    size = s0.shape[1] // 8
    for me in range(COPIES):

        @pl.when(me_ref[0] == me)
        def _():
            for n in range(COPIES):
                whole_down_ref[n * step : (n + 1) * step] = slots[me ^ n][rows:].astype(F32)
            for group in range(8):
                at = group * size * COPIES
                whole_up_ref[:, at : at + size * COPIES] = jnp.concatenate(
                    [
                        slots[me ^ n][:rows, group * size : (group + 1) * size]
                        for n in range(COPIES)
                    ],
                    1,
                ).astype(F32)


def spread(me, slots, rows):
    lines, width = slots[0].shape
    return pl.pallas_call(
        spread_kernel,
        in_specs=[SCALARS] + [WHOLE] * COPIES,
        out_specs=[WHOLE] * 2,
        out_shape=[
            like((rows, COPIES * width), F32),
            like((COPIES * (lines - rows), width), F32),
        ],
        compiler_params=params(),
        cost_estimate=cost(),
    )(me, *slots)


def finish_kernel(part, me_ref, s0, s1, s2, s3, whole_qkv_ref, whole_out_ref, *sum_refs):
    slots = (s0, s1, s2, s3)
    rows = whole_qkv_ref.shape[0]
    for me in range(COPIES):

        @pl.when(me_ref[0] == me)
        def _():
            for n in range(3):
                whole_qkv_ref[:, n * COPIES * part : (n + 1) * COPIES * part] = jnp.concatenate(
                    [slots[me ^ m][:rows, n * part : (n + 1) * part] for m in range(COPIES)], 1
                ).astype(F32)
            whole_out_ref[...] = jnp.concatenate(
                [slots[me ^ m][:rows, 3 * part :] for m in range(COPIES)], 1
            ).astype(F32)
            sums = sum(slots[me ^ m][rows:].astype(F32) for m in range(COPIES))
            for n, ref in enumerate(sum_refs):
                ref[...] = sums[n, : ref.shape[0]]


def finish(me, slots, part, vectors):
    lines, width = slots[0].shape
    rows = lines - EXTRA
    return pl.pallas_call(
        lambda *refs: finish_kernel(part, *refs),
        in_specs=[SCALARS] + [WHOLE] * COPIES,
        out_specs=[WHOLE] * (2 + len(vectors)),
        out_shape=[like((rows, 3 * COPIES * part), F32), like((rows, COPIES * part), F32)]
        + [like(shape, F32) for shape in vectors],
        compiler_params=params(),
        cost_estimate=cost(),
    )(me, *slots)


def add_low(one, other):
    return (one.astype(F32) + other.astype(F32)).astype(BF16)


def slot_pairs(kept, sent):
    return (kept.astype(F32) + to_core(sent).astype(F32)).astype(BF16)


def on_eight(
    hidden_in,
    seg_ids,
    patch_rows,
    patch_cols,
    ln1_scale,
    ln1_shift,
    qkv_weight,
    qkv_bias,
    out_weight,
    out_bias,
    ln2_scale,
    ln2_shift,
    up_weight,
    up_bias,
    down_weight,
    down_bias,
    cotangent,
):
    me = lax.axis_index("rep")
    me_list = me.reshape(1).astype(jnp.int32)
    length, width = hidden_in.shape
    rows = ln1_scale.shape[0]
    size = width // HEADS
    heads = HEADS // COPIES
    part = heads * size
    hidden = up_weight.shape[1] // COPIES
    slots = ring_slots()
    vectors = (
        ln1_scale, ln1_shift, out_bias, ln2_scale, ln2_shift, down_bias, qkv_bias, up_bias,
    )

    order, masks = column_order(heads, size), head_masks(heads, size)
    table = rotary_table(heads, size)
    first = first_piece(me_list, order, qkv_weight, out_weight, vectors, part)
    ids, own_x, first = tie((jnp.concatenate([seg_ids, patch_rows, patch_cols]), hidden_in, first))
    ids = gather_rep(ids)
    own_x, ids[2] = tie((own_x, ids[2]))
    x = gather_rep(own_x)
    own_feed = second_piece(me_list, up_weight, down_weight, 8)
    x[2], own_grad = tie((x[2], cotangent))
    grad = gather_rep(own_grad)
    qkv_pieces = ring_gather(
        first, (), {1: x[2:3], 2: [own_feed, slots] + x[1:2] + grad[2:3], 3: x[3:] + ids[1:] + grad[1:2]}
    )
    ids = jnp.stack(ids)
    out_pieces = gather_rep(collect(qkv_pieces, rows, part))

    normed_one, qkv, lse, mixed, vec = ring_attend(
        me_list, slots, order, masks, table, x, ids, qkv_pieces, heads, size
    )
    mixed_all, middle, normed_two, w_own = middle_of(
        me_list, slots, gather_rep(mixed), vec, x, out_pieces, rows
    )
    feed_weights = ring_gather(
        own_feed, qkv_pieces[5:7], {1: [mixed, out_pieces[2]], 3: [normed_two]}
    )
    act, low, sent, kept, feed_sums = feed(
        slots, normed_two, grad, vec, feed_weights, hidden
    )

    arrived = to_core(sent)
    act, arrived = tie((act, arrived))
    chip_own, chip_far = (add_low(kept[n], arrived[n]) for n in range(2))
    far_one, far_two = to_x(chip_far), to_x(chip_own)

    tokens = COPIES * length
    feed_grad, feed_right, feed_left = feed_grads(
        slots, normed_two.reshape(tokens, width), act.reshape(tokens, hidden), low.reshape(tokens, hidden), grad
    )
    far_one, feed_grad, feed_right, feed_left = tie((far_one, feed_grad, feed_right, feed_left))

    (late,) = tie([act], [far_one])
    sent, kept = down_of(slots, late, feed_weights, width)
    made = {}

    def back(name, values, core):
        made[name] = ring_back(
            me_list, slots, order, masks, table, values, middle, grad, x, vec, w_own, qkv, lse, ids,
            qkv_pieces, heads, size, core == 0,
        )
        return made[name]

    def first_hop(_):
        made["far_two"], made["sent"], made["kept"] = tie((far_two, sent, kept))
        return [made["far_two"], made["sent"], made["kept"]]

    def second_hop(moved):
        own, other, _ = tie((far_one, made["far_two"], moved))
        made["total"] = jnp.stack([add_low(chip_own, own), add_low(chip_far, other)])
        made["out_pair"] = slot_pairs(made["kept"], made["sent"])
        return [back("own", made["total"], 0)[2], made["out_pair"]]

    def third_hop(_):
        made["out_far"] = to_x(made["out_pair"][1])
        return [back("near", to_core(made["total"]), 1)[1], made["out_far"]]

    def fourth_hop(_):
        grad_middle, cols, grad_qkv, _, sums = made["own"]
        near_cols, near_qkv, _, near_sums = made["near"]
        made["last"] = last_grads(
            me_list, slots, normed_one, mixed_all, (grad_qkv, near_qkv), (cols, near_cols),
            (sums, near_sums), feed_sums,
        )
        return [made["last"][0]]

    feed_grad = ring_scatter(
        feed_grad, feed_right, feed_left, slots, dict(enumerate((first_hop, second_hop, third_hop, fourth_hop))),
        [far_one], 4,
    )
    feed_slots = gather_rep(feed_grad)
    whole_up, whole_down = spread(me_list, feed_slots, rows)
    output = output_of(middle, made["out_pair"], made["out_far"], vec)

    pair = slot_pairs(made["own"][3], made["near"][2])
    far_pair = to_x(pair[1])
    grad_inputs = last_norm(made["own"][0], pair, far_pair, hidden_in, vec)
    last = ring_scatter(
        *made["last"],
        slots,
        {0: [pair], 1: [feed_grad, far_pair], 2: [output], 3: [feed_slots[2], grad_inputs]},
        (),
        1,
    )
    last_far, whole_up, whole_down = tie((to_x(last), whole_up, whole_down))
    last_slots = [last, to_core(last), last_far, to_core(last_far)]
    whole_qkv, whole_out, *totals = finish(
        me_list, last_slots, part, [vector.shape for vector in vectors]
    )
    return (
        output,
        grad_inputs,
        totals[0],
        totals[1],
        whole_qkv,
        totals[6],
        whole_out,
        totals[2],
        totals[3],
        totals[4],
        whole_up,
        totals[7],
        whole_down,
        totals[5],
    )


def solution(mesh):
    shards = mesh.shape["shard"]
    tokens, vector, matrix = P(("rep", "shard"), None), P("shard"), P("shard", None)
    in_specs = (
        (tokens,) * 4
        + (vector, vector, matrix, vector, matrix, vector)
        + (vector, vector, matrix, vector, matrix, vector)
        + (tokens,)
    )
    out_specs = (
        (tokens, tokens)
        + (vector, vector, matrix, vector, matrix, vector)
        + (vector, vector, matrix, vector, matrix, vector)
    )
    return jax.shard_map(
        on_eight if shards == 8 else lambda *args: on_any(shards, *args),
        mesh=mesh,
        in_specs=in_specs,
        out_specs=out_specs,
        check_vma=False,
    )
```
